128 devices in a mesh: scan: 32 (over y_hi, z, x), mode: 4 (over y_lo, core).
Axes of the slice: x: 4, y: 4 (y_hi: 2, y_lo: 2; y = y_hi * 2 + y_lo), z: 4, core: 2. Of those that a mesh axis runs over, the one named last changes fastest.
Arguments:
- object_field: float32 [2, 8192, 8192], P(None, 'scan', 'mode'), may hold values from -6 to 6
- probe_modes: float32 [2, 2, 256, 256], replicated, may hold values from -3 to 3
- measured: float32 [2048, 256, 256], P(('scan', 'mode')), may hold values from 0.3 to 4
- offsets: int32 [2048, 2], P(('scan', 'mode')), may hold values from 0 to 8191, as said below
- live_count: int32 [128], P(('scan', 'mode')), may hold values from 1 to 16, as said below
Outputs:
- object_step: float32 [2, 8192, 8192], P(None, 'scan', 'mode')
- probe_step: float32 [2, 2, 256, 256], replicated
The draws below stay inside these ranges and needn't reach their ends.
Inputs may be any that keep to these rules, and one draw needn't show every extreme that they name: `offsets`: slot q of device d = q div 16, with s = d div (4) and m = d mod (4), has its row in [s * 256, (s + 1) * 256) and its column in [m * 2048, (m + 1) * 2048); on every device one slot starts at the last row and last column of that range, and another at its first row and first column. `live_count`: the live slots of a device are its first ones; some device has all 16 slots live.
All inputs are finite; a program needn't handle non-finite values.
Results may differ from the reference program's by a relative error of at most 0.003.
The reference program's roundings to bfloat16 on the way count: a program that leaves them out, or rounds other values in their place, can miss the bound.
Values sent between devices are 32-bit elements; how exact they have to be, the bound alone decides.
No kernel may reach another device: no remote copies, remote signals or barrier semaphores. Data moves between devices by JAX's collectives and lax.ppermute only.
A program may use at most 128 MiB of HBM per device.

```python
import math
import jax
import jax.numpy as jnp
from jax import lax

PS = 256
MODES = 2
BR = 256
BC = 2048
P_DEV = 16
NOY = 8192
NOX = 8192
PATTERNS = 2048
N_SCAN = 32
N_MODE = 4


def draw_offsets(key, part):
    slot_ids = jnp.arange(PATTERNS, dtype=jnp.int32)
    device = slot_ids // P_DEV
    mode_groups = NOX // BC
    scan_index = device // mode_groups
    mode_index = device % mode_groups
    row_key, col_key, pick_key = jax.random.split(key, 3)
    row_inside = jax.random.randint(row_key, (PATTERNS,), 0, BR)
    col_inside = jax.random.randint(col_key, (PATTERNS,), 0, BC)
    corner_slot = jax.random.randint(pick_key, (PATTERNS // P_DEV,), 0, P_DEV)
    slot_place = slot_ids % P_DEV
    at_corner = slot_place == corner_slot[device]
    at_anchor = slot_place == (corner_slot[device] + 1) % P_DEV
    row_inside = jnp.where(at_corner, BR - 1, row_inside)
    col_inside = jnp.where(at_corner, BC - 1, col_inside)
    row_inside = jnp.where(at_anchor, 0, row_inside)
    col_inside = jnp.where(at_anchor, 0, col_inside)
    return jnp.stack([scan_index * BR + row_inside, mode_index * BC + col_inside], axis=1).astype(jnp.int32)


def draw_live_count(key, part):
    device_total = PATTERNS // P_DEV
    busy_key, small_key, full_key = jax.random.split(key, 3)
    is_busy = jax.random.randint(busy_key, (device_total,), 0, 20) < 3
    small_counts = jax.random.randint(small_key, (device_total,), 1, P_DEV // 2 + 1)
    full_device = jax.random.randint(full_key, (), 0, device_total)
    counts_drawn = jnp.where(is_busy, P_DEV, small_counts)
    counts_drawn = jnp.where(jnp.arange(device_total) == full_device, P_DEV, counts_drawn)
    return counts_drawn.astype(jnp.int32)


def steps_of(key, dims, pieces, least, largest):
    factor_of = 1.0
    for axis_at, blocks in pieces:
        heights = jax.random.uniform(jax.random.fold_in(jax.random.fold_in(key, 6), axis_at), (blocks,), jnp.float32, least / len(pieces), largest / len(pieces))
        factor_of = factor_of * jnp.repeat(jnp.exp(heights), dims[axis_at] // blocks).reshape((-1,) + (1,) * (len(dims) - 1 - axis_at))
    return factor_of


def normal_values(rng, extent, spread, reach, pieces=(), kind=jnp.bfloat16):
    values = spread * jax.random.normal(rng, extent, jnp.float32)
    if pieces:
        values = values * steps_of(rng, extent, pieces, -0.22, 0.18)
    return jnp.clip(values, -reach, reach).astype(kind)


def setup_inputs(seed: int = 0) -> dict:
    splits = jax.random.split(jax.random.key(seed), 6)
    return {
        "object_field": normal_values(splits[0], (2, NOY, NOX), 1.0, 6.0, ((1, 32), (2, 4)), jnp.float32),
        "probe_modes": normal_values(splits[1], (MODES, 2, PS, PS), 0.5, 3.0, (), jnp.float32),
        "measured": jnp.clip(jnp.exp(math.log(4.0) - 2.5902671 * jax.random.uniform(splits[2], (PATTERNS, PS, PS), jnp.float32) ** steps_of(splits[2], (PATTERNS, PS, PS), ((0, 128),), -0.2, 0.2)), 0.3, 4.0),
        "offsets": draw_offsets(jax.random.fold_in(splits[5], 71), 0),
        "live_count": draw_live_count(jax.random.fold_in(splits[5], 71), 0),
    }


floor_level = 0.5

def dft_tables(length, direction):
    positions = jnp.arange(length, dtype=jnp.int32)
    phase_int = positions[:, None] * positions[None, :] % length
    angles = phase_int.astype(jnp.float32) * (2.0 * math.pi / length)
    scaling = 1.0 / math.sqrt(length)
    cosine = jnp.cos(angles) * scaling
    sine_part = jnp.sin(angles) * scaling * direction
    left_table = jnp.stack([jnp.stack([cosine, sine_part]), jnp.stack([-sine_part, cosine])]).astype(jnp.bfloat16)
    right_table = jnp.stack([jnp.stack([cosine, -sine_part]), jnp.stack([sine_part, cosine])]).astype(jnp.bfloat16)
    return (left_table, right_table)

def transform(stacked, tables):
    left_table, right_table = tables
    half_done = jnp.einsum('ijab,kjbc->kiac', left_table.astype(jnp.float32), stacked.astype(jnp.float32), precision=lax.Precision.HIGHEST)
    half_done = half_done.astype(jnp.bfloat16)
    return jnp.einsum('kjac,jicd->kiad', half_done.astype(jnp.float32), right_table.astype(jnp.float32), precision=lax.Precision.HIGHEST)

def pattern_terms(window, probe_modes, amplitude, forward, backward):
    exit_re = probe_modes[:, 0] * window[0] - probe_modes[:, 1] * window[1]
    exit_im = probe_modes[:, 0] * window[1] + probe_modes[:, 1] * window[0]
    exit_wave = jnp.stack([exit_re, exit_im], axis=1).astype(jnp.bfloat16)
    far_field = transform(exit_wave, forward)
    intensity = lax.optimization_barrier(jnp.sum(far_field * far_field, axis=(0, 1)))
    factor = amplitude * lax.rsqrt(jnp.maximum(intensity, floor_level)) - 1.0
    change = (far_field * factor).astype(jnp.bfloat16)
    delta_wave = transform(change, backward)
    object_re = lax.optimization_barrier(jnp.sum(probe_modes[:, 0] * delta_wave[:, 0] + probe_modes[:, 1] * delta_wave[:, 1], axis=0))
    object_im = lax.optimization_barrier(jnp.sum(probe_modes[:, 0] * delta_wave[:, 1] - probe_modes[:, 1] * delta_wave[:, 0], axis=0))
    probe_re = window[0] * delta_wave[:, 0] + window[1] * delta_wave[:, 1]
    probe_im = window[0] * delta_wave[:, 1] - window[1] * delta_wave[:, 0]
    return (jnp.stack([object_re, object_im]), jnp.stack([probe_re, probe_im], axis=1))

def reference(object_field, probe_modes, measured, offsets, live_count):
    forward = dft_tables(PS, 1.0)
    backward = dft_tables(PS, -1.0)
    padded = jnp.pad(object_field, ((0, 0), (0, PS), (0, PS)))
    zero_grad = jnp.zeros(padded.shape, jnp.float32)
    zero_probe = jnp.zeros(probe_modes.shape, jnp.float32)

    def per_device(device, carried):
        gradient, probe_acc = carried
        anchor_row = device // N_MODE * BR
        anchor_col = device % N_MODE * BC
        anchor = (jnp.int32(0), anchor_row, anchor_col)
        extended = lax.dynamic_slice(padded, anchor, (2, BR + PS, BC + PS))
        local_zero = jnp.zeros(extended.shape, jnp.float32)

        def visit(slot_index, inner):
            local_grad, probe_inner = inner
            row_pick = device * P_DEV + slot_index
            start = (jnp.int32(0), (offsets[row_pick, 0] - anchor_row).astype(jnp.int32), (offsets[row_pick, 1] - anchor_col).astype(jnp.int32))
            window = lax.dynamic_slice(extended, start, (2, PS, PS))
            object_term, probe_term = pattern_terms(window, probe_modes, measured[row_pick], forward, backward)
            current = lax.dynamic_slice(local_grad, start, (2, PS, PS))
            local_grad = lax.dynamic_update_slice(local_grad, current + object_term, start)
            return (local_grad, probe_inner + probe_term)
        local_grad, probe_acc = lax.fori_loop(jnp.int32(0), live_count[device].astype(jnp.int32), visit, (local_zero, probe_acc))
        current = lax.dynamic_slice(gradient, anchor, (2, BR + PS, BC + PS))
        gradient = lax.dynamic_update_slice(gradient, current + local_grad, anchor)
        return (gradient, probe_acc)
    gradient, probe_acc = lax.fori_loop(jnp.int32(0), jnp.int32(N_SCAN * N_MODE), per_device, (zero_grad, zero_probe))
    return (gradient[:, :NOY, :NOX], probe_acc / math.sqrt(PATTERNS))
```

```python
import functools
import math

import jax
import jax.numpy as jnp
import ml_dtypes
import numpy as np
from jax import lax
from jax.experimental import pallas as pl
from jax.experimental.pallas import tpu as pltpu
from jax.sharding import PartitionSpec as P

SLOTS = 16
SIZE = 256
LANE = 128
CHUNK = 256
FLOOR = 0.5
AXES = ("scan", "mode")
f32 = jnp.float32
bf16 = jnp.bfloat16


def tables():
    place = np.arange(SIZE)
    angles = (place[:, None] * place[None, :] % SIZE) * (2.0 * math.pi / SIZE)
    c = np.cos(angles) / math.sqrt(SIZE)
    s = np.sin(angles) / math.sqrt(SIZE)
    order = np.concatenate([place[0::2], place[1::2]])

    def block(c, s):
        return np.block([[c, s], [-s, c]]).astype(ml_dtypes.bfloat16)

    return (
        block(c[:, order], s[:, order]),
        block(c, -s),
        block(c[order], -s[order]),
        block(c, s),
    )


def turned(h):
    n = SIZE
    return jnp.concatenate(
        [
            jnp.concatenate([h[:n, :n], h[n:, :n]], 1),
            jnp.concatenate([h[:n, n:], h[n:, n:]], 1),
        ],
        0,
    )


def pattern(ext, grad, acc, probe, amplitude, tabs, r, c):
    left_fwd, right_fwd, left_bwd, right_bwd = tabs
    n = SIZE
    half = n // 2
    block = c // LANE
    shift = c % LANE
    dot = functools.partial(jnp.dot, preferred_element_type=f32)

    def window(part):
        cols = []
        for j in range(3):
            view = ext.at[part, block + j]
            cols.append(
                jnp.concatenate(
                    [view[pl.ds(r + p, half, stride=2), :] for p in (0, 1)], 0
                )
            )
        wide = jnp.concatenate(cols, 1)
        return pltpu.roll(wide, 3 * LANE - shift, 1)[:, :n]

    wr = window(0)
    wi = window(1)
    x_re = [probe[k, 0] * wr - probe[k, 1] * wi for k in (0, 1)]
    x_im = [probe[k, 0] * wi + probe[k, 1] * wr for k in (0, 1)]
    x = jnp.concatenate([jnp.concatenate(x_re, 1), jnp.concatenate(x_im, 1)], 0).astype(bf16)
    h = turned(dot(left_fwd[...], x).astype(bf16))
    far = dot(h, right_fwd[...])
    sq = far * far
    intensity = (sq[:n, :n] + sq[:n, n:]) + (sq[n:, :n] + sq[n:, n:])
    factor = amplitude * lax.rsqrt(jnp.maximum(intensity, FLOOR)) - 1.0
    factor = jnp.concatenate([jnp.concatenate([factor, factor], 1)] * 2, 0)
    change = turned((far * factor).astype(bf16))
    h = turned(dot(left_bwd[...], change).astype(bf16))
    delta = dot(h, right_bwd[...])
    terms = [None, None]
    for k in (0, 1):
        d_re = delta[n * k : n * k + n, :n]
        d_im = delta[n * k : n * k + n, n:]
        new = (
            probe[k, 0] * d_re + probe[k, 1] * d_im,
            probe[k, 0] * d_im - probe[k, 1] * d_re,
        )
        terms = [b if a is None else a + b for a, b in zip(terms, new)]
        acc[k, 0] += wr * d_re + wi * d_im
        acc[k, 1] += wr * d_im - wi * d_re
    blank = jnp.zeros((n, LANE), f32)
    for part, term in enumerate(terms):
        moved = pltpu.roll(jnp.concatenate([term, blank], 1), shift, 1)
        for j in range(3):
            view = grad.at[part, block + j]
            for p in (0, 1):
                rows = pl.ds(r + p, half, stride=2)
                view[rows, :] = view[rows, :] + moved[half * p : half * (p + 1), LANE * j : LANE * (j + 1)]


def group_kernel(first, count, own_blocks, live, off, *refs):
    wide = count + 2
    n_halo = wide // 2
    has_right = first + wide > own_blocks
    refs = list(refs)
    field = refs.pop(0)
    right = refs.pop(0) if has_right else None
    halos = [refs.pop(0) for _ in range(n_halo)]
    measured, probe, t0, t1, t2, t3, carry, acc_in = refs[:8]
    done, carry_out, acc = refs[8:11]
    ext, grad, frame, picked, load_sem, frame_sem = refs[11:]

    def pick(q, n):
        b = off[q, 1] // LANE - first
        picked[n] = q
        return n + jnp.where((b >= 0) & (b < count), 1, 0)

    n = lax.fori_loop(0, live[0], pick, jnp.int32(0))

    def loads():
        out = []
        for b in range(wide):
            at = (first + b) * LANE
            if first + b < own_blocks:
                src = field.at[:, :, at : at + LANE]
            else:
                at -= own_blocks * LANE
                src = right.at[:, :, at : at + LANE]
            out.append(pltpu.make_async_copy(src, ext.at[:, b, 0:SIZE, :], load_sem.at[2 * b]))
            low = (b % 2) * LANE
            src = halos[b // 2].at[:, :, low : low + LANE]
            out.append(
                pltpu.make_async_copy(src, ext.at[:, b, SIZE : 2 * SIZE, :], load_sem.at[2 * b + 1])
            )
        return out

    def frame_copy(i):
        slot = i % 2
        return pltpu.make_async_copy(measured.at[picked[i]], frame.at[slot], frame_sem.at[slot])

    @pl.when(n > 0)
    def _():
        for copy in loads():
            copy.start()
        frame_copy(0).start()

    grad[:, 0:2] = carry[...]
    grad[:, 2:] = jnp.zeros((2, count, 2 * SIZE, LANE), f32)
    acc[...] = acc_in[...]

    @pl.when(n > 0)
    def _():
        for copy in loads():
            copy.wait()

    def step(i, _):
        @pl.when(i + 1 < n)
        def _():
            frame_copy(i + 1).start()

        frame_copy(i).wait()
        q = picked[i]
        pattern(
            ext, grad, acc, probe, frame[i % 2], (t0, t1, t2, t3), off[q, 0], off[q, 1] - first * LANE
        )
        return 0

    lax.fori_loop(0, n, step, 0)
    done[...] = grad[:, 0:count]
    carry_out[...] = grad[:, count:]


def run_group(first, count, own_blocks, live, off, field, right, halos, measured, probe, tabs, carry, acc):
    wide = count + 2
    anywhere = pl.BlockSpec(memory_space=pl.ANY)
    smem = pl.BlockSpec(memory_space=pltpu.SMEM)
    vmem = pl.BlockSpec(memory_space=pltpu.VMEM)
    rights = [right] if first + wide > own_blocks else []
    args = [live, off, field, *rights, *halos, measured, probe, *tabs, carry, acc]
    specs = [smem, smem] + [anywhere] * (2 + len(rights) + len(halos)) + [vmem] * 7
    out_shape = (
        jax.ShapeDtypeStruct((2, count, 2 * SIZE, LANE), f32),
        jax.ShapeDtypeStruct((2, 2, 2 * SIZE, LANE), f32),
        jax.ShapeDtypeStruct((2, 2, SIZE, SIZE), f32),
    )
    return pl.pallas_call(
        functools.partial(group_kernel, first, count, own_blocks),
        out_shape=out_shape,
        in_specs=specs,
        out_specs=(vmem,) * 3,
        scratch_shapes=[
            pltpu.VMEM((2, wide, 2 * SIZE, LANE), f32),
            pltpu.VMEM((2, wide, 2 * SIZE, LANE), f32),
            pltpu.VMEM((2, SIZE, SIZE), f32),
            pltpu.SMEM((SLOTS + 1,), jnp.int32),
            pltpu.SemaphoreType.DMA((2 * wide,)),
            pltpu.SemaphoreType.DMA((2,)),
        ],
        compiler_params=pltpu.CompilerParams(vmem_limit_bytes=32 * 2**20),
        cost_estimate=pl.CostEstimate(
            flops=2 * 1024**3, bytes_accessed=8 * 2**20, transcendentals=0
        ),
        name=f"group_{first}",
    )(*args)


def shifted(array, axis, by):
    count = lax.axis_size(axis)
    pairs = [(i, i + by) for i in range(count) if 0 <= i + by < count]
    return lax.ppermute(array, axis, pairs)


def shifted_both(array):
    rows, cols = (lax.axis_size(a) for a in AXES)
    pairs = [
        (i * cols + j, (i + 1) * cols + j + 1) for i in range(rows - 1) for j in range(cols - 1)
    ]
    return lax.ppermute(array, AXES, pairs)


def place_of(index):
    s, m = divmod(index, 4)
    return [m % 2, (s // 16) * 2 + m // 2, (s // 4) % 4, s % 4]


def index_of(place):
    core, y, z, x = place
    return ((y // 2) * 16 + z * 4 + x) * 4 + (y % 2) * 2 + core


def swapped(array, axis, bits):
    pairs = []
    for i in range(128):
        place = place_of(i)
        place[axis] ^= bits
        pairs.append((i, index_of(place)))
    return lax.ppermute(array, AXES, pairs)


def sum_everywhere(total):
    s = lax.axis_index("scan")
    m = lax.axis_index("mode")
    core, y = m % 2, (s // 16) * 2 + m // 2
    pick = functools.partial(lax.dynamic_index_in_dim, axis=0, keepdims=False)
    v = total.reshape(2, 512, 256)
    v = pick(v, core) + swapped(pick(v, 1 - core), 0, 1)
    v = v.reshape(4, 128, 256)
    a, b, c = [swapped(pick(v, y ^ k), 1, k) for k in (1, 2, 3)]
    v = (pick(v, y) + a) + (b + c)
    for axis in (2, 3):
        a, b, c = [swapped(v, axis, k) for k in (1, 2, 3)]
        v = (v + a) + (b + c)
    parts = jnp.stack([v] + [swapped(v, 1, k) for k in (1, 2, 3)])
    v = jnp.concatenate([pick(parts, y ^ i) for i in range(4)], 0)
    w = swapped(v, 0, 1)
    low = jnp.where(core == 0, v, w)
    high = jnp.where(core == 0, w, v)
    return jnp.stack([low, high]).reshape(total.shape)


def unblocked(part):
    return jnp.transpose(part, (0, 2, 1, 3)).reshape(2, SIZE, -1)


def shards(field, probe, measured, offsets, live):
    rows, cols = field.shape[1:]
    base = jnp.stack([lax.axis_index("scan") * rows, lax.axis_index("mode") * cols])
    off = offsets - base[None, :]
    tabs = [jnp.asarray(t) for t in tables()]
    probe_rows = probe.reshape(2, 2, 128, 2, 256).transpose(0, 1, 3, 2, 4).reshape(probe.shape)
    chunks = cols // CHUNK
    blocks = cols // LANE
    halos = [shifted(field[:, :, CHUNK * i : CHUNK * (i + 1)], "scan", -1) for i in range(chunks)]
    right = shifted(field[:, :, :CHUNK], "mode", -1)
    halos.append(shifted(halos[0], "mode", -1))
    carry = jnp.zeros((2, 2, 2 * SIZE, LANE), f32)
    acc = jnp.zeros(probe.shape, f32)
    uppers, lowers = [], []
    plan = [(2 * i, 2) for i in range(chunks - 2)] + [(blocks - 4, 4)]
    for first, count in plan:
        near = halos[first // 2 : first // 2 + count // 2 + 1]
        done, carry, acc = run_group(
            first, count, blocks, live, off, field, right, near, measured, probe_rows, tabs, carry, acc
        )
        uppers.append(unblocked(done[:, :, :SIZE]))
        lowers.append(unblocked(shifted(done[:, :, SIZE:], "scan", 1)))
    beside = unblocked(shifted(carry[:, :, :SIZE], "mode", 1)) + unblocked(shifted_both(carry[:, :, SIZE:]))
    uppers[0] = uppers[0] + beside
    step = jnp.concatenate([a + b for a, b in zip(uppers, lowers)], 2)
    acc = sum_everywhere(acc)
    acc = acc.reshape(2, 2, 2, 128, 256).transpose(0, 1, 3, 2, 4).reshape(probe.shape)
    slots_all = lax.axis_size("scan") * lax.axis_size("mode") * SLOTS
    return (step, acc * (1.0 / math.sqrt(slots_all)))


def solution(mesh):
    in_specs = (
        P(None, "scan", "mode"),
        P(),
        P(AXES, None, None),
        P(AXES, None),
        P(AXES),
    )
    out_specs = (P(None, "scan", "mode"), P())
    return jax.shard_map(shards, mesh=mesh, in_specs=in_specs, out_specs=out_specs, check_vma=False)
```

```python
import functools
import math

import jax
import jax.numpy as jnp
import ml_dtypes
import numpy as np
from jax import lax
from jax.experimental import pallas as pl
from jax.experimental.pallas import tpu as pltpu
from jax.sharding import PartitionSpec as P

SLOTS = 16
SIZE = 256
LANE = 128
CHUNK = 256
FLOOR = 0.5
AXES = ("scan", "mode")
f32 = jnp.float32
bf16 = jnp.bfloat16


def tables():
    place = np.arange(SIZE)
    angles = (place[:, None] * place[None, :] % SIZE) * (2.0 * math.pi / SIZE)
    c = np.cos(angles) / math.sqrt(SIZE)
    s = np.sin(angles) / math.sqrt(SIZE)
    order = np.concatenate([place[0::2], place[1::2]])

    def block(c, s):
        return np.block([[c, s], [-s, c]]).astype(ml_dtypes.bfloat16)

    return (
        block(c[:, order], s[:, order]),
        block(c, -s),
        block(c[order], -s[order]),
        block(c, s),
    )


def turned(h):
    n = SIZE
    return jnp.concatenate(
        [
            jnp.concatenate([h[:n, :n], h[n:, :n]], 1),
            jnp.concatenate([h[:n, n:], h[n:, n:]], 1),
        ],
        0,
    )


def pattern(ext, grad, acc, probe, amplitude, tabs, r, c):
    left_fwd, right_fwd, left_bwd, right_bwd = tabs
    n = SIZE
    half = n // 2
    block = c // LANE
    shift = c % LANE
    dot = functools.partial(jnp.dot, preferred_element_type=f32)

    def window(part):
        cols = []
        for j in range(3):
            view = ext.at[part, block + j]
            cols.append(
                jnp.concatenate(
                    [view[pl.ds(r + p, half, stride=2), :] for p in (0, 1)], 0
                )
            )
        wide = jnp.concatenate(cols, 1)
        return pltpu.roll(wide, 3 * LANE - shift, 1)[:, :n]

    wr = window(0)
    wi = window(1)
    x_re = [probe[k, 0] * wr - probe[k, 1] * wi for k in (0, 1)]
    x_im = [probe[k, 0] * wi + probe[k, 1] * wr for k in (0, 1)]
    x = jnp.concatenate([jnp.concatenate(x_re, 1), jnp.concatenate(x_im, 1)], 0).astype(bf16)
    h = turned(dot(left_fwd[...], x).astype(bf16))
    far = dot(h, right_fwd[...])
    sq = far * far
    intensity = (sq[:n, :n] + sq[:n, n:]) + (sq[n:, :n] + sq[n:, n:])
    factor = amplitude * lax.rsqrt(jnp.maximum(intensity, FLOOR)) - 1.0
    factor = jnp.concatenate([jnp.concatenate([factor, factor], 1)] * 2, 0)
    change = turned((far * factor).astype(bf16))
    h = turned(dot(left_bwd[...], change).astype(bf16))
    delta = dot(h, right_bwd[...])
    terms = [None, None]
    for k in (0, 1):
        d_re = delta[n * k : n * k + n, :n]
        d_im = delta[n * k : n * k + n, n:]
        new = (
            probe[k, 0] * d_re + probe[k, 1] * d_im,
            probe[k, 0] * d_im - probe[k, 1] * d_re,
        )
        terms = [b if a is None else a + b for a, b in zip(terms, new)]
        acc[k, 0] += wr * d_re + wi * d_im
        acc[k, 1] += wr * d_im - wi * d_re
    blank = jnp.zeros((n, LANE), f32)
    for part, term in enumerate(terms):
        moved = pltpu.roll(jnp.concatenate([term, blank], 1), shift, 1)
        for j in range(3):
            view = grad.at[part, block + j]
            for p in (0, 1):
                rows = pl.ds(r + p, half, stride=2)
                view[rows, :] = view[rows, :] + moved[half * p : half * (p + 1), LANE * j : LANE * (j + 1)]


def group_kernel(first, count, homes, n_after, last, live, off, *refs):
    wide = count + 2
    refs = list(refs)
    sources = refs[: len(homes[2])]
    refs = refs[len(homes[2]) + n_after :]
    measured, probe, t0, t1, t2, t3, carry, acc_in = refs[:8]
    upper, lower, carry_out, acc = refs[8:12]
    ext, grad, frame, picked, load_sem, frame_sem = refs[12:]

    def pick(q, n):
        b = off[q, 1] // LANE - first
        picked[n] = q
        return n + jnp.where((b >= 0) & (b < count), 1, 0)

    n = lax.fori_loop(0, live[0], pick, jnp.int32(0))

    def loads():
        out = []
        for half in (0, 1):
            for b in range(wide):
                which, row, at = homes[half][b]
                src = sources[which].at[:, row : row + SIZE, at : at + LANE]
                dst = ext.at[:, b, SIZE * half : SIZE * (half + 1), :]
                out.append(pltpu.make_async_copy(src, dst, load_sem.at[2 * b + half]))
        return out

    def frame_copy(i):
        slot = i % 2
        return pltpu.make_async_copy(measured.at[picked[i]], frame.at[slot], frame_sem.at[slot])

    @pl.when(n > 0)
    def _():
        for copy in loads():
            copy.start()
        frame_copy(0).start()

    grad[:, 0:2] = carry[...]
    grad[:, 2:] = jnp.zeros((2, count, 2 * SIZE, LANE), f32)
    acc[...] = acc_in[...]

    @pl.when(n > 0)
    def _():
        for copy in loads():
            copy.wait()

    def step(i, _):
        @pl.when(i + 1 < n)
        def _():
            frame_copy(i + 1).start()

        frame_copy(i).wait()
        q = picked[i]
        pattern(
            ext, grad, acc, probe, frame[i % 2], (t0, t1, t2, t3), off[q, 0], off[q, 1] - first * LANE
        )
        return 0

    lax.fori_loop(0, n, step, 0)
    upper[...] = grad[:, 0:count, :SIZE]
    lower[...] = grad[:, 0:count, SIZE:]
    carry_out[...] = grad[:, count:]
    if last:
        for k in (0, 1):
            for part in (0, 1):
                for b in (0, 1):
                    view = ext.at[part, 2 * k + b]
                    at = slice(LANE * b, LANE * (b + 1))
                    for p in (0, 1):
                        rows = pl.ds(p, SIZE // 2, stride=2)
                        view[rows, :] = acc[k, part, LANE * p : LANE * (p + 1), at]
                    acc[k, part, :, at] = view[0:SIZE, :]


ANYWHERE = pl.BlockSpec(memory_space=pl.ANY)
IN_SMEM = pl.BlockSpec(memory_space=pltpu.SMEM)
IN_VMEM = pl.BlockSpec(memory_space=pltpu.VMEM)


def run_group(first, count, bounds, live, off, field, halos, corner, measured, probe, tabs, carry, acc, after):
    wide = count + 2
    arrays, homes = [], [[], []]

    def index_in(array):
        for i, other in enumerate(arrays):
            if other is array:
                return i
        arrays.append(array)
        return len(arrays) - 1

    for b in range(first, first + wide):
        if b < bounds[-1]:
            chunk = next(i for i, end in enumerate(bounds) if b < end)
            begin = bounds[chunk - 1] if chunk else 0
            homes[0].append((index_in(field), 0, b * LANE))
            homes[1].append((index_in(halos[chunk]), 0, (b - begin) * LANE))
        else:
            at = (b - bounds[-1]) * LANE
            homes[0].append((index_in(corner), 0, at))
            homes[1].append((index_in(corner), SIZE, at))
    homes.append(arrays)
    args = [live, off, *arrays, *after, measured, probe, *tabs, carry, acc]
    specs = [IN_SMEM] * 2 + [ANYWHERE] * (1 + len(arrays) + len(after)) + [IN_VMEM] * 7
    part = jax.ShapeDtypeStruct((2, count, SIZE, LANE), f32)
    out_shape = (
        part,
        part,
        jax.ShapeDtypeStruct((2, 2, 2 * SIZE, LANE), f32),
        jax.ShapeDtypeStruct((2, 2, SIZE, SIZE), f32),
    )
    return pl.pallas_call(
        functools.partial(group_kernel, first, count, (homes[0], homes[1], [None] * len(arrays)),
            len(after), first + count == bounds[-1]),
        out_shape=out_shape,
        in_specs=specs,
        out_specs=(IN_VMEM,) * 4,
        scratch_shapes=[
            pltpu.VMEM((2, wide, 2 * SIZE, LANE), f32),
            pltpu.VMEM((2, wide, 2 * SIZE, LANE), f32),
            pltpu.VMEM((2, SIZE, SIZE), f32),
            pltpu.SMEM((SLOTS + 1,), jnp.int32),
            pltpu.SemaphoreType.DMA((2 * wide,)),
            pltpu.SemaphoreType.DMA((2,)),
        ],
        compiler_params=pltpu.CompilerParams(vmem_limit_bytes=30 * 2**20),
        cost_estimate=pl.CostEstimate(flops=2**34, bytes_accessed=2**12, transcendentals=0),
        name=f"group_{first}",
    )(*args)


def finish_kernel(parts, extra, *refs):
    refs = list(refs)
    uppers = [refs.pop(0) for _ in parts]
    comings = [refs.pop(0) for _ in parts]
    extras = [refs.pop(0) for _ in range(extra)]
    refs = refs[-3:]
    out, buf, sem = refs
    copies = []
    low = parts[0][0]
    for (first, count), upper, coming in zip(parts, uppers, comings):
        for b in range(count):
            value = upper[:, b] + coming[:, b]
            if first + b < 2:
                for more in extras:
                    value = value + more[:, b]
            at = (first + b - low) * LANE
            buf[:, :, at : at + LANE] = value
        begin, end = (first - low) * LANE, (first - low + count) * LANE
        copy = pltpu.make_async_copy(
            buf.at[:, :, begin:end],
            out.at[:, :, first * LANE : (first + count) * LANE],
            sem.at[len(copies)],
        )
        copy.start()
        copies.append(copy)
    for copy in copies:
        copy.wait()


def finish(parts, uppers, comings, extras, shape, onto):
    total = sum(count for _, count in parts)
    args = [*uppers, *comings, *extras]
    specs = [IN_VMEM] * len(args)
    aliases = {}
    if onto is not None:
        aliases = {len(args): 0}
        args.append(onto)
        specs.append(ANYWHERE)
    return pl.pallas_call(
        functools.partial(finish_kernel, parts, len(extras)),
        out_shape=jax.ShapeDtypeStruct(shape, f32),
        in_specs=specs,
        out_specs=ANYWHERE,
        scratch_shapes=[
            pltpu.VMEM((2, SIZE, total * LANE), f32),
            pltpu.SemaphoreType.DMA((len(parts),)),
        ],
        input_output_aliases=aliases,
        compiler_params=pltpu.CompilerParams(vmem_limit_bytes=24 * 2**20),
        name=f"finish_{parts[0][0]}",
    )(*args)


def shifted(array, axis, by, name):
    count = lax.axis_size(axis)
    pairs = [(i, i + by) for i in range(count) if 0 <= i + by < count]
    with jax.named_scope(name):
        return lax.ppermute(array, axis, pairs)


def shifted_both(array):
    rows, cols = (lax.axis_size(a) for a in AXES)
    pairs = [
        (i * cols + j, (i + 1) * cols + j + 1) for i in range(rows - 1) for j in range(cols - 1)
    ]
    with jax.named_scope("slant"):
        return lax.ppermute(array, AXES, pairs)


def place_of(index):
    s, m = divmod(index, 4)
    return [m % 2, (s // 16) * 2 + m // 2, (s // 4) % 4, s % 4]


def index_of(place):
    core, y, z, x = place
    return ((y // 2) * 16 + z * 4 + x) * 4 + (y % 2) * 2 + core


def swapped(array, axis, bits):
    pairs = []
    for i in range(128):
        place = place_of(i)
        place[axis] ^= bits
        pairs.append((i, index_of(place)))
    with jax.named_scope("swap_" + "cyzx"[axis] + str(bits)):
        return lax.ppermute(array, AXES, pairs)


def sum_everywhere(total, scale, before_x, after_x):
    s = lax.axis_index("scan")
    m = lax.axis_index("mode")
    core, y = m % 2, (s // 16) * 2 + m // 2
    pick = functools.partial(lax.dynamic_index_in_dim, axis=0, keepdims=False)
    v = total.reshape(2, 512, 256)
    v = pick(v, core) + swapped(pick(v, 1 - core), 0, 1)
    v = v.reshape(4, 128, 256)
    a, b, c = [swapped(pick(v, y ^ k), 1, k) for k in (1, 2, 3)]
    v = (pick(v, y) + a) + (b + c)
    v, before_x = lax.optimization_barrier((v, before_x))
    v = v + swapped(v, 3, 1)
    v = v + swapped(v, 3, 2)
    v, after_x = lax.optimization_barrier((v, after_x))
    v = v + swapped(v, 2, 1)
    v = v + swapped(v, 2, 2)
    v = v * scale
    parts = jnp.stack([v] + [swapped(v, 1, k) for k in (1, 2, 3)])
    v = jnp.concatenate([pick(parts, y ^ i) for i in range(4)], 0)
    w = swapped(v, 0, 1)
    low = jnp.where(core == 0, v, w)
    high = jnp.where(core == 0, w, v)
    return jnp.stack([low, high]).reshape(total.shape), before_x, after_x


BOUNDS = (6, 9, 12, 15, 16)


def shards(field, probe, measured, offsets, live):
    rows, cols = field.shape[1:]
    base = jnp.stack([lax.axis_index("scan") * rows, lax.axis_index("mode") * cols])
    off = offsets - base[None, :]
    tabs = [jnp.asarray(t) for t in tables()]
    probe_rows = probe.reshape(2, 2, 128, 2, 256).transpose(0, 1, 3, 2, 4).reshape(probe.shape)
    head, field_rest = lax.optimization_barrier((field[:, :, : LANE * BOUNDS[0]], field))
    halos = [shifted(head, "scan", -1, "halo_0")]
    halos += [
        shifted(field_rest[:, :, LANE * a : LANE * b], "scan", -1, f"halo_{i + 1}")
        for i, (a, b) in enumerate(zip(BOUNDS[:-1], BOUNDS[1:]))
    ]
    beside = jnp.concatenate([field[:, :, :SIZE], halos[0][:, :, :SIZE]], 1)
    corner = shifted(beside, "mode", -1, "corner")
    carry = jnp.zeros((2, 2, 2 * SIZE, LANE), f32)
    acc = jnp.zeros(probe.shape, f32)
    ends = [b - 2 for b in BOUNDS[:-1]] + [BOUNDS[-1]]
    plan = [(a, b - a) for a, b in zip([0] + ends[:-1], ends)]
    uppers, comings = [], []
    for i, (first, count) in enumerate(plan):
        after = [comings[i - 2]] if i >= 2 else []
        upper, lower, carry, acc = run_group(
            first, count, BOUNDS, live, off, field, halos, corner, measured, probe_rows, tabs, carry, acc, after
        )
        uppers.append(upper)
        if i + 1 < len(plan):
            comings.append(shifted(lower, "scan", 1, f"grad_{i}"))
    slots_all = lax.axis_size("scan") * lax.axis_size("mode") * SLOTS
    slant = shifted_both(carry[:, :, SIZE:])
    acc, (comings[-1], slant), (last, over) = sum_everywhere(
        acc, 1.0 / math.sqrt(slots_all), (comings[-1], slant), (lower, carry[:, :, :SIZE])
    )
    extras = [slant, shifted(over, "mode", 1, "over")]
    step = finish(plan[:-1], uppers[:-1], comings, extras, field.shape, None)
    step = finish(plan[-1:], uppers[-1:], [shifted(last, "scan", 1, "grad_last")], [], field.shape, step)
    return (step, acc)


def solution(mesh):
    in_specs = (
        P(None, "scan", "mode"),
        P(),
        P(AXES, None, None),
        P(AXES, None),
        P(AXES),
    )
    out_specs = (P(None, "scan", "mode"), P())
    return jax.shard_map(shards, mesh=mesh, in_specs=in_specs, out_specs=out_specs, check_vma=False)
```

```python
import functools
import math

import jax
import jax.numpy as jnp
import ml_dtypes
import numpy as np
from jax import lax
from jax.experimental import pallas as pl
from jax.experimental.pallas import tpu as pltpu
from jax.sharding import PartitionSpec as P

SLOTS = 16
SIZE = 256
LANE = 128
CHUNK = 256
FLOOR = 0.5
AXES = ("scan", "mode")
f32 = jnp.float32
bf16 = jnp.bfloat16


def tables():
    n = SIZE
    place = np.arange(n)
    angles = (place[:, None] * place[None, :] % n) * (2.0 * math.pi / n)
    c = np.cos(angles) / math.sqrt(n)
    s = np.sin(angles) / math.sqrt(n)
    rows = np.concatenate([place[0 : n // 2 : 2], place[1 : n // 2 : 2]])

    def block(c, s):
        return np.block([[c, s], [-s, c]])

    def halves(c, s):
        return np.stack([block(c[rows, p::2], s[rows, p::2]) for p in (0, 1)])

    both = (halves(c, s), block(c, -s), halves(c, -s), block(c, s))
    return [t.astype(ml_dtypes.bfloat16) for t in both]


def stack(parts, axis):
    return jnp.concatenate(parts, axis)


def left_product(table, even, odd):
    dot = functools.partial(jnp.dot, preferred_element_type=f32)
    a = dot(table[0], even)
    b = dot(table[1], odd)
    return (a + b).astype(bf16), (a - b).astype(bf16)


def pattern(ext, grad, acc, probe, frame, tabs, r, c):
    left_fwd, right_fwd, left_bwd, right_bwd = tabs
    n = SIZE
    half, quarter = n // 2, n // 4
    block = c // LANE
    shift = c % LANE
    dot = functools.partial(jnp.dot, preferred_element_type=f32)

    def window(part):
        cols = []
        for j in range(3):
            view = ext.at[part, block + j]
            cols.append(stack([view[pl.ds(r + p, half, stride=2), :] for p in (0, 1)], 0))
        return pltpu.roll(stack(cols, 1), 3 * LANE - shift, 1)[:, :n]

    wr = window(0)
    wi = window(1)
    x_re = [probe[k, 0] * wr - probe[k, 1] * wi for k in (0, 1)]
    x_im = [probe[k, 0] * wi + probe[k, 1] * wr for k in (0, 1)]

    def rows_of(p):
        rows = slice(half * p, half * (p + 1))
        return stack([stack([x_re[k][rows], x_im[k][rows]], 0) for k in (0, 1)], 1).astype(bf16)

    sums = left_product(left_fwd, rows_of(0), rows_of(1))
    h = stack(
        [
            stack([t[:half, n * k : n * (k + 1)], t[half:, n * k : n * (k + 1)]], 1)
            for k in (0, 1)
            for t in sums
        ],
        0,
    )
    far = dot(h, right_fwd[...])
    sq = far * far
    intensity = (sq[:n, :n] + sq[:n, n:]) + (sq[n:, :n] + sq[n:, n:])
    amplitude = stack(
        [
            stack([frame.at[b][pl.ds(row, quarter, stride=2), :] for b in (0, 1)], 1)
            for row in (0, 1, half, half + 1)
        ],
        0,
    )
    factor = amplitude * lax.rsqrt(jnp.maximum(intensity, FLOOR)) - 1.0
    change = [
        [(far[n * k : n * (k + 1), n * p : n * (p + 1)] * factor).astype(bf16) for p in (0, 1)]
        for k in (0, 1)
    ]

    def quarters(q):
        return stack(
            [
                stack([change[k][p][at : at + quarter] for p in (0, 1) for at in (q, q + half)], 0)
                for k in (0, 1)
            ],
            1,
        )

    plus, minus = left_product(left_bwd, quarters(0), quarters(quarter))
    h = stack(
        [
            stack(
                [
                    t[at : at + quarter, n * k : n * (k + 1)],
                    t[half + at : half + at + quarter, n * k : n * (k + 1)],
                ],
                1,
            )
            for k in (0, 1)
            for t, at in ((plus, 0), (minus, 0), (plus, quarter), (minus, quarter))
        ],
        0,
    )
    delta = dot(h, right_bwd[...])
    terms = [None, None]
    for k in (0, 1):
        d_re = delta[n * k : n * k + n, :n]
        d_im = delta[n * k : n * k + n, n:]
        new = (
            probe[k, 0] * d_re + probe[k, 1] * d_im,
            probe[k, 0] * d_im - probe[k, 1] * d_re,
        )
        terms = [b if a is None else a + b for a, b in zip(terms, new)]
        acc[k, 0] += wr * d_re + wi * d_im
        acc[k, 1] += wr * d_im - wi * d_re
    blank = jnp.zeros((n, LANE), f32)
    for part, term in enumerate(terms):
        moved = pltpu.roll(stack([term, blank], 1), shift, 1)
        for j in range(3):
            view = grad.at[part, block + j]
            for p in (0, 1):
                rows = pl.ds(r + p, half, stride=2)
                view[rows, :] = view[rows, :] + moved[half * p : half * (p + 1), LANE * j : LANE * (j + 1)]


def group_kernel(first, count, homes, n_after, last, live, off, *refs):
    wide = count + 2
    refs = list(refs)
    sources = refs[: len(homes[2])]
    refs = refs[len(homes[2]) + n_after :]
    measured, probe, t0, t1, t2, t3, carry, acc_in = refs[:8]
    if last:
        upper, lower, over_upper, over_lower, acc = refs[8:13]
    else:
        upper, lower, carry_out, acc = refs[8:12]
    ext, grad, frame, picked, load_sem, frame_sem = refs[-6:]

    def pick(q, n):
        b = off[q, 1] // LANE - first
        picked[n] = q
        return n + jnp.where((b >= 0) & (b < count), 1, 0)

    n = lax.fori_loop(0, live[0], pick, jnp.int32(0))

    def loads():
        out = []
        for half in (0, 1):
            for b in range(wide):
                which, row, at = homes[half][b]
                src = sources[which].at[:, row : row + SIZE, at : at + LANE]
                dst = ext.at[:, b, SIZE * half : SIZE * (half + 1), :]
                out.append(pltpu.make_async_copy(src, dst, load_sem.at[2 * b + half]))
        return out

    def frame_copies(i):
        slot = i % 2
        return [
            pltpu.make_async_copy(
                measured.at[picked[i], :, LANE * b : LANE * (b + 1)],
                frame.at[slot, b],
                frame_sem.at[2 * slot + b],
            )
            for b in (0, 1)
        ]

    @pl.when(n > 0)
    def _():
        for copy in loads():
            copy.start()
        for copy in frame_copies(0):
            copy.start()

    grad[:, 0:2] = carry[...]
    grad[:, 2:] = jnp.zeros((2, count, 2 * SIZE, LANE), f32)
    acc[...] = acc_in[...]

    @pl.when(n > 0)
    def _():
        for copy in loads():
            copy.wait()

    def step(i, _):
        @pl.when(i + 1 < n)
        def _():
            for copy in frame_copies(i + 1):
                copy.start()

        for copy in frame_copies(i):
            copy.wait()
        q = picked[i]
        pattern(
            ext, grad, acc, probe, frame.at[i % 2], (t0, t1, t2, t3), off[q, 0], off[q, 1] - first * LANE
        )
        return 0

    lax.fori_loop(0, n, step, 0)
    upper[...] = grad[:, 0:count, :SIZE]
    lower[...] = grad[:, 0:count, SIZE:]
    if not last:
        carry_out[...] = grad[:, count:]
    else:
        over_upper[...] = grad[:, count:, :SIZE]
        over_lower[...] = grad[:, count:, SIZE:]
        for k in (0, 1):
            for part in (0, 1):
                for b in (0, 1):
                    view = ext.at[part, 2 * k + b]
                    at = slice(LANE * b, LANE * (b + 1))
                    for p in (0, 1):
                        rows = pl.ds(p, SIZE // 2, stride=2)
                        view[rows, :] = acc[k, part, LANE * p : LANE * (p + 1), at]
                    acc[k, part, :, at] = view[0:SIZE, :]


IN_HBM = pl.BlockSpec(memory_space=pltpu.HBM)
IN_SMEM = pl.BlockSpec(memory_space=pltpu.SMEM)
IN_VMEM = pl.BlockSpec(memory_space=pltpu.VMEM)


def run_group(first, count, bounds, live, off, field, halos, corner, measured, probe, tabs, carry, acc, after):
    wide = count + 2
    arrays, homes = [], [[], []]

    def index_in(array):
        for i, other in enumerate(arrays):
            if other is array:
                return i
        arrays.append(array)
        return len(arrays) - 1

    for b in range(first, first + wide):
        if b < bounds[-1]:
            chunk = next(i for i, end in enumerate(bounds) if b < end)
            begin = bounds[chunk - 1] if chunk else 0
            homes[0].append((index_in(field), 0, b * LANE))
            homes[1].append((index_in(halos[chunk]), 0, (b - begin) * LANE))
        else:
            at = (b - bounds[-1]) * LANE
            homes[0].append((index_in(corner), 0, at))
            homes[1].append((index_in(corner), SIZE, at))
    homes.append(arrays)
    args = [live, off, *arrays, *after, measured, probe, *tabs, carry, acc]
    specs = [IN_SMEM] * 2 + [IN_HBM] * (1 + len(arrays) + len(after)) + [IN_VMEM] * 7
    part = jax.ShapeDtypeStruct((2, count, SIZE, LANE), f32)
    last = first + count == bounds[-1]
    edge = jax.ShapeDtypeStruct((2, 2, SIZE, LANE), f32)
    whole = jax.ShapeDtypeStruct((2, 2, 2 * SIZE, LANE), f32)
    out_shape = (part, part) + ((edge, edge) if last else (whole,))
    out_shape += (jax.ShapeDtypeStruct((2, 2, SIZE, SIZE), f32),)
    return pl.pallas_call(
        functools.partial(group_kernel, first, count, (homes[0], homes[1], [None] * len(arrays)),
            len(after), last),
        out_shape=out_shape,
        in_specs=specs,
        out_specs=(IN_VMEM,) * len(out_shape),
        scratch_shapes=[
            pltpu.VMEM((2, wide, 2 * SIZE, LANE), f32),
            pltpu.VMEM((2, wide, 2 * SIZE, LANE), f32),
            pltpu.VMEM((2, 2, SIZE, LANE), f32),
            pltpu.SMEM((SLOTS + 1,), jnp.int32),
            pltpu.SemaphoreType.DMA((2 * wide,)),
            pltpu.SemaphoreType.DMA((4,)),
        ],
        compiler_params=pltpu.CompilerParams(vmem_limit_bytes=30 * 2**20),
        cost_estimate=pl.CostEstimate(flops=2**34, bytes_accessed=2**12, transcendentals=0),
        name=f"group_{first}",
    )(*args)


def finish_kernel(blocks, terms, *refs):
    out, buf, sem = refs[-3:]
    copies = []
    for at, (block, many) in enumerate(zip(blocks, terms)):
        value = None
        for which, b in many:
            term = refs[which][:, b]
            value = term if value is None else value + term
        buf[at] = value
        copy = pltpu.make_async_copy(
            buf.at[at], out.at[:, :, block * LANE : (block + 1) * LANE], sem.at[at]
        )
        copy.start()
        copies.append(copy)
    for copy in copies:
        copy.wait()


def finish(blocks, sources, shape, onto):
    args = [array for _, array in sources]
    terms = tuple(
        tuple(
            (i, block - first)
            for i, (first, array) in enumerate(sources)
            if first <= block < first + array.shape[1]
        )
        for block in blocks
    )
    specs = [IN_VMEM] * len(args)
    aliases = {}
    if onto is not None:
        aliases = {len(args): 0}
        args.append(onto)
        specs.append(IN_HBM)
    return pl.pallas_call(
        functools.partial(finish_kernel, tuple(blocks), terms),
        out_shape=jax.ShapeDtypeStruct(shape, f32),
        in_specs=specs,
        out_specs=IN_HBM,
        scratch_shapes=[
            pltpu.VMEM((len(blocks), 2, SIZE, LANE), f32),
            pltpu.SemaphoreType.DMA((len(blocks),)),
        ],
        input_output_aliases=aliases,
        compiler_params=pltpu.CompilerParams(vmem_limit_bytes=24 * 2**20),
        name=f"finish_{blocks[0]}",
    )(*args)


def shifted(array, axis, by, name):
    count = lax.axis_size(axis)
    pairs = [(i, i + by) for i in range(count) if 0 <= i + by < count]
    with jax.named_scope(name):
        return lax.ppermute(array, axis, pairs)


def shifted_both(array):
    rows, cols = (lax.axis_size(a) for a in AXES)
    pairs = [
        (i * cols + j, (i + 1) * cols + j + 1) for i in range(rows - 1) for j in range(cols - 1)
    ]
    with jax.named_scope("slant"):
        return lax.ppermute(array, AXES, pairs)


def place_of(index):
    s, m = divmod(index, 4)
    return [m % 2, (s // 16) * 2 + m // 2, (s // 4) % 4, s % 4]


def index_of(place):
    core, y, z, x = place
    return ((y // 2) * 16 + z * 4 + x) * 4 + (y % 2) * 2 + core


def swapped(array, axis, bits):
    pairs = []
    for i in range(128):
        place = place_of(i)
        place[axis] ^= bits
        pairs.append((i, index_of(place)))
    with jax.named_scope("swap_" + "cyzx"[axis] + str(bits)):
        return lax.ppermute(array, AXES, pairs)


def halved_sum(v, axis, here, pieces):
    v = v.reshape(pieces, -1, v.shape[-1])
    pick = functools.partial(lax.dynamic_index_in_dim, axis=0, keepdims=False)
    got = [swapped(pick(v, here ^ k), axis, k) for k in range(1, pieces)]
    if pieces == 2:
        return pick(v, here) + got[0]
    return (pick(v, here) + got[0]) + (got[1] + got[2])


def exchanged_sum(v, axis):
    a, b, c = [swapped(v, axis, k) for k in (1, 2, 3)]
    return (v + a) + (b + c)


def gathered(v, axis, here, pieces):
    parts = [v] + [swapped(v, axis, k) for k in range(1, pieces)]

    def part_of(i):
        which = here ^ i
        if pieces == 2:
            return jnp.where(which == 0, parts[0], parts[1])
        return jnp.where(
            which < 2,
            jnp.where(which == 0, parts[0], parts[1]),
            jnp.where(which == 2, parts[2], parts[3]),
        )

    return jnp.concatenate([part_of(i) for i in range(pieces)], 0)


BOUNDS = (3, 6, 9, 12, 15, 16)


def shards(field, probe, measured, offsets, live):
    rows, cols = field.shape[1:]
    base = jnp.stack([lax.axis_index("scan") * rows, lax.axis_index("mode") * cols])
    off = offsets - base[None, :]
    tabs = [jnp.asarray(t) for t in tables()]
    probe_rows = probe.reshape(2, 2, 128, 2, 256).transpose(0, 1, 3, 2, 4).reshape(probe.shape)
    tie = lax.optimization_barrier
    halos = []
    left_over = field
    for i, (a, b) in enumerate(zip((0,) + BOUNDS[:-1], BOUNDS)):
        part, left_over = tie((left_over[:, :, LANE * a : LANE * b], left_over))
        if i >= 4:
            part, halos[i - 4] = tie((part, halos[i - 4]))
        halos.append(shifted(part, "scan", -1, f"halo_{i}"))
    beside = jnp.concatenate([field[:, :, :SIZE], halos[0][:, :, :SIZE]], 1)
    corner = shifted(beside, "mode", -1, "corner")
    carry = jnp.zeros((2, 2, 2 * SIZE, LANE), f32)
    acc = jnp.zeros(probe.shape, f32)
    ends = [b - 2 for b in BOUNDS[:-1]] + [BOUNDS[-1]]
    plan = [(a, b - a) for a, b in zip([0] + ends[:-1], ends)]
    needed = {3: (0, 1), 4: (2,), 5: (3,)}
    uppers, lowers, comings = [], [], []
    for i, (first, count) in enumerate(plan):
        after = [comings[j] for j in needed.get(i, ())]
        *parts, acc = run_group(
            first, count, BOUNDS, live, off, field, halos, corner, measured, probe_rows, tabs, carry, acc, after
        )
        uppers.append(parts[0])
        lowers.append(parts[1])
        if i + 1 < len(plan):
            carry = parts[2]
        comings.append(shifted(lowers[i], "scan", 1, f"grad_{i}"))
    over_upper, over_lower = parts[2:]
    s, m = lax.axis_index("scan"), lax.axis_index("mode")
    core, y = m % 2, (s // 16) * 2 + m // 2
    v = halved_sum(acc.reshape(1024, 256), 0, core, 2)
    over = shifted(over_upper, "mode", 1, "over")
    v, comings[4] = tie((v, comings[4]))
    v = halved_sum(v, 1, y, 4)
    v, over = tie((v, over))
    v = exchanged_sum(v, 2)
    v, comings[5] = tie((v, comings[5]))
    v = exchanged_sum(v, 3)
    slots_all = lax.axis_size("scan") * lax.axis_size("mode") * SLOTS
    v = v * (1.0 / math.sqrt(slots_all))
    sources = [(first, array) for (first, _), pair in zip(plan, zip(uppers, comings)) for array in pair]
    step = finish(range(2, 13), sources[2:10], field.shape, None)
    v, over_lower, step = tie((v, over_lower, step))
    slant = shifted_both(over_lower)
    v = gathered(v, 1, y, 4)
    v, slant = tie((v, slant))
    probe_step = gathered(v, 0, core, 2).reshape(probe.shape)
    rest = sources[:4] + sources[10:] + [(0, over), (0, slant)]
    step = finish([0, 1, 13, 14, 15], rest, field.shape, step)
    return (step, probe_step)


def solution(mesh):
    in_specs = (
        P(None, "scan", "mode"),
        P(),
        P(AXES, None, None),
        P(AXES, None),
        P(AXES),
    )
    out_specs = (P(None, "scan", "mode"), P())
    return jax.shard_map(shards, mesh=mesh, in_specs=in_specs, out_specs=out_specs, check_vma=False)
```

```python
import functools
import math

import jax
import jax.numpy as jnp
import ml_dtypes
import numpy as np
from jax import lax
from jax.experimental import pallas as pl
from jax.experimental.pallas import tpu as pltpu
from jax.sharding import PartitionSpec as P

SLOTS = 16
SIZE = 256
LANE = 128
CHUNK = 256
FLOOR = 0.5
AXES = ("scan", "mode")
f32 = jnp.float32
bf16 = jnp.bfloat16


def tables():
    n = SIZE
    place = np.arange(n)
    angles = (place[:, None] * place[None, :] % n) * (2.0 * math.pi / n)
    c = np.cos(angles) / math.sqrt(n)
    s = np.sin(angles) / math.sqrt(n)
    rows = np.concatenate([place[0 : n // 2 : 2], place[1 : n // 2 : 2]])

    def block(c, s):
        return np.block([[c, s], [-s, c]])

    def halves(c, s):
        return np.stack([block(c[rows, p::2], s[rows, p::2]) for p in (0, 1)])

    both = (halves(c, s), block(c, -s), halves(c, -s), block(c, s))
    return [t.astype(ml_dtypes.bfloat16) for t in both]


def stack(parts, axis):
    return jnp.concatenate(parts, axis)


def left_product(table, even, odd):
    dot = functools.partial(jnp.dot, preferred_element_type=f32)
    a = dot(table[0], even)
    b = dot(table[1], odd)
    return (a + b).astype(bf16), (a - b).astype(bf16)


def pattern(ext, grad, acc, probe, frame, tabs, r, c):
    left_fwd, right_fwd, left_bwd, right_bwd = tabs
    n = SIZE
    half, quarter = n // 2, n // 4
    block = c // LANE
    shift = c % LANE
    dot = functools.partial(jnp.dot, preferred_element_type=f32)

    def window(part):
        cols = []
        for j in range(3):
            view = ext.at[part, block + j]
            cols.append(stack([view[pl.ds(r + p, half, stride=2), :] for p in (0, 1)], 0))
        return pltpu.roll(stack(cols, 1), 3 * LANE - shift, 1)[:, :n]

    wr = window(0)
    wi = window(1)
    x_re = [probe[k, 0] * wr - probe[k, 1] * wi for k in (0, 1)]
    x_im = [probe[k, 0] * wi + probe[k, 1] * wr for k in (0, 1)]

    def rows_of(p):
        rows = slice(half * p, half * (p + 1))
        return stack([stack([x_re[k][rows], x_im[k][rows]], 0) for k in (0, 1)], 1).astype(bf16)

    sums = left_product(left_fwd, rows_of(0), rows_of(1))
    h = stack(
        [
            stack([t[:half, n * k : n * (k + 1)], t[half:, n * k : n * (k + 1)]], 1)
            for k in (0, 1)
            for t in sums
        ],
        0,
    )
    far = dot(h, right_fwd[...])
    sq = far * far
    intensity = (sq[:n, :n] + sq[:n, n:]) + (sq[n:, :n] + sq[n:, n:])
    amplitude = stack(
        [
            stack([frame.at[b][pl.ds(row, quarter, stride=2), :] for b in (0, 1)], 1)
            for row in (0, 1, half, half + 1)
        ],
        0,
    )
    factor = amplitude * lax.rsqrt(jnp.maximum(intensity, FLOOR)) - 1.0
    change = [
        [(far[n * k : n * (k + 1), n * p : n * (p + 1)] * factor).astype(bf16) for p in (0, 1)]
        for k in (0, 1)
    ]

    def quarters(q):
        return stack(
            [
                stack([change[k][p][at : at + quarter] for p in (0, 1) for at in (q, q + half)], 0)
                for k in (0, 1)
            ],
            1,
        )

    plus, minus = left_product(left_bwd, quarters(0), quarters(quarter))
    h = stack(
        [
            stack(
                [
                    t[at : at + quarter, n * k : n * (k + 1)],
                    t[half + at : half + at + quarter, n * k : n * (k + 1)],
                ],
                1,
            )
            for k in (0, 1)
            for t, at in ((plus, 0), (minus, 0), (plus, quarter), (minus, quarter))
        ],
        0,
    )
    delta = dot(h, right_bwd[...])
    terms = [None, None]
    for k in (0, 1):
        d_re = delta[n * k : n * k + n, :n]
        d_im = delta[n * k : n * k + n, n:]
        new = (
            probe[k, 0] * d_re + probe[k, 1] * d_im,
            probe[k, 0] * d_im - probe[k, 1] * d_re,
        )
        terms = [b if a is None else a + b for a, b in zip(terms, new)]
        acc[k, 0] += wr * d_re + wi * d_im
        acc[k, 1] += wr * d_im - wi * d_re
    blank = jnp.zeros((n, LANE), f32)
    for part, term in enumerate(terms):
        moved = pltpu.roll(stack([term, blank], 1), shift, 1)
        for j in range(3):
            view = grad.at[part, block + j]
            for p in (0, 1):
                rows = pl.ds(r + p, half, stride=2)
                view[rows, :] = view[rows, :] + moved[half * p : half * (p + 1), LANE * j : LANE * (j + 1)]


def group_kernel(first, count, homes, n_after, last, live, off, *refs):
    wide = count + 2
    refs = list(refs)
    sources = refs[: len(homes[2])]
    refs = refs[len(homes[2]) + n_after :]
    measured, probe, t0, t1, t2, t3, carry, acc_in = refs[:8]
    upper, lower, carry_out, acc = refs[8:12]
    ext, grad, frame, picked, load_sem, frame_sem = refs[-6:]

    def pick(q, n):
        b = off[q, 1] // LANE - first
        picked[n] = q
        return n + jnp.where((b >= 0) & (b < count), 1, 0)

    n = lax.fori_loop(0, live[0], pick, jnp.int32(0))

    def loads():
        out = []
        for half in (0, 1):
            for b in range(wide):
                which, row, at = homes[half][b]
                src = sources[which].at[:, row : row + SIZE, at : at + LANE]
                dst = ext.at[:, b, SIZE * half : SIZE * (half + 1), :]
                out.append(pltpu.make_async_copy(src, dst, load_sem.at[2 * b + half]))
        return out

    def frame_copies(i):
        slot = i % 2
        return [
            pltpu.make_async_copy(
                measured.at[picked[i], :, LANE * b : LANE * (b + 1)],
                frame.at[slot, b],
                frame_sem.at[2 * slot + b],
            )
            for b in (0, 1)
        ]

    @pl.when(n > 0)
    def _():
        for copy in loads():
            copy.start()
        for copy in frame_copies(0):
            copy.start()

    grad[:, 0:2] = carry[...]
    grad[:, 2:] = jnp.zeros((2, count, 2 * SIZE, LANE), f32)
    acc[...] = acc_in[...]

    @pl.when(n > 0)
    def _():
        for copy in loads():
            copy.wait()

    def step(i, _):
        @pl.when(i + 1 < n)
        def _():
            for copy in frame_copies(i + 1):
                copy.start()

        for copy in frame_copies(i):
            copy.wait()
        q = picked[i]
        pattern(
            ext, grad, acc, probe, frame.at[i % 2], (t0, t1, t2, t3), off[q, 0], off[q, 1] - first * LANE
        )
        return 0

    lax.fori_loop(0, n, step, 0)
    upper[...] = grad[:, 0:count, :SIZE]
    lower[...] = grad[:, 0:count, SIZE:]
    carry_out[...] = grad[:, count:]
    if last:
        for k in (0, 1):
            for part in (0, 1):
                for b in (0, 1):
                    view = ext.at[part, 2 * k + b]
                    at = slice(LANE * b, LANE * (b + 1))
                    for p in (0, 1):
                        rows = pl.ds(p, SIZE // 2, stride=2)
                        view[rows, :] = acc[k, part, LANE * p : LANE * (p + 1), at]
                    acc[k, part, :, at] = view[0:SIZE, :]


IN_HBM = pl.BlockSpec(memory_space=pltpu.HBM)
IN_SMEM = pl.BlockSpec(memory_space=pltpu.SMEM)
IN_VMEM = pl.BlockSpec(memory_space=pltpu.VMEM)


def run_group(first, count, bounds, live, off, field, halos, corner, measured, probe, tabs, carry, acc, after):
    wide = count + 2
    arrays, homes = [], [[], []]

    def index_in(array):
        for i, other in enumerate(arrays):
            if other is array:
                return i
        arrays.append(array)
        return len(arrays) - 1

    for b in range(first, first + wide):
        if b < bounds[-1]:
            chunk = next(i for i, end in enumerate(bounds) if b < end)
            begin = bounds[chunk - 1] if chunk else 0
            homes[0].append((index_in(field), 0, b * LANE))
            homes[1].append((index_in(halos[chunk]), 0, (b - begin) * LANE))
        else:
            at = (b - bounds[-1]) * LANE
            homes[0].append((index_in(corner), 0, at))
            homes[1].append((index_in(corner), SIZE, at))
    homes.append(arrays)
    args = [live, off, *arrays, *after, measured, probe, *tabs, carry, acc]
    specs = [IN_SMEM] * 2 + [IN_HBM] * (1 + len(arrays) + len(after)) + [IN_VMEM] * 7
    part = jax.ShapeDtypeStruct((2, count, SIZE, LANE), f32)
    last = first + count == bounds[-1]
    whole = jax.ShapeDtypeStruct((2, 2, 2 * SIZE, LANE), f32)
    out_shape = (part, part, whole)
    out_shape += (jax.ShapeDtypeStruct((2, 2, SIZE, SIZE), f32),)
    return pl.pallas_call(
        functools.partial(group_kernel, first, count, (homes[0], homes[1], [None] * len(arrays)),
            len(after), last),
        out_shape=out_shape,
        in_specs=specs,
        out_specs=(IN_VMEM,) * len(out_shape),
        scratch_shapes=[
            pltpu.VMEM((2, wide, 2 * SIZE, LANE), f32),
            pltpu.VMEM((2, wide, 2 * SIZE, LANE), f32),
            pltpu.VMEM((2, 2, SIZE, LANE), f32),
            pltpu.SMEM((SLOTS + 1,), jnp.int32),
            pltpu.SemaphoreType.DMA((2 * wide,)),
            pltpu.SemaphoreType.DMA((4,)),
        ],
        compiler_params=pltpu.CompilerParams(vmem_limit_bytes=30 * 2**20),
        cost_estimate=pl.CostEstimate(flops=2**32, bytes_accessed=2**12, transcendentals=0),
        name=f"group_{first}",
    )(*args)


def finish_kernel(blocks, terms, *refs):
    out, buf, sem = refs[-3:]
    copies = []
    for at, (block, many) in enumerate(zip(blocks, terms)):
        value = None
        for which, b in many:
            term = refs[which][:, b, :SIZE]
            value = term if value is None else value + term
        buf[at] = value
        copy = pltpu.make_async_copy(
            buf.at[at], out.at[:, :, block * LANE : (block + 1) * LANE], sem.at[at]
        )
        copy.start()
        copies.append(copy)
    for copy in copies:
        copy.wait()


def finish(blocks, sources, shape, onto):
    args = [array for _, array in sources]
    terms = tuple(
        tuple(
            (i, block - first)
            for i, (first, array) in enumerate(sources)
            if first <= block < first + array.shape[1]
        )
        for block in blocks
    )
    specs = [IN_VMEM] * len(args)
    aliases = {}
    if onto is not None:
        aliases = {len(args): 0}
        args.append(onto)
        specs.append(IN_HBM)
    return pl.pallas_call(
        functools.partial(finish_kernel, tuple(blocks), terms),
        out_shape=jax.ShapeDtypeStruct(shape, f32),
        in_specs=specs,
        out_specs=IN_HBM,
        scratch_shapes=[
            pltpu.VMEM((len(blocks), 2, SIZE, LANE), f32),
            pltpu.SemaphoreType.DMA((len(blocks),)),
        ],
        input_output_aliases=aliases,
        compiler_params=pltpu.CompilerParams(vmem_limit_bytes=24 * 2**20),
        name=f"finish_{blocks[0]}",
    )(*args)


def shifted(array, axis, by, name):
    count = lax.axis_size(axis)
    pairs = [(i, i + by) for i in range(count) if 0 <= i + by < count]
    with jax.named_scope(name):
        return lax.ppermute(array, axis, pairs)


def place_of(index):
    s, m = divmod(index, 4)
    return [m % 2, (s // 16) * 2 + m // 2, (s // 4) % 4, s % 4]


def index_of(place):
    core, y, z, x = place
    return ((y // 2) * 16 + z * 4 + x) * 4 + (y % 2) * 2 + core


def swapped(array, axis, bits):
    pairs = []
    for i in range(128):
        place = place_of(i)
        place[axis] ^= bits
        pairs.append((i, index_of(place)))
    with jax.named_scope("swap_" + "cyzx"[axis] + str(bits)):
        return lax.ppermute(array, AXES, pairs)


def halved_sum(v, axis, here, pieces):
    v = v.reshape(pieces, -1, v.shape[-1])
    pick = functools.partial(lax.dynamic_index_in_dim, axis=0, keepdims=False)
    got = [swapped(pick(v, here ^ k), axis, k) for k in range(1, pieces)]
    if pieces == 2:
        return pick(v, here) + got[0]
    return (pick(v, here) + got[0]) + (got[1] + got[2])


def exchanged_sum(v, axis):
    a, b, c = [swapped(v, axis, k) for k in (1, 2, 3)]
    return (v + a) + (b + c)


def gathered(v, axis, here, pieces):
    parts = [v] + [swapped(v, axis, k) for k in range(1, pieces)]

    def part_of(i):
        which = here ^ i
        if pieces == 2:
            return jnp.where(which == 0, parts[0], parts[1])
        return jnp.where(
            which < 2,
            jnp.where(which == 0, parts[0], parts[1]),
            jnp.where(which == 2, parts[2], parts[3]),
        )

    return jnp.concatenate([part_of(i) for i in range(pieces)], 0)


BOUNDS = (4, 7, 10, 12, 15, 16)


def shards(field, probe, measured, offsets, live):
    rows, cols = field.shape[1:]
    base = jnp.stack([lax.axis_index("scan") * rows, lax.axis_index("mode") * cols])
    off = offsets - base[None, :]
    tabs = [jnp.asarray(t) for t in tables()]
    probe_rows = probe.reshape(2, 2, 128, 2, 256).transpose(0, 1, 3, 2, 4).reshape(probe.shape)
    tie = lax.optimization_barrier
    head, rest = tie((field[:, :, : LANE * BOUNDS[0]], field))
    halos = [shifted(head, "scan", -1, "halo_0")]
    for i, (a, b) in enumerate(zip(BOUNDS[:-1], BOUNDS[1:])):
        part = rest[:, :, LANE * a : LANE * b]
        halos.append(shifted(part, "scan", -1, f"halo_{i + 1}"))
    beside = jnp.concatenate([field[:, :, :SIZE], halos[0][:, :, :SIZE]], 1)
    corner = shifted(beside, "mode", -1, "corner")
    carry = jnp.zeros((2, 2, 2 * SIZE, LANE), f32)
    acc = jnp.zeros(probe.shape, f32)
    ends = [b - 2 for b in BOUNDS[:-1]] + [BOUNDS[-1]]
    plan = [(a, b - a) for a, b in zip([0] + ends[:-1], ends)]
    uppers, lowers, comings = [], [], []
    for i, (first, count) in enumerate(plan):
        after = {3: (corner, 1), 4: (2,), 5: (3,)}.get(i, ())
        after = [comings[j] if isinstance(j, int) else j for j in after]
        upper, lower, carry, acc = run_group(
            first, count, BOUNDS, live, off, field, halos, corner, measured, probe_rows, tabs, carry, acc, after
        )
        uppers.append(upper)
        lowers.append(lower)
        early = 0 < i < len(plan) - 1
        comings.append(shifted(lower, "scan", 1, f"grad_{i}") if early else None)
    s, m = lax.axis_index("scan"), lax.axis_index("mode")
    core, y = m % 2, (s // 16) * 2 + m // 2
    v = halved_sum(acc.reshape(1024, 256), 0, core, 2)
    v, comings[4], final = tie((v, comings[4], lowers[5]))
    comings[5] = shifted(final, "scan", 1, "grad_5")
    v = halved_sum(v, 1, y, 4)
    v, carry = tie((v, carry))
    over = shifted(carry, "mode", 1, "over")
    v = exchanged_sum(v, 2)
    sources = [(first, array) for (first, _), pair in zip(plan, zip(uppers, comings)) for array in pair]
    step = finish(range(2, 13), sources[2:10], field.shape, None)
    v, comings[5], step = tie((v, comings[5], step))
    v = exchanged_sum(v, 3)
    slots_all = lax.axis_size("scan") * lax.axis_size("mode") * SLOTS
    v = v * (1.0 / math.sqrt(slots_all))
    v, over = tie((v, over))
    comings[0] = shifted(lowers[0] + over[:, :, SIZE:], "scan", 1, "grad_0")
    v = gathered(v, 1, y, 4)
    v, comings[0] = tie((v, comings[0]))
    probe_step = gathered(v, 0, core, 2).reshape(probe.shape)
    rest = [(0, uppers[0]), (0, comings[0]), (0, over), (13, uppers[5]), (13, comings[5])]
    step = finish([0, 1, 13, 14, 15], rest, field.shape, step)
    return (step, probe_step)


def solution(mesh):
    in_specs = (
        P(None, "scan", "mode"),
        P(),
        P(AXES, None, None),
        P(AXES, None),
        P(AXES),
    )
    out_specs = (P(None, "scan", "mode"), P())
    return jax.shard_map(shards, mesh=mesh, in_specs=in_specs, out_specs=out_specs, check_vma=False)
```

```python
import functools
import math

import jax
import jax.numpy as jnp
import ml_dtypes
import numpy as np
from jax import lax
from jax.experimental import pallas as pl
from jax.experimental.pallas import tpu as pltpu
from jax.sharding import PartitionSpec as P

SLOTS = 16
SIZE = 256
LANE = 128
CHUNK = 256
FLOOR = 0.5
AXES = ("scan", "mode")
f32 = jnp.float32
bf16 = jnp.bfloat16


def tables():
    n = SIZE
    place = np.arange(n)
    angles = (place[:, None] * place[None, :] % n) * (2.0 * math.pi / n)
    c = np.cos(angles) / math.sqrt(n)
    s = np.sin(angles) / math.sqrt(n)
    rows = np.concatenate([place[0 : n // 2 : 2], place[1 : n // 2 : 2]])

    def block(c, s):
        return np.block([[c, s], [-s, c]])

    def halves(c, s):
        return np.stack([block(c[rows, p::2], s[rows, p::2]) for p in (0, 1)])

    both = (halves(c, s), block(c, -s), halves(c, -s), block(c, s))
    return [t.astype(ml_dtypes.bfloat16) for t in both]


def stack(parts, axis):
    return jnp.concatenate(parts, axis)


def left_product(table, even, odd):
    dot = functools.partial(jnp.dot, preferred_element_type=f32)
    a = dot(table[0], even)
    b = dot(table[1], odd)
    return (a + b).astype(bf16), (a - b).astype(bf16)


def pattern(ext, grad, acc, probe, frame, tabs, r, c):
    left_fwd, right_fwd, left_bwd, right_bwd = tabs
    n = SIZE
    half, quarter = n // 2, n // 4
    block = c // LANE
    shift = c % LANE
    dot = functools.partial(jnp.dot, preferred_element_type=f32)

    def window(part):
        cols = []
        for j in range(3):
            view = ext.at[part, block + j]
            cols.append(stack([view[pl.ds(r + p, half, stride=2), :] for p in (0, 1)], 0))
        return pltpu.roll(stack(cols, 1), 3 * LANE - shift, 1)[:, :n]

    wr = window(0)
    wi = window(1)
    x_re = [probe[k, 0] * wr - probe[k, 1] * wi for k in (0, 1)]
    x_im = [probe[k, 0] * wi + probe[k, 1] * wr for k in (0, 1)]

    def rows_of(p):
        rows = slice(half * p, half * (p + 1))
        return stack([stack([x_re[k][rows], x_im[k][rows]], 0) for k in (0, 1)], 1).astype(bf16)

    sums = left_product(left_fwd, rows_of(0), rows_of(1))
    h = stack(
        [
            stack([t[:half, n * k : n * (k + 1)], t[half:, n * k : n * (k + 1)]], 1)
            for k in (0, 1)
            for t in sums
        ],
        0,
    )
    far = dot(h, right_fwd[...])
    sq = far * far
    intensity = (sq[:n, :n] + sq[:n, n:]) + (sq[n:, :n] + sq[n:, n:])
    amplitude = stack(
        [
            stack([frame.at[b][pl.ds(row, quarter, stride=2), :] for b in (0, 1)], 1)
            for row in (0, 1, half, half + 1)
        ],
        0,
    )
    factor = amplitude * lax.rsqrt(jnp.maximum(intensity, FLOOR)) - 1.0
    change = [
        [(far[n * k : n * (k + 1), n * p : n * (p + 1)] * factor).astype(bf16) for p in (0, 1)]
        for k in (0, 1)
    ]

    def quarters(q):
        return stack(
            [
                stack([change[k][p][at : at + quarter] for p in (0, 1) for at in (q, q + half)], 0)
                for k in (0, 1)
            ],
            1,
        )

    plus, minus = left_product(left_bwd, quarters(0), quarters(quarter))
    h = stack(
        [
            stack(
                [
                    t[at : at + quarter, n * k : n * (k + 1)],
                    t[half + at : half + at + quarter, n * k : n * (k + 1)],
                ],
                1,
            )
            for k in (0, 1)
            for t, at in ((plus, 0), (minus, 0), (plus, quarter), (minus, quarter))
        ],
        0,
    )
    delta = dot(h, right_bwd[...])
    terms = [None, None]
    for k in (0, 1):
        d_re = delta[n * k : n * k + n, :n]
        d_im = delta[n * k : n * k + n, n:]
        new = (
            probe[k, 0] * d_re + probe[k, 1] * d_im,
            probe[k, 0] * d_im - probe[k, 1] * d_re,
        )
        terms = [b if a is None else a + b for a, b in zip(terms, new)]
        acc[k, 0] += wr * d_re + wi * d_im
        acc[k, 1] += wr * d_im - wi * d_re
    blank = jnp.zeros((n, LANE), f32)
    for part, term in enumerate(terms):
        moved = pltpu.roll(stack([term, blank], 1), shift, 1)
        for j in range(3):
            view = grad.at[part, block + j]
            for p in (0, 1):
                rows = pl.ds(r + p, half, stride=2)
                view[rows, :] = view[rows, :] + moved[half * p : half * (p + 1), LANE * j : LANE * (j + 1)]


def group_kernel(first, count, homes, n_after, last, live, off, *refs):
    wide = count + 2
    refs = list(refs)
    sources = refs[: len(homes[2])]
    refs = refs[len(homes[2]) + n_after :]
    measured, probe, t0, t1, t2, t3, carry, acc_in = refs[:8]
    upper, lower, carry_out, acc = refs[8:12]
    ext, grad, frame, picked, load_sem, frame_sem = refs[-6:]

    def pick(q, n):
        b = off[q, 1] // LANE - first
        picked[n] = q
        return n + jnp.where((b >= 0) & (b < count), 1, 0)

    n = lax.fori_loop(0, live[0], pick, jnp.int32(0))

    def loads():
        out = []
        for half in (0, 1):
            for b in range(wide):
                which, row, at = homes[half][b]
                src = sources[which].at[:, row : row + SIZE, at : at + LANE]
                dst = ext.at[:, b, SIZE * half : SIZE * (half + 1), :]
                out.append(pltpu.make_async_copy(src, dst, load_sem.at[2 * b + half]))
        return out

    def frame_copies(i):
        slot = i % 2
        return [
            pltpu.make_async_copy(
                measured.at[picked[i], :, LANE * b : LANE * (b + 1)],
                frame.at[slot, b],
                frame_sem.at[2 * slot + b],
            )
            for b in (0, 1)
        ]

    @pl.when(n > 0)
    def _():
        for copy in loads():
            copy.start()
        for copy in frame_copies(0):
            copy.start()

    grad[:, 0:2] = carry[...]
    grad[:, 2:] = jnp.zeros((2, count, 2 * SIZE, LANE), f32)
    acc[...] = acc_in[...]

    @pl.when(n > 0)
    def _():
        for copy in loads():
            copy.wait()

    def step(i, _):
        @pl.when(i + 1 < n)
        def _():
            for copy in frame_copies(i + 1):
                copy.start()

        for copy in frame_copies(i):
            copy.wait()
        q = picked[i]
        pattern(
            ext, grad, acc, probe, frame.at[i % 2], (t0, t1, t2, t3), off[q, 0], off[q, 1] - first * LANE
        )
        return 0

    lax.fori_loop(0, n, step, 0)
    upper[...] = grad[:, 0:count, :SIZE]
    lower[...] = grad[:, 0:count, SIZE:]
    carry_out[...] = grad[:, count:]
    if last:
        for k in (0, 1):
            for part in (0, 1):
                for b in (0, 1):
                    view = ext.at[part, 2 * k + b]
                    at = slice(LANE * b, LANE * (b + 1))
                    for p in (0, 1):
                        rows = pl.ds(p, SIZE // 2, stride=2)
                        view[rows, :] = acc[k, part, LANE * p : LANE * (p + 1), at]
                    acc[k, part, :, at] = view[0:SIZE, :]


IN_HBM = pl.BlockSpec(memory_space=pltpu.HBM)
IN_SMEM = pl.BlockSpec(memory_space=pltpu.SMEM)
IN_VMEM = pl.BlockSpec(memory_space=pltpu.VMEM)


def run_group(first, count, bounds, live, off, field, halos, right, corner, measured, probe, tabs, carry, acc, after):
    wide = count + 2
    arrays, homes = [], [[], []]

    def index_in(array):
        for i, other in enumerate(arrays):
            if other is array:
                return i
        arrays.append(array)
        return len(arrays) - 1

    for b in range(first, first + wide):
        if b < bounds[-1]:
            chunk = next(i for i, end in enumerate(bounds) if b < end)
            begin = bounds[chunk - 1] if chunk else 0
            homes[0].append((index_in(field), 0, b * LANE))
            homes[1].append((index_in(halos[chunk]), 0, (b - begin) * LANE))
        else:
            at = (b - bounds[-1]) * LANE
            homes[0].append((index_in(right), 0, at))
            homes[1].append((index_in(corner), 0, at))
    homes.append(arrays)
    args = [live, off, *arrays, *after, measured, probe, *tabs, carry, acc]
    specs = [IN_SMEM] * 2 + [IN_HBM] * (1 + len(arrays) + len(after)) + [IN_VMEM] * 7
    part = jax.ShapeDtypeStruct((2, count, SIZE, LANE), f32)
    last = first + count == bounds[-1]
    whole = jax.ShapeDtypeStruct((2, 2, 2 * SIZE, LANE), f32)
    out_shape = (part, part, whole)
    out_shape += (jax.ShapeDtypeStruct((2, 2, SIZE, SIZE), f32),)
    return pl.pallas_call(
        functools.partial(group_kernel, first, count, (homes[0], homes[1], [None] * len(arrays)),
            len(after), last),
        out_shape=out_shape,
        in_specs=specs,
        out_specs=(IN_VMEM,) * len(out_shape),
        scratch_shapes=[
            pltpu.VMEM((2, wide, 2 * SIZE, LANE), f32),
            pltpu.VMEM((2, wide, 2 * SIZE, LANE), f32),
            pltpu.VMEM((2, 2, SIZE, LANE), f32),
            pltpu.SMEM((SLOTS + 1,), jnp.int32),
            pltpu.SemaphoreType.DMA((2 * wide,)),
            pltpu.SemaphoreType.DMA((4,)),
        ],
        compiler_params=pltpu.CompilerParams(vmem_limit_bytes=44 * 2**20),
        cost_estimate=pl.CostEstimate(flops=2**32, bytes_accessed=2**12, transcendentals=0),
        name=f"group_{first}",
    )(*args)


def finish_kernel(blocks, terms, *refs):
    out, buf, sem = refs[-3:]
    copies = []
    for at, (block, many) in enumerate(zip(blocks, terms)):
        value = None
        for which, b in many:
            term = refs[which][:, b, :SIZE]
            value = term if value is None else value + term
        buf[at] = value
        copy = pltpu.make_async_copy(
            buf.at[at], out.at[:, :, block * LANE : (block + 1) * LANE], sem.at[at]
        )
        copy.start()
        copies.append(copy)
    for copy in copies:
        copy.wait()


def finish(blocks, sources, shape, onto):
    args = [array for _, array in sources]
    terms = tuple(
        tuple(
            (i, block - first)
            for i, (first, array) in enumerate(sources)
            if first <= block < first + array.shape[1]
        )
        for block in blocks
    )
    specs = [IN_VMEM] * len(args)
    aliases = {}
    if onto is not None:
        aliases = {len(args): 0}
        args.append(onto)
        specs.append(IN_HBM)
    return pl.pallas_call(
        functools.partial(finish_kernel, tuple(blocks), terms),
        out_shape=jax.ShapeDtypeStruct(shape, f32),
        in_specs=specs,
        out_specs=IN_HBM,
        scratch_shapes=[
            pltpu.VMEM((len(blocks), 2, SIZE, LANE), f32),
            pltpu.SemaphoreType.DMA((len(blocks),)),
        ],
        input_output_aliases=aliases,
        compiler_params=pltpu.CompilerParams(vmem_limit_bytes=24 * 2**20),
        name=f"finish_{blocks[0]}",
    )(*args)


def shifted(array, axis, by, name):
    count = lax.axis_size(axis)
    pairs = [(i, i + by) for i in range(count) if 0 <= i + by < count]
    with jax.named_scope(name):
        return lax.ppermute(array, axis, pairs)


def place_of(index):
    s, m = divmod(index, 4)
    return [m % 2, (s // 16) * 2 + m // 2, (s // 4) % 4, s % 4]


def index_of(place):
    core, y, z, x = place
    return ((y // 2) * 16 + z * 4 + x) * 4 + (y % 2) * 2 + core


def swapped(array, axis, bits):
    pairs = []
    for i in range(128):
        place = place_of(i)
        place[axis] ^= bits
        pairs.append((i, index_of(place)))
    with jax.named_scope("swap_" + "cyzx"[axis] + str(bits)):
        return lax.ppermute(array, AXES, pairs)


def halved_sum(v, axis, here, pieces):
    v = v.reshape(pieces, -1, v.shape[-1])
    pick = functools.partial(lax.dynamic_index_in_dim, axis=0, keepdims=False)
    got = [swapped(pick(v, here ^ k), axis, k) for k in range(1, pieces)]
    if pieces == 2:
        return pick(v, here) + got[0]
    return (pick(v, here) + got[0]) + (got[1] + got[2])


def exchanged_sum(v, axis):
    a, b, c = [swapped(v, axis, k) for k in (1, 2, 3)]
    return (v + a) + (b + c)


def gathered(v, axis, here, pieces):
    parts = [v] + [swapped(v, axis, k) for k in range(1, pieces)]

    def part_of(i):
        which = here ^ i
        if pieces == 2:
            return jnp.where(which == 0, parts[0], parts[1])
        return jnp.where(
            which < 2,
            jnp.where(which == 0, parts[0], parts[1]),
            jnp.where(which == 2, parts[2], parts[3]),
        )

    return jnp.concatenate([part_of(i) for i in range(pieces)], 0)


BOUNDS = (4, 7, 10, 12, 15, 16)


def shards(field, probe, measured, offsets, live):
    rows, cols = field.shape[1:]
    base = jnp.stack([lax.axis_index("scan") * rows, lax.axis_index("mode") * cols])
    off = offsets - base[None, :]
    tabs = [jnp.asarray(t) for t in tables()]
    probe_rows = probe.reshape(2, 2, 128, 2, 256).transpose(0, 1, 3, 2, 4).reshape(probe.shape)
    tie = lax.optimization_barrier
    head, rest = tie((field[:, :, : LANE * BOUNDS[0]], field))
    halos = [shifted(head, "scan", -1, "halo_0")]
    for i, (a, b) in enumerate(zip(BOUNDS[:-1], BOUNDS[1:])):
        part = rest[:, :, LANE * a : LANE * b]
        halos.append(shifted(part, "scan", -1, f"halo_{i + 1}"))
    right = shifted(field[:, :, :SIZE], "mode", -1, "right")
    corner = shifted(halos[0][:, :, :SIZE], "mode", -1, "corner")
    carry = jnp.zeros((2, 2, 2 * SIZE, LANE), f32)
    acc = jnp.zeros(probe.shape, f32)
    ends = [b - 2 for b in BOUNDS[:-1]] + [BOUNDS[-1]]
    plan = [(a, b - a) for a, b in zip([0] + ends[:-1], ends)]
    uppers, lowers, comings = [], [], []
    for i, (first, count) in enumerate(plan):
        after = {2: (right,), 3: (1,), 4: (2,), 5: (3,)}.get(i, ())
        after = [comings[j] if isinstance(j, int) else j for j in after]
        upper, lower, carry, acc = run_group(
            first, count, BOUNDS, live, off, field, halos, right, corner, measured, probe_rows, tabs, carry, acc, after
        )
        uppers.append(upper)
        lowers.append(lower)
        early = 0 < i < len(plan) - 1
        comings.append(shifted(lower, "scan", 1, f"grad_{i}") if early else None)
    s, m = lax.axis_index("scan"), lax.axis_index("mode")
    core, y = m % 2, (s // 16) * 2 + m // 2
    v = halved_sum(acc.reshape(1024, 256), 0, core, 2)
    v, comings[4], final = tie((v, comings[4], lowers[5]))
    comings[5] = shifted(final, "scan", 1, "grad_5")
    v = halved_sum(v, 1, y, 4)
    v, carry = tie((v, carry))
    over = shifted(carry, "mode", 1, "over")
    v = exchanged_sum(v, 2)
    sources = [(first, array) for (first, _), pair in zip(plan, zip(uppers, comings)) for array in pair]
    step = finish(range(2, 13), sources[2:10], field.shape, None)
    v, comings[5], step = tie((v, comings[5], step))
    v = exchanged_sum(v, 3)
    slots_all = lax.axis_size("scan") * lax.axis_size("mode") * SLOTS
    v = v * (1.0 / math.sqrt(slots_all))
    v, over = tie((v, over))
    comings[0] = shifted(lowers[0] + over[:, :, SIZE:], "scan", 1, "grad_0")
    v = gathered(v, 1, y, 4)
    v, comings[0] = tie((v, comings[0]))
    probe_step = gathered(v, 0, core, 2).reshape(probe.shape)
    rest = [(0, uppers[0]), (0, comings[0]), (0, over), (13, uppers[5]), (13, comings[5])]
    step = finish([0, 1, 13, 14, 15], rest, field.shape, step)
    return (step, probe_step)


def solution(mesh):
    in_specs = (
        P(None, "scan", "mode"),
        P(),
        P(AXES, None, None),
        P(AXES, None),
        P(AXES),
    )
    out_specs = (P(None, "scan", "mode"), P())
    return jax.shard_map(shards, mesh=mesh, in_specs=in_specs, out_specs=out_specs, check_vma=False)
```

```python
import functools
import math

import jax
import jax.numpy as jnp
import ml_dtypes
import numpy as np
from jax import lax
from jax.experimental import pallas as pl
from jax.experimental.pallas import tpu as pltpu
from jax.sharding import PartitionSpec as P

SLOTS = 16
SIZE = 256
LANE = 128
CHUNK = 256
FLOOR = 0.5
AXES = ("scan", "mode")
f32 = jnp.float32
bf16 = jnp.bfloat16


def tables():
    n = SIZE
    place = np.arange(n)
    angles = (place[:, None] * place[None, :] % n) * (2.0 * math.pi / n)
    c = np.cos(angles) / math.sqrt(n)
    s = np.sin(angles) / math.sqrt(n)
    rows = np.concatenate([place[0 : n // 2 : 2], place[1 : n // 2 : 2]])

    def block(c, s):
        return np.block([[c, s], [-s, c]])

    def halves(c, s):
        return np.stack([block(c[rows, p::2], s[rows, p::2]) for p in (0, 1)])

    both = (halves(c, s), block(c, -s), halves(c, -s), block(c, s))
    return [t.astype(ml_dtypes.bfloat16) for t in both]


def stack(parts, axis):
    return jnp.concatenate(parts, axis)


def left_product(table, even, odd):
    dot = functools.partial(jnp.dot, preferred_element_type=f32)
    a = dot(table[0], even)
    b = dot(table[1], odd)
    return (a + b).astype(bf16), (a - b).astype(bf16)


def pattern(ext, grad, acc, probe, frame, tabs, r, c):
    left_fwd, right_fwd, left_bwd, right_bwd = tabs
    n = SIZE
    half, quarter = n // 2, n // 4
    block = c // LANE
    shift = c % LANE
    dot = functools.partial(jnp.dot, preferred_element_type=f32)

    def window(part):
        cols = []
        for j in range(3):
            view = ext.at[part, block + j]
            cols.append(stack([view[pl.ds(r + p, half, stride=2), :] for p in (0, 1)], 0))
        return pltpu.roll(stack(cols, 1), 3 * LANE - shift, 1)[:, :n]

    wr = window(0)
    wi = window(1)
    x_re = [probe[k, 0] * wr - probe[k, 1] * wi for k in (0, 1)]
    x_im = [probe[k, 0] * wi + probe[k, 1] * wr for k in (0, 1)]

    def rows_of(p):
        rows = slice(half * p, half * (p + 1))
        return stack([stack([x_re[k][rows], x_im[k][rows]], 0) for k in (0, 1)], 1).astype(bf16)

    sums = left_product(left_fwd, rows_of(0), rows_of(1))
    h = stack(
        [
            stack([t[:half, n * k : n * (k + 1)], t[half:, n * k : n * (k + 1)]], 1)
            for k in (0, 1)
            for t in sums
        ],
        0,
    )
    far = dot(h, right_fwd[...])
    sq = far * far
    intensity = (sq[:n, :n] + sq[:n, n:]) + (sq[n:, :n] + sq[n:, n:])
    amplitude = stack(
        [
            stack([frame.at[b][pl.ds(row, quarter, stride=2), :] for b in (0, 1)], 1)
            for row in (0, 1, half, half + 1)
        ],
        0,
    )
    factor = amplitude * lax.rsqrt(jnp.maximum(intensity, FLOOR)) - 1.0
    change = [
        [(far[n * k : n * (k + 1), n * p : n * (p + 1)] * factor).astype(bf16) for p in (0, 1)]
        for k in (0, 1)
    ]

    def quarters(q):
        return stack(
            [
                stack([change[k][p][at : at + quarter] for p in (0, 1) for at in (q, q + half)], 0)
                for k in (0, 1)
            ],
            1,
        )

    plus, minus = left_product(left_bwd, quarters(0), quarters(quarter))
    h = stack(
        [
            stack(
                [
                    t[at : at + quarter, n * k : n * (k + 1)],
                    t[half + at : half + at + quarter, n * k : n * (k + 1)],
                ],
                1,
            )
            for k in (0, 1)
            for t, at in ((plus, 0), (minus, 0), (plus, quarter), (minus, quarter))
        ],
        0,
    )
    delta = dot(h, right_bwd[...])
    terms = [None, None]
    for k in (0, 1):
        d_re = delta[n * k : n * k + n, :n]
        d_im = delta[n * k : n * k + n, n:]
        new = (
            probe[k, 0] * d_re + probe[k, 1] * d_im,
            probe[k, 0] * d_im - probe[k, 1] * d_re,
        )
        terms = [b if a is None else a + b for a, b in zip(terms, new)]
        acc[k, 0] += wr * d_re + wi * d_im
        acc[k, 1] += wr * d_im - wi * d_re
    blank = jnp.zeros((n, LANE), f32)
    for part, term in enumerate(terms):
        moved = pltpu.roll(stack([term, blank], 1), shift, 1)
        for j in range(3):
            view = grad.at[part, block + j]
            for p in (0, 1):
                rows = pl.ds(r + p, half, stride=2)
                view[rows, :] = view[rows, :] + moved[half * p : half * (p + 1), LANE * j : LANE * (j + 1)]


def group_kernel(first, count, homes, n_after, last, live, off, *refs):
    wide = count + 2
    refs = list(refs)
    sources = refs[: len(homes[2])]
    refs = refs[len(homes[2]) + n_after :]
    measured, probe, t0, t1, t2, t3, carry, acc_in = refs[:8]
    upper, lower, carry_out, acc = refs[8:12]
    ext, grad, frame, picked, load_sem, frame_sem = refs[-6:]

    def pick(q, n):
        b = off[q, 1] // LANE - first
        picked[n] = q
        return n + jnp.where((b >= 0) & (b < count), 1, 0)

    n = lax.fori_loop(0, live[0], pick, jnp.int32(0))

    def loads():
        out = []
        for half in (0, 1):
            for b in range(wide):
                which, row, at = homes[half][b]
                src = sources[which].at[:, row : row + SIZE, at : at + LANE]
                dst = ext.at[:, b, SIZE * half : SIZE * (half + 1), :]
                out.append(pltpu.make_async_copy(src, dst, load_sem.at[2 * b + half]))
        return out

    def frame_copies(i):
        slot = i % 2
        return [
            pltpu.make_async_copy(
                measured.at[picked[i], :, LANE * b : LANE * (b + 1)],
                frame.at[slot, b],
                frame_sem.at[2 * slot + b],
            )
            for b in (0, 1)
        ]

    @pl.when(n > 0)
    def _():
        for copy in loads():
            copy.start()
        for copy in frame_copies(0):
            copy.start()

    grad[:, 0:2] = carry[...]
    grad[:, 2:] = jnp.zeros((2, count, 2 * SIZE, LANE), f32)
    acc[...] = acc_in[...]

    @pl.when(n > 0)
    def _():
        for copy in loads():
            copy.wait()

    def step(i, _):
        @pl.when(i + 1 < n)
        def _():
            for copy in frame_copies(i + 1):
                copy.start()

        for copy in frame_copies(i):
            copy.wait()
        q = picked[i]
        pattern(
            ext, grad, acc, probe, frame.at[i % 2], (t0, t1, t2, t3), off[q, 0], off[q, 1] - first * LANE
        )
        return 0

    lax.fori_loop(0, n, step, 0)
    upper[...] = grad[:, 0:count, :SIZE]
    lower[...] = grad[:, 0:count, SIZE:]
    carry_out[...] = grad[:, count:]
    if last:
        for k in (0, 1):
            for part in (0, 1):
                for b in (0, 1):
                    view = ext.at[part, 2 * k + b]
                    at = slice(LANE * b, LANE * (b + 1))
                    for p in (0, 1):
                        rows = pl.ds(p, SIZE // 2, stride=2)
                        view[rows, :] = acc[k, part, LANE * p : LANE * (p + 1), at]
                    acc[k, part, :, at] = view[0:SIZE, :]


IN_HBM = pl.BlockSpec(memory_space=pltpu.HBM)
IN_SMEM = pl.BlockSpec(memory_space=pltpu.SMEM)
IN_VMEM = pl.BlockSpec(memory_space=pltpu.VMEM)


def run_group(first, count, bounds, live, off, field, halos, right, measured, probe, tabs, carry, acc, after):
    wide = count + 2
    arrays, homes = [], [[], []]

    def index_in(array):
        for i, other in enumerate(arrays):
            if other is array:
                return i
        arrays.append(array)
        return len(arrays) - 1

    for b in range(first, first + wide):
        chunk = next(i for i, end in enumerate(bounds) if b < end)
        begin = bounds[chunk - 1] if chunk else 0
        own = field.shape[2] // LANE
        if b < own:
            homes[0].append((index_in(field), 0, b * LANE))
        else:
            homes[0].append((index_in(right), 0, (b - own) * LANE))
        homes[1].append((index_in(halos[chunk]), 0, (b - begin) * LANE))
    homes.append(arrays)
    args = [live, off, *arrays, *after, measured, probe, *tabs, carry, acc]
    specs = [IN_SMEM] * 2 + [IN_HBM] * (1 + len(arrays) + len(after)) + [IN_VMEM] * 7
    part = jax.ShapeDtypeStruct((2, count, SIZE, LANE), f32)
    last = first + count + 2 == bounds[-1]
    whole = jax.ShapeDtypeStruct((2, 2, 2 * SIZE, LANE), f32)
    out_shape = (part, part, whole)
    out_shape += (jax.ShapeDtypeStruct((2, 2, SIZE, SIZE), f32),)
    return pl.pallas_call(
        functools.partial(group_kernel, first, count, (homes[0], homes[1], [None] * len(arrays)),
            len(after), last),
        out_shape=out_shape,
        in_specs=specs,
        out_specs=(IN_VMEM,) * len(out_shape),
        scratch_shapes=[
            pltpu.VMEM((2, wide, 2 * SIZE, LANE), f32),
            pltpu.VMEM((2, wide, 2 * SIZE, LANE), f32),
            pltpu.VMEM((2, 2, SIZE, LANE), f32),
            pltpu.SMEM((SLOTS + 1,), jnp.int32),
            pltpu.SemaphoreType.DMA((2 * wide,)),
            pltpu.SemaphoreType.DMA((4,)),
        ],
        compiler_params=pltpu.CompilerParams(vmem_limit_bytes=44 * 2**20),
        cost_estimate=pl.CostEstimate(flops=2**33, bytes_accessed=2**12, transcendentals=0),
        name=f"group_{first}",
    )(*args)


def finish_kernel(blocks, terms, *refs):
    out, buf, sem = refs[-3:]
    copies = []
    for at, (block, many) in enumerate(zip(blocks, terms)):
        value = None
        for which, b in many:
            term = refs[which][:, b, :SIZE]
            value = term if value is None else value + term
        buf[at] = value
        copy = pltpu.make_async_copy(
            buf.at[at], out.at[:, :, block * LANE : (block + 1) * LANE], sem.at[at]
        )
        copy.start()
        copies.append(copy)
    for copy in copies:
        copy.wait()


def finish(blocks, sources, shape, onto):
    args = [array for _, array in sources]
    terms = tuple(
        tuple(
            (i, block - first)
            for i, (first, array) in enumerate(sources)
            if first <= block < first + array.shape[1]
        )
        for block in blocks
    )
    specs = [IN_VMEM] * len(args)
    aliases = {}
    if onto is not None:
        aliases = {len(args): 0}
        args.append(onto)
        specs.append(IN_HBM)
    return pl.pallas_call(
        functools.partial(finish_kernel, tuple(blocks), terms),
        out_shape=jax.ShapeDtypeStruct(shape, f32),
        in_specs=specs,
        out_specs=IN_HBM,
        scratch_shapes=[
            pltpu.VMEM((len(blocks), 2, SIZE, LANE), f32),
            pltpu.SemaphoreType.DMA((len(blocks),)),
        ],
        input_output_aliases=aliases,
        compiler_params=pltpu.CompilerParams(vmem_limit_bytes=24 * 2**20),
        name=f"finish_{blocks[0]}",
    )(*args)


def shifted(array, axis, by, name):
    count = lax.axis_size(axis)
    pairs = [(i, i + by) for i in range(count) if 0 <= i + by < count]
    with jax.named_scope(name):
        return lax.ppermute(array, axis, pairs)


def place_of(index):
    s, m = divmod(index, 4)
    return [m % 2, (s // 16) * 2 + m // 2, (s // 4) % 4, s % 4]


def index_of(place):
    core, y, z, x = place
    return ((y // 2) * 16 + z * 4 + x) * 4 + (y % 2) * 2 + core


def swapped(array, axis, bits):
    pairs = []
    for i in range(128):
        place = place_of(i)
        place[axis] ^= bits
        pairs.append((i, index_of(place)))
    with jax.named_scope("swap_" + "cyzx"[axis] + str(bits)):
        return lax.ppermute(array, AXES, pairs)


def halved_sum(v, axis, here, pieces, held=None):
    v = v.reshape(pieces, -1, v.shape[-1])
    pick = functools.partial(lax.dynamic_index_in_dim, axis=0, keepdims=False)
    got = [swapped(pick(v, here ^ k), axis, k) for k in range(1, pieces)]
    if pieces == 2:
        return pick(v, here) + got[0], held
    if held is not None:
        got[0], held = lax.optimization_barrier((got[0], held))
    return (pick(v, here) + got[0]) + (got[1] + got[2]), held


def exchanged_sum(v, axis, held=None):
    a, b, c = [swapped(v, axis, k) for k in (1, 2, 3)]
    if held is not None:
        a, held = lax.optimization_barrier((a, held))
    return (v + a) + (b + c), held


def gathered(v, axis, here, pieces):
    parts = [v] + [swapped(v, axis, k) for k in range(1, pieces)]

    def part_of(i):
        which = here ^ i
        if pieces == 2:
            return jnp.where(which == 0, parts[0], parts[1])
        return jnp.where(
            which < 2,
            jnp.where(which == 0, parts[0], parts[1]),
            jnp.where(which == 2, parts[2], parts[3]),
        )

    return jnp.concatenate([part_of(i) for i in range(pieces)], 0)


BOUNDS = (4, 7, 10, 13, 16, 18)


def shards(field, probe, measured, offsets, live):
    rows, cols = field.shape[1:]
    base = jnp.stack([lax.axis_index("scan") * rows, lax.axis_index("mode") * cols])
    off = offsets - base[None, :]
    tabs = [jnp.asarray(t) for t in tables()]
    probe_rows = probe.reshape(2, 2, 128, 2, 256).transpose(0, 1, 3, 2, 4).reshape(probe.shape)
    tie = lax.optimization_barrier
    beside, rest = tie((field[:, :, :SIZE], field))
    right = shifted(beside, "mode", -1, "right")
    head, rest = tie((rest[:, :, : LANE * BOUNDS[0]], rest))
    halos = [shifted(head, "scan", -1, "halo_0")]
    for i, (a, b) in enumerate(zip(BOUNDS[:-1], BOUNDS[1:])):
        part = right if a * LANE == cols else rest[:, :, LANE * a : LANE * b]
        halos.append(shifted(part, "scan", -1, f"halo_{i + 1}"))
    carry = jnp.zeros((2, 2, 2 * SIZE, LANE), f32)
    acc = jnp.zeros(probe.shape, f32)
    ends = [b - 2 for b in BOUNDS]
    plan = [(a, b - a) for a, b in zip([0] + ends[:-1], ends)]
    uppers, lowers, comings = [], [], []
    for i, (first, count) in enumerate(plan):
        after = {0: (right,), 3: (1,), 4: (2,), 5: (3,)}.get(i, ())
        after = [comings[j] if isinstance(j, int) else j for j in after]
        upper, lower, carry, acc = run_group(
            first, count, BOUNDS, live, off, field, halos, right, measured, probe_rows, tabs, carry, acc, after
        )
        uppers.append(upper)
        lowers.append(lower)
        early = 0 < i < len(plan) - 1
        comings.append(shifted(lower, "scan", 1, f"grad_{i}") if early else None)
    s, m = lax.axis_index("scan"), lax.axis_index("mode")
    core, y = m % 2, (s // 16) * 2 + m // 2
    v, _ = halved_sum(acc.reshape(1024, 256), 0, core, 2)
    v, comings[4], final, carry = tie((v, comings[4], lowers[5], carry))
    comings[5] = shifted(final, "scan", 1, "grad_5")
    over = shifted(carry, "mode", 1, "over")
    v, _ = halved_sum(v, 1, y, 4)
    v, _ = exchanged_sum(v, 2)
    sources = [(first, array) for (first, _), pair in zip(plan, zip(uppers, comings)) for array in pair]
    step = finish(range(2, 14), sources[2:10], field.shape, None)
    v, comings[5], step = tie((v, comings[5], step))
    v, over = exchanged_sum(v, 3, over)
    slots_all = lax.axis_size("scan") * lax.axis_size("mode") * SLOTS
    v = v * (1.0 / math.sqrt(slots_all))
    comings[0] = shifted(lowers[0] + over[:, :, SIZE:], "scan", 1, "grad_0")
    v = gathered(v, 1, y, 4)
    v, comings[0] = tie((v, comings[0]))
    probe_step = gathered(v, 0, core, 2).reshape(probe.shape)
    rest = [(0, uppers[0]), (0, comings[0]), (0, over), *sources[10:]]
    step = finish([0, 1, 14, 15], rest, field.shape, step)
    return (step, probe_step)


def solution(mesh):
    in_specs = (
        P(None, "scan", "mode"),
        P(),
        P(AXES, None, None),
        P(AXES, None),
        P(AXES),
    )
    out_specs = (P(None, "scan", "mode"), P())
    return jax.shard_map(shards, mesh=mesh, in_specs=in_specs, out_specs=out_specs, check_vma=False)
```

```python
import functools
import math

import jax
import jax.numpy as jnp
import ml_dtypes
import numpy as np
from jax import lax
from jax.experimental import pallas as pl
from jax.experimental.pallas import tpu as pltpu
from jax.sharding import PartitionSpec as P

SLOTS = 16
SIZE = 256
LANE = 128
CHUNK = 256
FLOOR = 0.5
AXES = ("scan", "mode")
f32 = jnp.float32
bf16 = jnp.bfloat16


def tables():
    n = SIZE
    place = np.arange(n)
    angles = (place[:, None] * place[None, :] % n) * (2.0 * math.pi / n)
    c = np.cos(angles) / math.sqrt(n)
    s = np.sin(angles) / math.sqrt(n)
    rows = np.concatenate([place[0 : n // 2 : 2], place[1 : n // 2 : 2]])

    def block(c, s):
        return np.block([[c, s], [-s, c]])

    def halves(c, s):
        return np.stack([block(c[rows, p::2], s[rows, p::2]) for p in (0, 1)])

    both = (halves(c, s), block(c, -s), halves(c, -s), block(c, s))
    return [t.astype(ml_dtypes.bfloat16) for t in both]


def stack(parts, axis):
    return jnp.concatenate(parts, axis)


def left_product(table, even, odd):
    dot = functools.partial(jnp.dot, preferred_element_type=f32)
    a = dot(table[0], even)
    b = dot(table[1], odd)
    return (a + b).astype(bf16), (a - b).astype(bf16)


def pattern(ext, grad, acc, probe, frame, tabs, r, c):
    left_fwd, right_fwd, left_bwd, right_bwd = tabs
    n = SIZE
    half, quarter = n // 2, n // 4
    block = c // LANE
    shift = c % LANE
    dot = functools.partial(jnp.dot, preferred_element_type=f32)

    def window(part):
        cols = []
        for j in range(3):
            view = ext.at[part, block + j]
            cols.append(stack([view[pl.ds(r + p, half, stride=2), :] for p in (0, 1)], 0))
        return pltpu.roll(stack(cols, 1), 3 * LANE - shift, 1)[:, :n]

    wr = window(0)
    wi = window(1)
    x_re = [probe[k, 0] * wr - probe[k, 1] * wi for k in (0, 1)]
    x_im = [probe[k, 0] * wi + probe[k, 1] * wr for k in (0, 1)]

    def rows_of(p):
        rows = slice(half * p, half * (p + 1))
        return stack([stack([x_re[k][rows], x_im[k][rows]], 0) for k in (0, 1)], 1).astype(bf16)

    sums = left_product(left_fwd, rows_of(0), rows_of(1))
    h = stack(
        [
            stack([t[:half, n * k : n * (k + 1)], t[half:, n * k : n * (k + 1)]], 1)
            for k in (0, 1)
            for t in sums
        ],
        0,
    )
    far = dot(h, right_fwd[...])
    sq = far * far
    intensity = (sq[:n, :n] + sq[:n, n:]) + (sq[n:, :n] + sq[n:, n:])
    amplitude = stack(
        [
            stack([frame.at[b][pl.ds(row, quarter, stride=2), :] for b in (0, 1)], 1)
            for row in (0, 1, half, half + 1)
        ],
        0,
    )
    factor = amplitude * lax.rsqrt(jnp.maximum(intensity, FLOOR)) - 1.0
    change = [
        [(far[n * k : n * (k + 1), n * p : n * (p + 1)] * factor).astype(bf16) for p in (0, 1)]
        for k in (0, 1)
    ]

    def quarters(q):
        return stack(
            [
                stack([change[k][p][at : at + quarter] for p in (0, 1) for at in (q, q + half)], 0)
                for k in (0, 1)
            ],
            1,
        )

    plus, minus = left_product(left_bwd, quarters(0), quarters(quarter))
    h = stack(
        [
            stack(
                [
                    t[at : at + quarter, n * k : n * (k + 1)],
                    t[half + at : half + at + quarter, n * k : n * (k + 1)],
                ],
                1,
            )
            for k in (0, 1)
            for t, at in ((plus, 0), (minus, 0), (plus, quarter), (minus, quarter))
        ],
        0,
    )
    delta = dot(h, right_bwd[...])
    terms = [None, None]
    for k in (0, 1):
        d_re = delta[n * k : n * k + n, :n]
        d_im = delta[n * k : n * k + n, n:]
        new = (
            probe[k, 0] * d_re + probe[k, 1] * d_im,
            probe[k, 0] * d_im - probe[k, 1] * d_re,
        )
        terms = [b if a is None else a + b for a, b in zip(terms, new)]
        acc[k, 0] += wr * d_re + wi * d_im
        acc[k, 1] += wr * d_im - wi * d_re
    blank = jnp.zeros((n, LANE), f32)
    for part, term in enumerate(terms):
        moved = pltpu.roll(stack([term, blank], 1), shift, 1)
        for j in range(3):
            view = grad.at[part, block + j]
            for p in (0, 1):
                rows = pl.ds(r + p, half, stride=2)
                view[rows, :] = view[rows, :] + moved[half * p : half * (p + 1), LANE * j : LANE * (j + 1)]


def group_kernel(first, count, homes, n_after, last, live, off, *refs):
    wide = count + 2
    refs = list(refs)
    sources = refs[: len(homes[2])]
    refs = refs[len(homes[2]) + n_after :]
    measured, probe, t0, t1, t2, t3, carry, acc_in = refs[:8]
    upper, lower, carry_out, acc = refs[8:12]
    ext, grad, frame, picked, load_sem, frame_sem = refs[-6:]

    def pick(q, n):
        b = off[q, 1] // LANE - first
        picked[n] = q
        return n + jnp.where((b >= 0) & (b < count), 1, 0)

    n = lax.fori_loop(0, live[0], pick, jnp.int32(0))

    def loads():
        out = []
        for half in (0, 1):
            for b in range(wide):
                which, row, at = homes[half][b]
                src = sources[which].at[:, row : row + SIZE, at : at + LANE]
                dst = ext.at[:, b, SIZE * half : SIZE * (half + 1), :]
                out.append(pltpu.make_async_copy(src, dst, load_sem.at[2 * b + half]))
        return out

    def frame_copies(i):
        slot = i % 2
        return [
            pltpu.make_async_copy(
                measured.at[picked[i], :, LANE * b : LANE * (b + 1)],
                frame.at[slot, b],
                frame_sem.at[2 * slot + b],
            )
            for b in (0, 1)
        ]

    @pl.when(n > 0)
    def _():
        for copy in loads():
            copy.start()
        for copy in frame_copies(0):
            copy.start()

    grad[:, 0:2] = carry[...]
    grad[:, 2:] = jnp.zeros((2, count, 2 * SIZE, LANE), f32)
    acc[...] = acc_in[...]

    @pl.when(n > 0)
    def _():
        for copy in loads():
            copy.wait()

    def step(i, _):
        @pl.when(i + 1 < n)
        def _():
            for copy in frame_copies(i + 1):
                copy.start()

        for copy in frame_copies(i):
            copy.wait()
        q = picked[i]
        pattern(
            ext, grad, acc, probe, frame.at[i % 2], (t0, t1, t2, t3), off[q, 0], off[q, 1] - first * LANE
        )
        return 0

    lax.fori_loop(0, n, step, 0)
    upper[...] = grad[:, 0:count, :SIZE]
    lower[...] = grad[:, 0:count, SIZE:]
    carry_out[...] = grad[:, count:]
    if last:
        for k in (0, 1):
            for part in (0, 1):
                for b in (0, 1):
                    view = ext.at[part, 2 * k + b]
                    at = slice(LANE * b, LANE * (b + 1))
                    for p in (0, 1):
                        rows = pl.ds(p, SIZE // 2, stride=2)
                        view[rows, :] = acc[k, part, LANE * p : LANE * (p + 1), at]
                    acc[k, part, :, at] = view[0:SIZE, :]


IN_HBM = pl.BlockSpec(memory_space=pltpu.HBM)
IN_SMEM = pl.BlockSpec(memory_space=pltpu.SMEM)
IN_VMEM = pl.BlockSpec(memory_space=pltpu.VMEM)


def run_group(first, count, bounds, live, off, field, halos, corner, measured, probe, tabs, carry, acc, after):
    wide = count + 2
    arrays, homes = [], [[], []]

    def index_in(array):
        for i, other in enumerate(arrays):
            if other is array:
                return i
        arrays.append(array)
        return len(arrays) - 1

    for b in range(first, first + wide):
        if b < bounds[-1]:
            chunk = next(i for i, end in enumerate(bounds) if b < end)
            begin = bounds[chunk - 1] if chunk else 0
            homes[0].append((index_in(field), 0, b * LANE))
            homes[1].append((index_in(halos[chunk]), 0, (b - begin) * LANE))
        else:
            at = (b - bounds[-1]) * LANE
            homes[0].append((index_in(corner), 0, at))
            homes[1].append((index_in(corner), SIZE, at))
    homes.append(arrays)
    args = [live, off, *arrays, *after, measured, probe, *tabs, carry, acc]
    specs = [IN_SMEM] * 2 + [IN_HBM] * (1 + len(arrays) + len(after)) + [IN_VMEM] * 7
    part = jax.ShapeDtypeStruct((2, count, SIZE, LANE), f32)
    last = first + count == bounds[-1]
    whole = jax.ShapeDtypeStruct((2, 2, 2 * SIZE, LANE), f32)
    out_shape = (part, part, whole)
    out_shape += (jax.ShapeDtypeStruct((2, 2, SIZE, SIZE), f32),)
    return pl.pallas_call(
        functools.partial(group_kernel, first, count, (homes[0], homes[1], [None] * len(arrays)),
            len(after), last),
        out_shape=out_shape,
        in_specs=specs,
        out_specs=(IN_VMEM,) * len(out_shape),
        scratch_shapes=[
            pltpu.VMEM((2, wide, 2 * SIZE, LANE), f32),
            pltpu.VMEM((2, wide, 2 * SIZE, LANE), f32),
            pltpu.VMEM((2, 2, SIZE, LANE), f32),
            pltpu.SMEM((SLOTS + 1,), jnp.int32),
            pltpu.SemaphoreType.DMA((2 * wide,)),
            pltpu.SemaphoreType.DMA((4,)),
        ],
        compiler_params=pltpu.CompilerParams(vmem_limit_bytes=44 * 2**20),
        cost_estimate=pl.CostEstimate(flops=2**34, bytes_accessed=2**12, transcendentals=0),
        name=f"group_{first}",
    )(*args)


def finish_kernel(blocks, terms, *refs):
    out, buf, sem = refs[-3:]
    copies = []
    for at, (block, many) in enumerate(zip(blocks, terms)):
        value = None
        for which, b in many:
            term = refs[which][:, b, :SIZE]
            value = term if value is None else value + term
        buf[at] = value
        copy = pltpu.make_async_copy(
            buf.at[at], out.at[:, :, block * LANE : (block + 1) * LANE], sem.at[at]
        )
        copy.start()
        copies.append(copy)
    for copy in copies:
        copy.wait()


def finish(blocks, sources, shape, onto):
    args = [array for _, array in sources]
    terms = tuple(
        tuple(
            (i, block - first)
            for i, (first, array) in enumerate(sources)
            if first <= block < first + array.shape[1]
        )
        for block in blocks
    )
    specs = [IN_VMEM] * len(args)
    aliases = {}
    if onto is not None:
        aliases = {len(args): 0}
        args.append(onto)
        specs.append(IN_HBM)
    return pl.pallas_call(
        functools.partial(finish_kernel, tuple(blocks), terms),
        out_shape=jax.ShapeDtypeStruct(shape, f32),
        in_specs=specs,
        out_specs=IN_HBM,
        scratch_shapes=[
            pltpu.VMEM((len(blocks), 2, SIZE, LANE), f32),
            pltpu.SemaphoreType.DMA((len(blocks),)),
        ],
        input_output_aliases=aliases,
        compiler_params=pltpu.CompilerParams(vmem_limit_bytes=24 * 2**20),
        name=f"finish_{blocks[0]}",
    )(*args)


def shifted(array, axis, by, name):
    count = lax.axis_size(axis)
    pairs = [(i, i + by) for i in range(count) if 0 <= i + by < count]
    with jax.named_scope(name):
        return lax.ppermute(array, axis, pairs)


def place_of(index):
    s, m = divmod(index, 4)
    return [m % 2, (s // 16) * 2 + m // 2, (s // 4) % 4, s % 4]


def index_of(place):
    core, y, z, x = place
    return ((y // 2) * 16 + z * 4 + x) * 4 + (y % 2) * 2 + core


def swapped(array, axis, bits):
    pairs = []
    for i in range(128):
        place = place_of(i)
        place[axis] ^= bits
        pairs.append((i, index_of(place)))
    with jax.named_scope("swap_" + "cyzx"[axis] + str(bits)):
        return lax.ppermute(array, AXES, pairs)


def halved_sum(v, axis, here, pieces, held=None):
    v = v.reshape(pieces, -1, v.shape[-1])
    pick = functools.partial(lax.dynamic_index_in_dim, axis=0, keepdims=False)
    got = [swapped(pick(v, here ^ k), axis, k) for k in range(1, pieces)]
    if pieces == 2:
        return pick(v, here) + got[0], held
    if held is not None:
        got[0], held = lax.optimization_barrier((got[0], held))
    return (pick(v, here) + got[0]) + (got[1] + got[2]), held


def exchanged_sum(v, axis, held=None):
    a, b, c = [swapped(v, axis, k) for k in (1, 2, 3)]
    if held is not None:
        a, held = lax.optimization_barrier((a, held))
    return (v + a) + (b + c), held


def gathered(v, axis, here, pieces):
    parts = [v] + [swapped(v, axis, k) for k in range(1, pieces)]

    def part_of(i):
        which = here ^ i
        if pieces == 2:
            return jnp.where(which == 0, parts[0], parts[1])
        return jnp.where(
            which < 2,
            jnp.where(which == 0, parts[0], parts[1]),
            jnp.where(which == 2, parts[2], parts[3]),
        )

    return jnp.concatenate([part_of(i) for i in range(pieces)], 0)


BOUNDS = (5, 9, 13, 15, 16)


def shards(field, probe, measured, offsets, live):
    rows, cols = field.shape[1:]
    base = jnp.stack([lax.axis_index("scan") * rows, lax.axis_index("mode") * cols])
    off = offsets - base[None, :]
    tabs = [jnp.asarray(t) for t in tables()]
    probe_rows = probe.reshape(2, 2, 128, 2, 256).transpose(0, 1, 3, 2, 4).reshape(probe.shape)
    tie = lax.optimization_barrier
    head, rest = tie((field[:, :, : LANE * BOUNDS[0]], field))
    halos = [shifted(head, "scan", -1, "halo_0")]
    for i, (a, b) in enumerate(zip(BOUNDS[:-1], BOUNDS[1:])):
        part = rest[:, :, LANE * a : LANE * b]
        halos.append(shifted(part, "scan", -1, f"halo_{i + 1}"))
    beside = jnp.concatenate([field[:, :, :SIZE], halos[0][:, :, :SIZE]], 1)
    corner = shifted(beside, "mode", -1, "corner")
    carry = jnp.zeros((2, 2, 2 * SIZE, LANE), f32)
    acc = jnp.zeros(probe.shape, f32)
    ends = [b - 2 for b in BOUNDS[:-1]] + [BOUNDS[-1]]
    plan = [(a, b - a) for a, b in zip([0] + ends[:-1], ends)]
    uppers, lowers, comings = [], [], []
    for i, (first, count) in enumerate(plan):
        after = {3: (1,)}.get(i, ())
        after = [comings[j] if isinstance(j, int) else j for j in after]
        upper, lower, carry, acc = run_group(
            first, count, BOUNDS, live, off, field, halos, corner, measured, probe_rows, tabs, carry, acc, after
        )
        uppers.append(upper)
        lowers.append(lower)
        early = 0 < i < len(plan) - 1
        comings.append(shifted(lower, "scan", 1, f"grad_{i}") if early else None)
    s, m = lax.axis_index("scan"), lax.axis_index("mode")
    core, y = m % 2, (s // 16) * 2 + m // 2
    v, _ = halved_sum(acc.reshape(1024, 256), 0, core, 2)
    v, comings[1], comings[2], final = tie((v, comings[1], comings[2], lowers[4]))
    comings[4] = shifted(final, "scan", 1, "grad_4")
    v, _ = halved_sum(v, 1, y, 4)
    v, comings[3], carry = tie((v, comings[3], carry))
    over = shifted(carry, "mode", 1, "over")
    v, _ = exchanged_sum(v, 2)
    sources = [(first, array) for (first, _), pair in zip(plan, zip(uppers, comings)) for array in pair]
    step = finish(range(3, 13), sources[2:8], field.shape, None)
    v, comings[4], step = tie((v, comings[4], step))
    v, _ = exchanged_sum(v, 3)
    v, over = tie((v, over))
    slots_all = lax.axis_size("scan") * lax.axis_size("mode") * SLOTS
    v = v * (1.0 / math.sqrt(slots_all))
    held = jnp.concatenate([lowers[0][:, :2] + over[:, :, SIZE:], lowers[0][:, 2:]], 1)
    comings[0] = shifted(held, "scan", 1, "grad_0")
    v = gathered(v, 1, y, 4)
    v, comings[0] = tie((v, comings[0]))
    probe_step = gathered(v, 0, core, 2).reshape(probe.shape)
    rest = [(0, uppers[0]), (0, comings[0]), (0, over), *sources[8:]]
    step = finish([0, 1, 2, 13, 14, 15], rest, field.shape, step)
    return (step, probe_step)


def solution(mesh):
    in_specs = (
        P(None, "scan", "mode"),
        P(),
        P(AXES, None, None),
        P(AXES, None),
        P(AXES),
    )
    out_specs = (P(None, "scan", "mode"), P())
    return jax.shard_map(shards, mesh=mesh, in_specs=in_specs, out_specs=out_specs, check_vma=False)
```

```python
import functools
import math

import jax
import jax.numpy as jnp
import ml_dtypes
import numpy as np
from jax import lax
from jax.experimental import pallas as pl
from jax.experimental.pallas import tpu as pltpu
from jax.sharding import PartitionSpec as P

SLOTS = 16
SIZE = 256
LANE = 128
CHUNK = 256
FLOOR = 0.5
AXES = ("scan", "mode")
f32 = jnp.float32
bf16 = jnp.bfloat16


def tables():
    n = SIZE
    place = np.arange(n)
    angles = (place[:, None] * place[None, :] % n) * (2.0 * math.pi / n)
    c = np.cos(angles) / math.sqrt(n)
    s = np.sin(angles) / math.sqrt(n)
    rows = np.concatenate([place[0 : n // 2 : 2], place[1 : n // 2 : 2]])

    def block(c, s):
        return np.block([[c, s], [-s, c]])

    def halves(c, s):
        return np.stack([block(c[rows, p::2], s[rows, p::2]) for p in (0, 1)])

    both = (halves(c, s), block(c, -s), halves(c, -s), block(c, s))
    return [t.astype(ml_dtypes.bfloat16) for t in both]


def stack(parts, axis):
    return jnp.concatenate(parts, axis)


def left_product(table, even, odd):
    dot = functools.partial(jnp.dot, preferred_element_type=f32)
    a = dot(table[0], even)
    b = dot(table[1], odd)
    return (a + b).astype(bf16), (a - b).astype(bf16)


def pattern(ext, grad, acc, probe, frame, tabs, r, c):
    left_fwd, right_fwd, left_bwd, right_bwd = tabs
    n = SIZE
    half, quarter = n // 2, n // 4
    block = c // LANE
    shift = c % LANE
    dot = functools.partial(jnp.dot, preferred_element_type=f32)

    def window(part):
        cols = []
        for j in range(3):
            view = ext.at[part, block + j]
            cols.append(stack([view[pl.ds(r + p, half, stride=2), :] for p in (0, 1)], 0))
        return pltpu.roll(stack(cols, 1), 3 * LANE - shift, 1)[:, :n]

    wr = window(0)
    wi = window(1)
    x_re = [probe[k, 0] * wr - probe[k, 1] * wi for k in (0, 1)]
    x_im = [probe[k, 0] * wi + probe[k, 1] * wr for k in (0, 1)]

    def rows_of(p):
        rows = slice(half * p, half * (p + 1))
        return stack([stack([x_re[k][rows], x_im[k][rows]], 0) for k in (0, 1)], 1).astype(bf16)

    sums = left_product(left_fwd, rows_of(0), rows_of(1))
    h = stack(
        [
            stack([t[:half, n * k : n * (k + 1)], t[half:, n * k : n * (k + 1)]], 1)
            for k in (0, 1)
            for t in sums
        ],
        0,
    )
    far = dot(h, right_fwd[...])
    sq = far * far
    intensity = (sq[:n, :n] + sq[:n, n:]) + (sq[n:, :n] + sq[n:, n:])
    amplitude = stack(
        [
            stack([frame.at[b][pl.ds(row, quarter, stride=2), :] for b in (0, 1)], 1)
            for row in (0, 1, half, half + 1)
        ],
        0,
    )
    factor = amplitude * lax.rsqrt(jnp.maximum(intensity, FLOOR)) - 1.0
    change = [
        [(far[n * k : n * (k + 1), n * p : n * (p + 1)] * factor).astype(bf16) for p in (0, 1)]
        for k in (0, 1)
    ]

    def quarters(q):
        return stack(
            [
                stack([change[k][p][at : at + quarter] for p in (0, 1) for at in (q, q + half)], 0)
                for k in (0, 1)
            ],
            1,
        )

    plus, minus = left_product(left_bwd, quarters(0), quarters(quarter))
    h = stack(
        [
            stack(
                [
                    t[at : at + quarter, n * k : n * (k + 1)],
                    t[half + at : half + at + quarter, n * k : n * (k + 1)],
                ],
                1,
            )
            for k in (0, 1)
            for t, at in ((plus, 0), (minus, 0), (plus, quarter), (minus, quarter))
        ],
        0,
    )
    delta = dot(h, right_bwd[...])
    terms = [None, None]
    for k in (0, 1):
        d_re = delta[n * k : n * k + n, :n]
        d_im = delta[n * k : n * k + n, n:]
        new = (
            probe[k, 0] * d_re + probe[k, 1] * d_im,
            probe[k, 0] * d_im - probe[k, 1] * d_re,
        )
        terms = [b if a is None else a + b for a, b in zip(terms, new)]
        acc[k, 0] += wr * d_re + wi * d_im
        acc[k, 1] += wr * d_im - wi * d_re
    blank = jnp.zeros((n, LANE), f32)
    for part, term in enumerate(terms):
        moved = pltpu.roll(stack([term, blank], 1), shift, 1)
        for j in range(3):
            view = grad.at[part, block + j]
            for p in (0, 1):
                rows = pl.ds(r + p, half, stride=2)
                view[rows, :] = view[rows, :] + moved[half * p : half * (p + 1), LANE * j : LANE * (j + 1)]


def group_kernel(first, count, homes, n_after, last, live, off, *refs):
    wide = count + 2
    refs = list(refs)
    sources = refs[: len(homes[2])]
    refs = refs[len(homes[2]) + n_after :]
    measured, probe, t0, t1, t2, t3, carry, acc_in = refs[:8]
    if last:
        upper, lower, over_upper, over_lower, acc = refs[8:13]
    else:
        upper, lower, carry_out, acc = refs[8:12]
    ext, grad, frame, picked, load_sem, frame_sem = refs[-6:]

    def pick(q, n):
        b = off[q, 1] // LANE - first
        picked[n] = q
        return n + jnp.where((b >= 0) & (b < count), 1, 0)

    n = lax.fori_loop(0, live[0], pick, jnp.int32(0))

    def loads():
        out = []
        for half in (0, 1):
            for b in range(wide):
                which, row, at = homes[half][b]
                src = sources[which].at[:, row : row + SIZE, at : at + LANE]
                dst = ext.at[:, b, SIZE * half : SIZE * (half + 1), :]
                out.append(pltpu.make_async_copy(src, dst, load_sem.at[2 * b + half]))
        return out

    def frame_copies(i):
        slot = i % 2
        return [
            pltpu.make_async_copy(
                measured.at[picked[i], :, LANE * b : LANE * (b + 1)],
                frame.at[slot, b],
                frame_sem.at[2 * slot + b],
            )
            for b in (0, 1)
        ]

    @pl.when(n > 0)
    def _():
        for copy in loads():
            copy.start()
        for copy in frame_copies(0):
            copy.start()

    grad[:, 0:2] = carry[...]
    grad[:, 2:] = jnp.zeros((2, count, 2 * SIZE, LANE), f32)
    acc[...] = acc_in[...]

    @pl.when(n > 0)
    def _():
        for copy in loads():
            copy.wait()

    def step(i, _):
        @pl.when(i + 1 < n)
        def _():
            for copy in frame_copies(i + 1):
                copy.start()

        for copy in frame_copies(i):
            copy.wait()
        q = picked[i]
        pattern(
            ext, grad, acc, probe, frame.at[i % 2], (t0, t1, t2, t3), off[q, 0], off[q, 1] - first * LANE
        )
        return 0

    lax.fori_loop(0, n, step, 0)
    upper[...] = grad[:, 0:count, :SIZE]
    lower[...] = grad[:, 0:count, SIZE:]
    if not last:
        carry_out[...] = grad[:, count:]
    if last:
        over_upper[...] = grad[:, count:, :SIZE]
        over_lower[...] = grad[:, count:, SIZE:]
        for k in (0, 1):
            for part in (0, 1):
                for b in (0, 1):
                    view = ext.at[part, 2 * k + b]
                    at = slice(LANE * b, LANE * (b + 1))
                    for p in (0, 1):
                        rows = pl.ds(p, SIZE // 2, stride=2)
                        view[rows, :] = acc[k, part, LANE * p : LANE * (p + 1), at]
                    acc[k, part, :, at] = view[0:SIZE, :]


IN_HBM = pl.BlockSpec(memory_space=pltpu.HBM)
IN_SMEM = pl.BlockSpec(memory_space=pltpu.SMEM)
IN_VMEM = pl.BlockSpec(memory_space=pltpu.VMEM)


def run_group(first, count, bounds, live, off, field, halos, corner, measured, probe, tabs, carry, acc, after):
    wide = count + 2
    arrays, homes = [], [[], []]

    def index_in(array):
        for i, other in enumerate(arrays):
            if other is array:
                return i
        arrays.append(array)
        return len(arrays) - 1

    for b in range(first, first + wide):
        if b < bounds[-1]:
            chunk = next(i for i, end in enumerate(bounds) if b < end)
            begin = bounds[chunk - 1] if chunk else 0
            homes[0].append((index_in(field), 0, b * LANE))
            homes[1].append((index_in(halos[chunk]), 0, (b - begin) * LANE))
        else:
            at = (b - bounds[-1]) * LANE
            homes[0].append((index_in(corner), 0, at))
            homes[1].append((index_in(corner), SIZE, at))
    homes.append(arrays)
    args = [live, off, *arrays, *after, measured, probe, *tabs, carry, acc]
    specs = [IN_SMEM] * 2 + [IN_HBM] * (1 + len(arrays) + len(after)) + [IN_VMEM] * 7
    part = jax.ShapeDtypeStruct((2, count, SIZE, LANE), f32)
    last = first + count == bounds[-1]
    whole = jax.ShapeDtypeStruct((2, 2, 2 * SIZE, LANE), f32)
    edge = jax.ShapeDtypeStruct((2, 2, SIZE, LANE), f32)
    out_shape = (part, part) + ((edge, edge) if last else (whole,))
    out_shape += (jax.ShapeDtypeStruct((2, 2, SIZE, SIZE), f32),)
    return pl.pallas_call(
        functools.partial(group_kernel, first, count, (homes[0], homes[1], [None] * len(arrays)),
            len(after), last),
        out_shape=out_shape,
        in_specs=specs,
        out_specs=(IN_VMEM,) * len(out_shape),
        scratch_shapes=[
            pltpu.VMEM((2, wide, 2 * SIZE, LANE), f32),
            pltpu.VMEM((2, wide, 2 * SIZE, LANE), f32),
            pltpu.VMEM((2, 2, SIZE, LANE), f32),
            pltpu.SMEM((SLOTS + 1,), jnp.int32),
            pltpu.SemaphoreType.DMA((2 * wide,)),
            pltpu.SemaphoreType.DMA((4,)),
        ],
        compiler_params=pltpu.CompilerParams(vmem_limit_bytes=44 * 2**20),
        cost_estimate=pl.CostEstimate(flops=2**33, bytes_accessed=2**12, transcendentals=0),
        name=f"group_{first}",
    )(*args)


def finish_kernel(blocks, terms, *refs):
    out, buf, sem = refs[-3:]
    copies = []
    for at, (block, many) in enumerate(zip(blocks, terms)):
        value = None
        for which, b in many:
            term = refs[which][:, b, :SIZE]
            value = term if value is None else value + term
        buf[at] = value
        copy = pltpu.make_async_copy(
            buf.at[at], out.at[:, :, block * LANE : (block + 1) * LANE], sem.at[at]
        )
        copy.start()
        copies.append(copy)
    for copy in copies:
        copy.wait()


def finish(blocks, sources, shape, onto):
    args = [array for _, array in sources]
    terms = tuple(
        tuple(
            (i, block - first)
            for i, (first, array) in enumerate(sources)
            if first <= block < first + array.shape[1]
        )
        for block in blocks
    )
    specs = [IN_VMEM] * len(args)
    aliases = {}
    if onto is not None:
        aliases = {len(args): 0}
        args.append(onto)
        specs.append(IN_HBM)
    return pl.pallas_call(
        functools.partial(finish_kernel, tuple(blocks), terms),
        out_shape=jax.ShapeDtypeStruct(shape, f32),
        in_specs=specs,
        out_specs=IN_HBM,
        scratch_shapes=[
            pltpu.VMEM((len(blocks), 2, SIZE, LANE), f32),
            pltpu.SemaphoreType.DMA((len(blocks),)),
        ],
        input_output_aliases=aliases,
        compiler_params=pltpu.CompilerParams(vmem_limit_bytes=24 * 2**20),
        name=f"finish_{blocks[0]}",
    )(*args)


def shifted(array, axis, by, name):
    count = lax.axis_size(axis)
    pairs = [(i, i + by) for i in range(count) if 0 <= i + by < count]
    with jax.named_scope(name):
        return lax.ppermute(array, axis, pairs)


def shifted_both(array, name):
    rows, cols = (lax.axis_size(a) for a in AXES)
    pairs = [
        (i * cols + j, (i + 1) * cols + j + 1) for i in range(rows - 1) for j in range(cols - 1)
    ]
    with jax.named_scope(name):
        return lax.ppermute(array, AXES, pairs)


def place_of(index):
    s, m = divmod(index, 4)
    return [m % 2, (s // 16) * 2 + m // 2, (s // 4) % 4, s % 4]


def index_of(place):
    core, y, z, x = place
    return ((y // 2) * 16 + z * 4 + x) * 4 + (y % 2) * 2 + core


def swapped(array, axis, bits):
    pairs = []
    for i in range(128):
        place = place_of(i)
        place[axis] ^= bits
        pairs.append((i, index_of(place)))
    with jax.named_scope("swap_" + "cyzx"[axis] + str(bits)):
        return lax.ppermute(array, AXES, pairs)


def halved_sum(v, axis, here, pieces, held=None):
    v = v.reshape(pieces, -1, v.shape[-1])
    pick = functools.partial(lax.dynamic_index_in_dim, axis=0, keepdims=False)
    got = [swapped(pick(v, here ^ k), axis, k) for k in range(1, pieces)]
    if pieces == 2:
        return pick(v, here) + got[0], held
    if held is not None:
        got[0], held = lax.optimization_barrier((got[0], held))
    return (pick(v, here) + got[0]) + (got[1] + got[2]), held


def exchanged_sum(v, axis, held=None):
    a, b, c = [swapped(v, axis, k) for k in (1, 2, 3)]
    if held is not None:
        a, held = lax.optimization_barrier((a, held))
    return (v + a) + (b + c), held


def gathered(v, axis, here, pieces):
    parts = [v] + [swapped(v, axis, k) for k in range(1, pieces)]

    def part_of(i):
        which = here ^ i
        if pieces == 2:
            return jnp.where(which == 0, parts[0], parts[1])
        return jnp.where(
            which < 2,
            jnp.where(which == 0, parts[0], parts[1]),
            jnp.where(which == 2, parts[2], parts[3]),
        )

    return jnp.concatenate([part_of(i) for i in range(pieces)], 0)


BOUNDS = (5, 9, 13, 15, 16)


def shards(field, probe, measured, offsets, live):
    rows, cols = field.shape[1:]
    base = jnp.stack([lax.axis_index("scan") * rows, lax.axis_index("mode") * cols])
    off = offsets - base[None, :]
    tabs = [jnp.asarray(t) for t in tables()]
    probe_rows = probe.reshape(2, 2, 128, 2, 256).transpose(0, 1, 3, 2, 4).reshape(probe.shape)
    tie = lax.optimization_barrier
    head, rest = tie((field[:, :, : LANE * BOUNDS[0]], field))
    halos = [shifted(head, "scan", -1, "halo_0")]
    for i, (a, b) in enumerate(zip(BOUNDS[:-1], BOUNDS[1:])):
        part = rest[:, :, LANE * a : LANE * b]
        if i == 1:
            part, halos[0] = tie((part, halos[0]))
        halos.append(shifted(part, "scan", -1, f"halo_{i + 1}"))
    beside = jnp.concatenate([field[:, :, :SIZE], halos[0][:, :, :SIZE]], 1)
    corner = shifted(beside, "mode", -1, "corner")
    carry = jnp.zeros((2, 2, 2 * SIZE, LANE), f32)
    acc = jnp.zeros(probe.shape, f32)
    ends = [b - 2 for b in BOUNDS[:-1]] + [BOUNDS[-1]]
    plan = [(a, b - a) for a, b in zip([0] + ends[:-1], ends)]
    uppers, lowers, comings = [], [], []
    for i, (first, count) in enumerate(plan):
        after = {2: (0,), 3: (1, corner)}.get(i, ())
        after = [comings[j] if isinstance(j, int) else j for j in after]
        upper, lower, *rest, acc = run_group(
            first, count, BOUNDS, live, off, field, halos, corner, measured, probe_rows, tabs, carry, acc, after
        )
        uppers.append(upper)
        lowers.append(lower)
        if i + 1 < len(plan):
            carry = rest[0]
            comings.append(shifted(lower, "scan", 1, f"grad_{i}"))
    over_upper, over_lower = rest
    s, m = lax.axis_index("scan"), lax.axis_index("mode")
    core, y = m % 2, (s // 16) * 2 + m // 2
    v, _ = halved_sum(acc.reshape(1024, 256), 0, core, 2)
    v, comings[2], final = tie((v, comings[2], lowers[4]))
    comings.append(shifted(final, "scan", 1, "grad_4"))
    v, _ = halved_sum(v, 1, y, 4)
    v, comings[3], over_lower = tie((v, comings[3], over_lower))
    slant = shifted_both(over_lower, "slant")
    v, _ = exchanged_sum(v, 2)
    sources = [(first, array) for (first, _), pair in zip(plan, zip(uppers, comings)) for array in pair]
    step = finish(range(2, 13), sources[:8], field.shape, None)
    v, comings[4], step, over_upper = tie((v, comings[4], step, over_upper))
    over = shifted(over_upper, "mode", 1, "over")
    v, _ = exchanged_sum(v, 3)
    slots_all = lax.axis_size("scan") * lax.axis_size("mode") * SLOTS
    v = v * (1.0 / math.sqrt(slots_all))
    v, slant = tie((v, slant))
    v = gathered(v, 1, y, 4)
    probe_step = gathered(v, 0, core, 2).reshape(probe.shape)
    sources = sources[:2] + [(13, uppers[4]), (13, comings[4]), (0, over), (0, slant)]
    step = finish([0, 1, 13, 14, 15], sources, field.shape, step)
    return (step, probe_step)


def solution(mesh):
    in_specs = (
        P(None, "scan", "mode"),
        P(),
        P(AXES, None, None),
        P(AXES, None),
        P(AXES),
    )
    out_specs = (P(None, "scan", "mode"), P())
    return jax.shard_map(shards, mesh=mesh, in_specs=in_specs, out_specs=out_specs, check_vma=False)
```

```python
import functools
import math

import jax
import jax.numpy as jnp
import ml_dtypes
import numpy as np
from jax import lax
from jax.experimental import pallas as pl
from jax.experimental.pallas import tpu as pltpu
from jax.sharding import PartitionSpec as P

SLOTS = 16
SIZE = 256
LANE = 128
CHUNK = 256
FLOOR = 0.5
AXES = ("scan", "mode")
f32 = jnp.float32
bf16 = jnp.bfloat16


def tables():
    n = SIZE
    place = np.arange(n)
    angles = (place[:, None] * place[None, :] % n) * (2.0 * math.pi / n)
    c = np.cos(angles) / math.sqrt(n)
    s = np.sin(angles) / math.sqrt(n)
    rows = np.concatenate([place[0 : n // 2 : 2], place[1 : n // 2 : 2]])

    def block(c, s):
        return np.block([[c, s], [-s, c]])

    def halves(c, s):
        return np.stack([block(c[rows, p::2], s[rows, p::2]) for p in (0, 1)])

    both = (halves(c, s), block(c, -s), halves(c, -s), block(c, s))
    return [t.astype(ml_dtypes.bfloat16) for t in both]


def stack(parts, axis):
    return jnp.concatenate(parts, axis)


def left_product(table, even, odd):
    dot = functools.partial(jnp.dot, preferred_element_type=f32)
    a = dot(table[0], even)
    b = dot(table[1], odd)
    return (a + b).astype(bf16), (a - b).astype(bf16)


def pattern(ext, grad, acc, probe, frame, tabs, r, c):
    left_fwd, right_fwd, left_bwd, right_bwd = tabs
    n = SIZE
    half, quarter = n // 2, n // 4
    block = c // LANE
    shift = c % LANE
    dot = functools.partial(jnp.dot, preferred_element_type=f32)

    def window(part):
        cols = []
        for j in range(3):
            view = ext.at[part, block + j]
            cols.append(stack([view[pl.ds(r + p, half, stride=2), :] for p in (0, 1)], 0))
        return pltpu.roll(stack(cols, 1), 3 * LANE - shift, 1)[:, :n]

    wr = window(0)
    wi = window(1)
    x_re = [probe[k, 0] * wr - probe[k, 1] * wi for k in (0, 1)]
    x_im = [probe[k, 0] * wi + probe[k, 1] * wr for k in (0, 1)]

    def rows_of(p):
        rows = slice(half * p, half * (p + 1))
        return stack([stack([x_re[k][rows], x_im[k][rows]], 0) for k in (0, 1)], 1).astype(bf16)

    sums = left_product(left_fwd, rows_of(0), rows_of(1))
    h = stack(
        [
            stack([t[:half, n * k : n * (k + 1)], t[half:, n * k : n * (k + 1)]], 1)
            for k in (0, 1)
            for t in sums
        ],
        0,
    )
    far = dot(h, right_fwd[...])
    sq = far * far
    intensity = (sq[:n, :n] + sq[:n, n:]) + (sq[n:, :n] + sq[n:, n:])
    amplitude = stack(
        [
            stack([frame.at[b][pl.ds(row, quarter, stride=2), :] for b in (0, 1)], 1)
            for row in (0, 1, half, half + 1)
        ],
        0,
    )
    factor = amplitude * lax.rsqrt(jnp.maximum(intensity, FLOOR)) - 1.0
    change = [
        [(far[n * k : n * (k + 1), n * p : n * (p + 1)] * factor).astype(bf16) for p in (0, 1)]
        for k in (0, 1)
    ]

    def quarters(q):
        return stack(
            [
                stack([change[k][p][at : at + quarter] for p in (0, 1) for at in (q, q + half)], 0)
                for k in (0, 1)
            ],
            1,
        )

    plus, minus = left_product(left_bwd, quarters(0), quarters(quarter))
    h = stack(
        [
            stack(
                [
                    t[at : at + quarter, n * k : n * (k + 1)],
                    t[half + at : half + at + quarter, n * k : n * (k + 1)],
                ],
                1,
            )
            for k in (0, 1)
            for t, at in ((plus, 0), (minus, 0), (plus, quarter), (minus, quarter))
        ],
        0,
    )
    delta = dot(h, right_bwd[...])
    terms = [None, None]
    for k in (0, 1):
        d_re = delta[n * k : n * k + n, :n]
        d_im = delta[n * k : n * k + n, n:]
        new = (
            probe[k, 0] * d_re + probe[k, 1] * d_im,
            probe[k, 0] * d_im - probe[k, 1] * d_re,
        )
        terms = [b if a is None else a + b for a, b in zip(terms, new)]
        acc[k, 0] += wr * d_re + wi * d_im
        acc[k, 1] += wr * d_im - wi * d_re
    blank = jnp.zeros((n, LANE), f32)
    for part, term in enumerate(terms):
        moved = pltpu.roll(stack([term, blank], 1), shift, 1)
        for j in range(3):
            view = grad.at[part, block + j]
            for p in (0, 1):
                rows = pl.ds(r + p, half, stride=2)
                view[rows, :] = view[rows, :] + moved[half * p : half * (p + 1), LANE * j : LANE * (j + 1)]


def group_kernel(first, count, homes, n_after, last, live, off, *refs):
    wide = count + 2
    refs = list(refs)
    sources = refs[: len(homes[2])]
    refs = refs[len(homes[2]) + n_after :]
    measured, probe, t0, t1, t2, t3, carry, acc_in = refs[:8]
    if last:
        upper, lower, over_upper, over_lower, acc = refs[8:13]
    else:
        upper, lower, carry_out, acc = refs[8:12]
    ext, grad, frame, picked, load_sem, frame_sem = refs[-6:]

    def pick(q, n):
        b = off[q, 1] // LANE - first
        picked[n] = q
        return n + jnp.where((b >= 0) & (b < count), 1, 0)

    n = lax.fori_loop(0, live[0], pick, jnp.int32(0))

    def loads():
        out = []
        for half in (0, 1):
            for b in range(wide):
                which, row, at = homes[half][b]
                src = sources[which].at[:, row : row + SIZE, at : at + LANE]
                dst = ext.at[:, b, SIZE * half : SIZE * (half + 1), :]
                out.append(pltpu.make_async_copy(src, dst, load_sem.at[2 * b + half]))
        return out

    def frame_copies(i):
        slot = i % 2
        return [
            pltpu.make_async_copy(
                measured.at[picked[i], :, LANE * b : LANE * (b + 1)],
                frame.at[slot, b],
                frame_sem.at[2 * slot + b],
            )
            for b in (0, 1)
        ]

    @pl.when(n > 0)
    def _():
        for copy in loads():
            copy.start()
        for copy in frame_copies(0):
            copy.start()

    grad[:, 0:2] = carry[...]
    grad[:, 2:] = jnp.zeros((2, count, 2 * SIZE, LANE), f32)
    acc[...] = acc_in[...]

    @pl.when(n > 0)
    def _():
        for copy in loads():
            copy.wait()

    def step(i, _):
        @pl.when(i + 1 < n)
        def _():
            for copy in frame_copies(i + 1):
                copy.start()

        for copy in frame_copies(i):
            copy.wait()
        q = picked[i]
        pattern(
            ext, grad, acc, probe, frame.at[i % 2], (t0, t1, t2, t3), off[q, 0], off[q, 1] - first * LANE
        )
        return 0

    lax.fori_loop(0, n, step, 0)
    upper[...] = grad[:, 0:count, :SIZE]
    lower[...] = grad[:, 0:count, SIZE:]
    if not last:
        carry_out[...] = grad[:, count:]
    if last:
        over_upper[...] = grad[:, count:, :SIZE]
        over_lower[...] = grad[:, count:, SIZE:]
        for k in (0, 1):
            for part in (0, 1):
                for b in (0, 1):
                    view = ext.at[part, 2 * k + b]
                    at = slice(LANE * b, LANE * (b + 1))
                    for p in (0, 1):
                        rows = pl.ds(p, SIZE // 2, stride=2)
                        view[rows, :] = acc[k, part, LANE * p : LANE * (p + 1), at]
                    acc[k, part, :, at] = view[0:SIZE, :]


IN_HBM = pl.BlockSpec(memory_space=pltpu.HBM)
IN_SMEM = pl.BlockSpec(memory_space=pltpu.SMEM)
IN_VMEM = pl.BlockSpec(memory_space=pltpu.VMEM)


def run_group(first, count, bounds, live, off, field, halos, corner, measured, probe, tabs, carry, acc, after):
    wide = count + 2
    arrays, homes = [], [[], []]

    def index_in(array):
        for i, other in enumerate(arrays):
            if other is array:
                return i
        arrays.append(array)
        return len(arrays) - 1

    for b in range(first, first + wide):
        if b < bounds[-1]:
            chunk = next(i for i, end in enumerate(bounds) if b < end)
            begin = bounds[chunk - 1] if chunk else 0
            homes[0].append((index_in(field), 0, b * LANE))
            homes[1].append((index_in(halos[chunk]), 0, (b - begin) * LANE))
        else:
            at = (b - bounds[-1]) * LANE
            homes[0].append((index_in(corner), 0, at))
            homes[1].append((index_in(corner), SIZE, at))
    homes.append(arrays)
    args = [live, off, *arrays, *after, measured, probe, *tabs, carry, acc]
    specs = [IN_SMEM] * 2 + [IN_HBM] * (1 + len(arrays) + len(after)) + [IN_VMEM] * 7
    part = jax.ShapeDtypeStruct((2, count, SIZE, LANE), f32)
    last = first + count == bounds[-1]
    whole = jax.ShapeDtypeStruct((2, 2, 2 * SIZE, LANE), f32)
    edge = jax.ShapeDtypeStruct((2, 2, SIZE, LANE), f32)
    out_shape = (part, part) + ((edge, edge) if last else (whole,))
    out_shape += (jax.ShapeDtypeStruct((2, 2, SIZE, SIZE), f32),)
    return pl.pallas_call(
        functools.partial(group_kernel, first, count, (homes[0], homes[1], [None] * len(arrays)),
            len(after), last),
        out_shape=out_shape,
        in_specs=specs,
        out_specs=(IN_VMEM,) * len(out_shape),
        scratch_shapes=[
            pltpu.VMEM((2, wide, 2 * SIZE, LANE), f32),
            pltpu.VMEM((2, wide, 2 * SIZE, LANE), f32),
            pltpu.VMEM((2, 2, SIZE, LANE), f32),
            pltpu.SMEM((SLOTS + 1,), jnp.int32),
            pltpu.SemaphoreType.DMA((2 * wide,)),
            pltpu.SemaphoreType.DMA((4,)),
        ],
        compiler_params=pltpu.CompilerParams(vmem_limit_bytes=44 * 2**20),
        cost_estimate=pl.CostEstimate(flops=2**33, bytes_accessed=2**12, transcendentals=0),
        name=f"group_{first}",
    )(*args)


def finish_kernel(blocks, terms, *refs):
    out, buf, sem = refs[-3:]
    copies = []
    for at, (block, many) in enumerate(zip(blocks, terms)):
        value = None
        for which, b in many:
            term = refs[which][:, b, :SIZE]
            value = term if value is None else value + term
        buf[at] = value
        copy = pltpu.make_async_copy(
            buf.at[at], out.at[:, :, block * LANE : (block + 1) * LANE], sem.at[at]
        )
        copy.start()
        copies.append(copy)
    for copy in copies:
        copy.wait()


def finish(blocks, sources, shape, onto):
    args = [array for _, array in sources]
    terms = tuple(
        tuple(
            (i, block - first)
            for i, (first, array) in enumerate(sources)
            if first <= block < first + array.shape[1]
        )
        for block in blocks
    )
    specs = [IN_VMEM] * len(args)
    aliases = {}
    if onto is not None:
        aliases = {len(args): 0}
        args.append(onto)
        specs.append(IN_HBM)
    return pl.pallas_call(
        functools.partial(finish_kernel, tuple(blocks), terms),
        out_shape=jax.ShapeDtypeStruct(shape, f32),
        in_specs=specs,
        out_specs=IN_HBM,
        scratch_shapes=[
            pltpu.VMEM((len(blocks), 2, SIZE, LANE), f32),
            pltpu.SemaphoreType.DMA((len(blocks),)),
        ],
        input_output_aliases=aliases,
        compiler_params=pltpu.CompilerParams(vmem_limit_bytes=24 * 2**20),
        name=f"finish_{blocks[0]}",
    )(*args)


def shifted(array, axis, by, name):
    count = lax.axis_size(axis)
    pairs = [(i, i + by) for i in range(count) if 0 <= i + by < count]
    with jax.named_scope(name):
        return lax.ppermute(array, axis, pairs)


def shifted_both(array, name):
    rows, cols = (lax.axis_size(a) for a in AXES)
    pairs = [
        (i * cols + j, (i + 1) * cols + j + 1) for i in range(rows - 1) for j in range(cols - 1)
    ]
    with jax.named_scope(name):
        return lax.ppermute(array, AXES, pairs)


def place_of(index):
    s, m = divmod(index, 4)
    return [m % 2, (s // 16) * 2 + m // 2, (s // 4) % 4, s % 4]


def index_of(place):
    core, y, z, x = place
    return ((y // 2) * 16 + z * 4 + x) * 4 + (y % 2) * 2 + core


def swapped(array, axis, bits):
    pairs = []
    for i in range(128):
        place = place_of(i)
        place[axis] ^= bits
        pairs.append((i, index_of(place)))
    with jax.named_scope("swap_" + "cyzx"[axis] + str(bits)):
        return lax.ppermute(array, AXES, pairs)


def halved_sum(v, axis, here, pieces, held=None):
    v = v.reshape(pieces, -1, v.shape[-1])
    pick = functools.partial(lax.dynamic_index_in_dim, axis=0, keepdims=False)
    got = [swapped(pick(v, here ^ k), axis, k) for k in range(1, pieces)]
    if pieces == 2:
        return pick(v, here) + got[0], held
    if held is not None:
        got[0], held = lax.optimization_barrier((got[0], held))
    return (pick(v, here) + got[0]) + (got[1] + got[2]), held


def exchanged_sum(v, axis, held=None):
    a, b, c = [swapped(v, axis, k) for k in (1, 2, 3)]
    if held is not None:
        a, held = lax.optimization_barrier((a, held))
    return (v + a) + (b + c), held


def gathered(v, axis, here, pieces):
    parts = [v] + [swapped(v, axis, k) for k in range(1, pieces)]

    def part_of(i):
        which = here ^ i
        if pieces == 2:
            return jnp.where(which == 0, parts[0], parts[1])
        return jnp.where(
            which < 2,
            jnp.where(which == 0, parts[0], parts[1]),
            jnp.where(which == 2, parts[2], parts[3]),
        )

    return jnp.concatenate([part_of(i) for i in range(pieces)], 0)


BOUNDS = (5, 9, 13, 15, 16)


def shards(field, probe, measured, offsets, live):
    rows, cols = field.shape[1:]
    base = jnp.stack([lax.axis_index("scan") * rows, lax.axis_index("mode") * cols])
    off = offsets - base[None, :]
    tabs = [jnp.asarray(t) for t in tables()]
    probe_rows = probe.reshape(2, 2, 128, 2, 256).transpose(0, 1, 3, 2, 4).reshape(probe.shape)
    tie = lax.optimization_barrier
    head, rest = tie((field[:, :, : LANE * BOUNDS[0]], field))
    halos = [shifted(head, "scan", -1, "halo_0")]
    for i, (a, b) in enumerate(zip(BOUNDS[:-1], BOUNDS[1:])):
        part = rest[:, :, LANE * a : LANE * b]
        if i == 1:
            part, halos[0] = tie((part, halos[0]))
        halos.append(shifted(part, "scan", -1, f"halo_{i + 1}"))
    beside = jnp.concatenate([field[:, :, :SIZE], halos[0][:, :, :SIZE]], 1)
    corner = shifted(beside, "mode", -1, "corner")
    carry = jnp.zeros((2, 2, 2 * SIZE, LANE), f32)
    acc = jnp.zeros(probe.shape, f32)
    ends = [b - 2 for b in BOUNDS[:-1]] + [BOUNDS[-1]]
    plan = [(a, b - a) for a, b in zip([0] + ends[:-1], ends)]
    uppers, lowers, comings = [], [], []
    for i, (first, count) in enumerate(plan):
        after = {2: (0,), 3: (1, corner)}.get(i, ())
        after = [comings[j] if isinstance(j, int) else j for j in after]
        upper, lower, *rest, acc = run_group(
            first, count, BOUNDS, live, off, field, halos, corner, measured, probe_rows, tabs, carry, acc, after
        )
        uppers.append(upper)
        lowers.append(lower)
        if i + 1 < len(plan):
            carry = rest[0]
        if i < len(plan) - 2:
            comings.append(shifted(lower, "scan", 1, f"grad_{i}"))
    over_upper, over_lower = rest
    s, m = lax.axis_index("scan"), lax.axis_index("mode")
    core, y = m % 2, (s // 16) * 2 + m // 2
    v, _ = halved_sum(acc.reshape(1024, 256), 0, core, 2)
    v, comings[2], later = tie((v, comings[2], lowers[3]))
    comings.append(shifted(later, "scan", 1, "grad_3"))
    v, _ = halved_sum(v, 1, y, 4)
    v, comings[3], final = tie((v, comings[3], lowers[4]))
    comings.append(shifted(final, "scan", 1, "grad_4"))
    v, _ = exchanged_sum(v, 2)
    v, _ = exchanged_sum(v, 3)
    slots_all = lax.axis_size("scan") * lax.axis_size("mode") * SLOTS
    v = v * (1.0 / math.sqrt(slots_all))
    v, comings[4], over_lower, over_upper = tie((v, comings[4], over_lower, over_upper))
    slant = shifted_both(over_lower, "slant")
    sources = [(first, array) for (first, _), pair in zip(plan, zip(uppers, comings)) for array in pair]
    step = finish(range(2, 13), sources[:8], field.shape, None)
    v = gathered(v, 1, y, 4)
    v, step, slant = tie((v, step, slant))
    over = shifted(over_upper, "mode", 1, "over")
    probe_step = gathered(v, 0, core, 2).reshape(probe.shape)
    sources = sources[:2] + [(13, uppers[4]), (13, comings[4]), (0, over), (0, slant)]
    step = finish([0, 1, 13, 14, 15], sources, field.shape, step)
    return (step, probe_step)


def solution(mesh):
    in_specs = (
        P(None, "scan", "mode"),
        P(),
        P(AXES, None, None),
        P(AXES, None),
        P(AXES),
    )
    out_specs = (P(None, "scan", "mode"), P())
    return jax.shard_map(shards, mesh=mesh, in_specs=in_specs, out_specs=out_specs, check_vma=False)
```

```python
import functools
import math

import jax
import jax.numpy as jnp
import ml_dtypes
import numpy as np
from jax import lax
from jax.experimental import pallas as pl
from jax.experimental.pallas import tpu as pltpu
from jax.sharding import PartitionSpec as P

SLOTS = 16
SIZE = 256
LANE = 128
CHUNK = 256
FLOOR = 0.5
AXES = ("scan", "mode")
f32 = jnp.float32
bf16 = jnp.bfloat16


def tables():
    n = SIZE
    place = np.arange(n)
    angles = (place[:, None] * place[None, :] % n) * (2.0 * math.pi / n)
    c = np.cos(angles) / math.sqrt(n)
    s = np.sin(angles) / math.sqrt(n)
    rows = np.concatenate([place[0 : n // 2 : 2], place[1 : n // 2 : 2]])

    def block(c, s):
        return np.block([[c, s], [-s, c]])

    def halves(c, s):
        return np.stack([block(c[rows, p::2], s[rows, p::2]) for p in (0, 1)])

    both = (halves(c, s), block(c, -s), halves(c, -s), block(c, s))
    return [t.astype(ml_dtypes.bfloat16) for t in both]


def stack(parts, axis):
    return jnp.concatenate(parts, axis)


def left_product(table, even, odd):
    dot = functools.partial(jnp.dot, preferred_element_type=f32)
    a = dot(table[0], even)
    b = dot(table[1], odd)
    return (a + b).astype(bf16), (a - b).astype(bf16)


def pattern(ext, grad, acc, probe, frame, tabs, r, c):
    left_fwd, right_fwd, left_bwd, right_bwd = tabs
    n = SIZE
    half, quarter = n // 2, n // 4
    block = c // LANE
    shift = c % LANE
    dot = functools.partial(jnp.dot, preferred_element_type=f32)

    def window(part):
        cols = []
        for j in range(3):
            view = ext.at[part, block + j]
            cols.append(stack([view[pl.ds(r + p, half, stride=2), :] for p in (0, 1)], 0))
        return pltpu.roll(stack(cols, 1), 3 * LANE - shift, 1)[:, :n]

    wr = window(0)
    wi = window(1)
    x_re = [probe[k, 0] * wr - probe[k, 1] * wi for k in (0, 1)]
    x_im = [probe[k, 0] * wi + probe[k, 1] * wr for k in (0, 1)]

    def rows_of(p):
        rows = slice(half * p, half * (p + 1))
        return stack([stack([x_re[k][rows], x_im[k][rows]], 0) for k in (0, 1)], 1).astype(bf16)

    sums = left_product(left_fwd, rows_of(0), rows_of(1))
    h = stack(
        [
            stack([t[:half, n * k : n * (k + 1)], t[half:, n * k : n * (k + 1)]], 1)
            for k in (0, 1)
            for t in sums
        ],
        0,
    )
    far = dot(h, right_fwd[...])
    sq = far * far
    intensity = (sq[:n, :n] + sq[:n, n:]) + (sq[n:, :n] + sq[n:, n:])
    amplitude = stack(
        [
            stack([frame.at[b][pl.ds(row, quarter, stride=2), :] for b in (0, 1)], 1)
            for row in (0, 1, half, half + 1)
        ],
        0,
    )
    factor = amplitude * lax.rsqrt(jnp.maximum(intensity, FLOOR)) - 1.0
    change = [
        [(far[n * k : n * (k + 1), n * p : n * (p + 1)] * factor).astype(bf16) for p in (0, 1)]
        for k in (0, 1)
    ]

    def quarters(q):
        return stack(
            [
                stack([change[k][p][at : at + quarter] for p in (0, 1) for at in (q, q + half)], 0)
                for k in (0, 1)
            ],
            1,
        )

    plus, minus = left_product(left_bwd, quarters(0), quarters(quarter))
    h = stack(
        [
            stack(
                [
                    t[at : at + quarter, n * k : n * (k + 1)],
                    t[half + at : half + at + quarter, n * k : n * (k + 1)],
                ],
                1,
            )
            for k in (0, 1)
            for t, at in ((plus, 0), (minus, 0), (plus, quarter), (minus, quarter))
        ],
        0,
    )
    delta = dot(h, right_bwd[...])
    terms = [None, None]
    for k in (0, 1):
        d_re = delta[n * k : n * k + n, :n]
        d_im = delta[n * k : n * k + n, n:]
        new = (
            probe[k, 0] * d_re + probe[k, 1] * d_im,
            probe[k, 0] * d_im - probe[k, 1] * d_re,
        )
        terms = [b if a is None else a + b for a, b in zip(terms, new)]
        acc[k, 0] += wr * d_re + wi * d_im
        acc[k, 1] += wr * d_im - wi * d_re
    blank = jnp.zeros((n, LANE), f32)
    for part, term in enumerate(terms):
        moved = pltpu.roll(stack([term, blank], 1), shift, 1)
        for j in range(3):
            view = grad.at[part, block + j]
            for p in (0, 1):
                rows = pl.ds(r + p, half, stride=2)
                view[rows, :] = view[rows, :] + moved[half * p : half * (p + 1), LANE * j : LANE * (j + 1)]


def group_kernel(first, count, homes, n_after, last, live, off, *refs):
    wide = count + 2
    refs = list(refs)
    sources = refs[: len(homes[2])]
    refs = refs[len(homes[2]) + n_after :]
    measured, probe, t0, t1, t2, t3, carry, acc_in = refs[:8]
    if last:
        upper, lower, over_upper, over_lower, acc = refs[8:13]
    else:
        upper, lower, carry_out, acc = refs[8:12]
    ext, grad, frame, picked, load_sem, frame_sem = refs[-6:]

    def pick(q, n):
        b = off[q, 1] // LANE - first
        picked[n] = q
        return n + jnp.where((b >= 0) & (b < count), 1, 0)

    n = lax.fori_loop(0, live[0], pick, jnp.int32(0))

    def loads():
        out = []
        for half in (0, 1):
            for b in range(wide):
                which, row, at = homes[half][b]
                src = sources[which].at[:, row : row + SIZE, at : at + LANE]
                dst = ext.at[:, b, SIZE * half : SIZE * (half + 1), :]
                out.append(pltpu.make_async_copy(src, dst, load_sem.at[2 * b + half]))
        return out

    def frame_copies(i):
        slot = i % 2
        return [
            pltpu.make_async_copy(
                measured.at[picked[i], :, LANE * b : LANE * (b + 1)],
                frame.at[slot, b],
                frame_sem.at[2 * slot + b],
            )
            for b in (0, 1)
        ]

    @pl.when(n > 0)
    def _():
        for copy in loads():
            copy.start()
        for copy in frame_copies(0):
            copy.start()

    grad[:, 0:2] = carry[...]
    grad[:, 2:] = jnp.zeros((2, count, 2 * SIZE, LANE), f32)
    acc[...] = acc_in[...]

    @pl.when(n > 0)
    def _():
        for copy in loads():
            copy.wait()

    def step(i, _):
        @pl.when(i + 1 < n)
        def _():
            for copy in frame_copies(i + 1):
                copy.start()

        for copy in frame_copies(i):
            copy.wait()
        q = picked[i]
        pattern(
            ext, grad, acc, probe, frame.at[i % 2], (t0, t1, t2, t3), off[q, 0], off[q, 1] - first * LANE
        )
        return 0

    lax.fori_loop(0, n, step, 0)
    upper[...] = grad[:, 0:count, :SIZE]
    lower[...] = grad[:, 0:count, SIZE:]
    if not last:
        carry_out[...] = grad[:, count:]
    if last:
        over_upper[...] = grad[:, count:, :SIZE]
        over_lower[...] = grad[:, count:, SIZE:]
        for k in (0, 1):
            for part in (0, 1):
                for b in (0, 1):
                    view = ext.at[part, 2 * k + b]
                    at = slice(LANE * b, LANE * (b + 1))
                    for p in (0, 1):
                        rows = pl.ds(p, SIZE // 2, stride=2)
                        view[rows, :] = acc[k, part, LANE * p : LANE * (p + 1), at]
                    acc[k, part, :, at] = view[0:SIZE, :]


IN_HBM = pl.BlockSpec(memory_space=pltpu.HBM)
IN_SMEM = pl.BlockSpec(memory_space=pltpu.SMEM)
IN_VMEM = pl.BlockSpec(memory_space=pltpu.VMEM)


def run_group(first, count, bounds, live, off, field, halos, corner, measured, probe, tabs, carry, acc, after):
    wide = count + 2
    arrays, homes = [], [[], []]

    def index_in(array):
        for i, other in enumerate(arrays):
            if other is array:
                return i
        arrays.append(array)
        return len(arrays) - 1

    for b in range(first, first + wide):
        if b < bounds[-1]:
            chunk = next(i for i, end in enumerate(bounds) if b < end)
            begin = bounds[chunk - 1] if chunk else 0
            homes[0].append((index_in(field), 0, b * LANE))
            homes[1].append((index_in(halos[chunk]), 0, (b - begin) * LANE))
        else:
            at = (b - bounds[-1]) * LANE
            homes[0].append((index_in(corner), 0, at))
            homes[1].append((index_in(corner), SIZE, at))
    homes.append(arrays)
    args = [live, off, *arrays, *after, measured, probe, *tabs, carry, acc]
    specs = [IN_SMEM] * 2 + [IN_HBM] * (1 + len(arrays) + len(after)) + [IN_VMEM] * 7
    part = jax.ShapeDtypeStruct((2, count, SIZE, LANE), f32)
    last = first + count == bounds[-1]
    whole = jax.ShapeDtypeStruct((2, 2, 2 * SIZE, LANE), f32)
    edge = jax.ShapeDtypeStruct((2, 2, SIZE, LANE), f32)
    out_shape = (part, part) + ((edge, edge) if last else (whole,))
    out_shape += (jax.ShapeDtypeStruct((2, 2, SIZE, SIZE), f32),)
    return pl.pallas_call(
        functools.partial(group_kernel, first, count, (homes[0], homes[1], [None] * len(arrays)),
            len(after), last),
        out_shape=out_shape,
        in_specs=specs,
        out_specs=(IN_VMEM,) * len(out_shape),
        scratch_shapes=[
            pltpu.VMEM((2, wide, 2 * SIZE, LANE), f32),
            pltpu.VMEM((2, wide, 2 * SIZE, LANE), f32),
            pltpu.VMEM((2, 2, SIZE, LANE), f32),
            pltpu.SMEM((SLOTS + 1,), jnp.int32),
            pltpu.SemaphoreType.DMA((2 * wide,)),
            pltpu.SemaphoreType.DMA((4,)),
        ],
        compiler_params=pltpu.CompilerParams(vmem_limit_bytes=44 * 2**20),
        cost_estimate=pl.CostEstimate(flops=2**33, bytes_accessed=2**12, transcendentals=0),
        name=f"group_{first}",
    )(*args)


def finish_kernel(blocks, terms, *refs):
    out, buf, sem = refs[-3:]
    copies = []
    for at, (block, many) in enumerate(zip(blocks, terms)):
        value = None
        for which, b in many:
            term = refs[which][:, b, :SIZE]
            value = term if value is None else value + term
        buf[at] = value
        copy = pltpu.make_async_copy(
            buf.at[at], out.at[:, :, block * LANE : (block + 1) * LANE], sem.at[at]
        )
        copy.start()
        copies.append(copy)
    for copy in copies:
        copy.wait()


def finish(blocks, sources, shape, onto):
    args = [array for _, array in sources]
    terms = tuple(
        tuple(
            (i, block - first)
            for i, (first, array) in enumerate(sources)
            if first <= block < first + array.shape[1]
        )
        for block in blocks
    )
    specs = [IN_VMEM] * len(args)
    aliases = {}
    if onto is not None:
        aliases = {len(args): 0}
        args.append(onto)
        specs.append(IN_HBM)
    return pl.pallas_call(
        functools.partial(finish_kernel, tuple(blocks), terms),
        out_shape=jax.ShapeDtypeStruct(shape, f32),
        in_specs=specs,
        out_specs=IN_HBM,
        scratch_shapes=[
            pltpu.VMEM((len(blocks), 2, SIZE, LANE), f32),
            pltpu.SemaphoreType.DMA((len(blocks),)),
        ],
        input_output_aliases=aliases,
        compiler_params=pltpu.CompilerParams(vmem_limit_bytes=24 * 2**20),
        name=f"finish_{blocks[0]}",
    )(*args)


def shifted(array, axis, by, name):
    count = lax.axis_size(axis)
    pairs = [(i, i + by) for i in range(count) if 0 <= i + by < count]
    with jax.named_scope(name):
        return lax.ppermute(array, axis, pairs)


def shifted_both(array, name):
    rows, cols = (lax.axis_size(a) for a in AXES)
    pairs = [
        (i * cols + j, (i + 1) * cols + j + 1) for i in range(rows - 1) for j in range(cols - 1)
    ]
    with jax.named_scope(name):
        return lax.ppermute(array, AXES, pairs)


def place_of(index):
    s, m = divmod(index, 4)
    return [m % 2, (s // 16) * 2 + m // 2, (s // 4) % 4, s % 4]


def index_of(place):
    core, y, z, x = place
    return ((y // 2) * 16 + z * 4 + x) * 4 + (y % 2) * 2 + core


def swapped(array, axis, bits):
    pairs = []
    for i in range(128):
        place = place_of(i)
        place[axis] ^= bits
        pairs.append((i, index_of(place)))
    with jax.named_scope("swap_" + "cyzx"[axis] + str(bits)):
        return lax.ppermute(array, AXES, pairs)


def halved_sum(v, axis, here, pieces, held=None):
    v = v.reshape(pieces, -1, v.shape[-1])
    pick = functools.partial(lax.dynamic_index_in_dim, axis=0, keepdims=False)
    got = [swapped(pick(v, here ^ k), axis, k) for k in range(1, pieces)]
    if pieces == 2:
        return pick(v, here) + got[0], held
    if held is not None:
        got[0], held = lax.optimization_barrier((got[0], held))
    return (pick(v, here) + got[0]) + (got[1] + got[2]), held


def exchanged_sum(v, axis, held=None):
    a, b, c = [swapped(v, axis, k) for k in (1, 2, 3)]
    if held is not None:
        a, held = lax.optimization_barrier((a, held))
    return (v + a) + (b + c), held


def gathered(v, axis, here, pieces):
    parts = [v] + [swapped(v, axis, k) for k in range(1, pieces)]

    def part_of(i):
        which = here ^ i
        if pieces == 2:
            return jnp.where(which == 0, parts[0], parts[1])
        return jnp.where(
            which < 2,
            jnp.where(which == 0, parts[0], parts[1]),
            jnp.where(which == 2, parts[2], parts[3]),
        )

    return jnp.concatenate([part_of(i) for i in range(pieces)], 0)


BOUNDS = (5, 9, 13, 15, 16)


def shards(field, probe, measured, offsets, live):
    rows, cols = field.shape[1:]
    base = jnp.stack([lax.axis_index("scan") * rows, lax.axis_index("mode") * cols])
    off = offsets - base[None, :]
    tabs = [jnp.asarray(t) for t in tables()]
    probe_rows = probe.reshape(2, 2, 128, 2, 256).transpose(0, 1, 3, 2, 4).reshape(probe.shape)
    tie = lax.optimization_barrier
    head, rest = tie((field[:, :, : LANE * BOUNDS[0]], field))
    halos = [shifted(head, "scan", -1, "halo_0")]
    for i, (a, b) in enumerate(zip(BOUNDS[:-1], BOUNDS[1:])):
        part = rest[:, :, LANE * a : LANE * b]
        if i == 1:
            part, halos[0] = tie((part, halos[0]))
        halos.append(shifted(part, "scan", -1, f"halo_{i + 1}"))
    beside = jnp.concatenate([field[:, :, :SIZE], halos[0][:, :, :SIZE]], 1)
    corner = shifted(beside, "mode", -1, "corner")
    carry = jnp.zeros((2, 2, 2 * SIZE, LANE), f32)
    acc = jnp.zeros(probe.shape, f32)
    ends = [b - 2 for b in BOUNDS[:-1]] + [BOUNDS[-1]]
    plan = [(a, b - a) for a, b in zip([0] + ends[:-1], ends)]
    uppers, lowers, comings = [], [], []
    for i, (first, count) in enumerate(plan):
        after = {2: (0,), 3: (1, corner)}.get(i, ())
        after = [comings[j] if isinstance(j, int) else j for j in after]
        upper, lower, *rest, acc = run_group(
            first, count, BOUNDS, live, off, field, halos, corner, measured, probe_rows, tabs, carry, acc, after
        )
        uppers.append(upper)
        lowers.append(lower)
        if i + 1 < len(plan):
            carry = rest[0]
            comings.append(shifted(lower, "scan", 1, f"grad_{i}"))
    over_upper, over_lower = rest
    s, m = lax.axis_index("scan"), lax.axis_index("mode")
    core, y = m % 2, (s // 16) * 2 + m // 2
    v, _ = halved_sum(acc.reshape(1024, 256), 0, core, 2)
    v, comings[2] = tie((v, comings[2]))
    v, _ = halved_sum(v, 1, y, 4)
    v, comings[3], final, over_lower = tie((v, comings[3], lowers[4], over_lower))
    comings.append(shifted(final, "scan", 1, "grad_4"))
    slant = shifted_both(over_lower, "slant")
    v, _ = exchanged_sum(v, 2)
    v, _ = exchanged_sum(v, 3)
    slots_all = lax.axis_size("scan") * lax.axis_size("mode") * SLOTS
    v = v * (1.0 / math.sqrt(slots_all))
    v, slant, comings[4], over_upper = tie((v, slant, comings[4], over_upper))
    over = shifted(over_upper, "mode", 1, "over")
    sources = [(first, array) for (first, _), pair in zip(plan, zip(uppers, comings)) for array in pair]
    step = finish(range(2, 13), sources[:8], field.shape, None)
    v = gathered(v, 1, y, 4)
    v, step = tie((v, step))
    probe_step = gathered(v, 0, core, 2).reshape(probe.shape)
    sources = sources[:2] + [(13, uppers[4]), (13, comings[4]), (0, over), (0, slant)]
    step = finish([0, 1, 13, 14, 15], sources, field.shape, step)
    return (step, probe_step)


def solution(mesh):
    in_specs = (
        P(None, "scan", "mode"),
        P(),
        P(AXES, None, None),
        P(AXES, None),
        P(AXES),
    )
    out_specs = (P(None, "scan", "mode"), P())
    return jax.shard_map(shards, mesh=mesh, in_specs=in_specs, out_specs=out_specs, check_vma=False)
```

```python
import functools
import math

import jax
import jax.numpy as jnp
import ml_dtypes
import numpy as np
from jax import lax
from jax.experimental import pallas as pl
from jax.experimental.pallas import tpu as pltpu
from jax.sharding import PartitionSpec as P

SLOTS = 16
SIZE = 256
LANE = 128
CHUNK = 256
FLOOR = 0.5
AXES = ("scan", "mode")
f32 = jnp.float32
bf16 = jnp.bfloat16


def tables():
    n = SIZE
    place = np.arange(n)
    angles = (place[:, None] * place[None, :] % n) * (2.0 * math.pi / n)
    c = np.cos(angles) / math.sqrt(n)
    s = np.sin(angles) / math.sqrt(n)
    rows = np.concatenate([place[0 : n // 2 : 2], place[1 : n // 2 : 2]])

    def block(c, s):
        return np.block([[c, s], [-s, c]])

    def halves(c, s):
        return np.stack([block(c[rows, p::2], s[rows, p::2]) for p in (0, 1)])

    both = (halves(c, s), block(c, -s), halves(c, -s), block(c, s))
    return [t.astype(ml_dtypes.bfloat16) for t in both]


def stack(parts, axis):
    return jnp.concatenate(parts, axis)


def left_product(table, even, odd):
    dot = functools.partial(jnp.dot, preferred_element_type=f32)
    a = dot(table[0], even)
    b = dot(table[1], odd)
    return (a + b).astype(bf16), (a - b).astype(bf16)


def pattern(ext, grad, acc, probe, frame, tabs, r, c):
    left_fwd, right_fwd, left_bwd, right_bwd = tabs
    n = SIZE
    half, quarter = n // 2, n // 4
    block = c // LANE
    shift = c % LANE
    dot = functools.partial(jnp.dot, preferred_element_type=f32)

    def window(part):
        cols = []
        for j in range(3):
            view = ext.at[part, block + j]
            cols.append(stack([view[pl.ds(r + p, half, stride=2), :] for p in (0, 1)], 0))
        return pltpu.roll(stack(cols, 1), 3 * LANE - shift, 1)[:, :n]

    wr = window(0)
    wi = window(1)
    x_re = [probe[k, 0] * wr - probe[k, 1] * wi for k in (0, 1)]
    x_im = [probe[k, 0] * wi + probe[k, 1] * wr for k in (0, 1)]

    def rows_of(p):
        rows = slice(half * p, half * (p + 1))
        return stack([stack([x_re[k][rows], x_im[k][rows]], 0) for k in (0, 1)], 1).astype(bf16)

    sums = left_product(left_fwd, rows_of(0), rows_of(1))
    h = stack(
        [
            stack([t[:half, n * k : n * (k + 1)], t[half:, n * k : n * (k + 1)]], 1)
            for k in (0, 1)
            for t in sums
        ],
        0,
    )
    far = dot(h, right_fwd[...])
    sq = far * far
    intensity = (sq[:n, :n] + sq[:n, n:]) + (sq[n:, :n] + sq[n:, n:])
    amplitude = stack(
        [
            stack([frame.at[b][pl.ds(row, quarter, stride=2), :] for b in (0, 1)], 1)
            for row in (0, 1, half, half + 1)
        ],
        0,
    )
    factor = amplitude * lax.rsqrt(jnp.maximum(intensity, FLOOR)) - 1.0
    change = [
        [(far[n * k : n * (k + 1), n * p : n * (p + 1)] * factor).astype(bf16) for p in (0, 1)]
        for k in (0, 1)
    ]

    def quarters(q):
        return stack(
            [
                stack([change[k][p][at : at + quarter] for p in (0, 1) for at in (q, q + half)], 0)
                for k in (0, 1)
            ],
            1,
        )

    plus, minus = left_product(left_bwd, quarters(0), quarters(quarter))
    h = stack(
        [
            stack(
                [
                    t[at : at + quarter, n * k : n * (k + 1)],
                    t[half + at : half + at + quarter, n * k : n * (k + 1)],
                ],
                1,
            )
            for k in (0, 1)
            for t, at in ((plus, 0), (minus, 0), (plus, quarter), (minus, quarter))
        ],
        0,
    )
    delta = dot(h, right_bwd[...])
    terms = [None, None]
    for k in (0, 1):
        d_re = delta[n * k : n * k + n, :n]
        d_im = delta[n * k : n * k + n, n:]
        new = (
            probe[k, 0] * d_re + probe[k, 1] * d_im,
            probe[k, 0] * d_im - probe[k, 1] * d_re,
        )
        terms = [b if a is None else a + b for a, b in zip(terms, new)]
        acc[k, 0] += wr * d_re + wi * d_im
        acc[k, 1] += wr * d_im - wi * d_re
    blank = jnp.zeros((n, LANE), f32)
    for part, term in enumerate(terms):
        moved = pltpu.roll(stack([term, blank], 1), shift, 1)
        for j in range(3):
            view = grad.at[part, block + j]
            for p in (0, 1):
                rows = pl.ds(r + p, half, stride=2)
                view[rows, :] = view[rows, :] + moved[half * p : half * (p + 1), LANE * j : LANE * (j + 1)]


def group_kernel(first, count, homes, n_after, last, live, off, *refs):
    wide = count + 2
    refs = list(refs)
    sources = refs[: len(homes[2])]
    refs = refs[len(homes[2]) + n_after :]
    measured, probe, t0, t1, t2, t3, carry, acc_in = refs[:8]
    if last:
        upper, lower, over_upper, over_lower, acc = refs[8:13]
    else:
        upper, lower, carry_out, acc = refs[8:12]
    ext, grad, frame, picked, load_sem, frame_sem = refs[-6:]

    def pick(q, n):
        b = off[q, 1] // LANE - first
        picked[n] = q
        return n + jnp.where((b >= 0) & (b < count), 1, 0)

    n = lax.fori_loop(0, live[0], pick, jnp.int32(0))

    def loads():
        out = []
        for half in (0, 1):
            for b in range(wide):
                which, row, at = homes[half][b]
                src = sources[which].at[:, row : row + SIZE, at : at + LANE]
                dst = ext.at[:, b, SIZE * half : SIZE * (half + 1), :]
                out.append(pltpu.make_async_copy(src, dst, load_sem.at[2 * b + half]))
        return out

    def frame_copies(i):
        slot = i % 2
        return [
            pltpu.make_async_copy(
                measured.at[picked[i], :, LANE * b : LANE * (b + 1)],
                frame.at[slot, b],
                frame_sem.at[2 * slot + b],
            )
            for b in (0, 1)
        ]

    @pl.when(n > 0)
    def _():
        for copy in loads():
            copy.start()
        for copy in frame_copies(0):
            copy.start()

    grad[:, 0:2] = carry[...]
    grad[:, 2:] = jnp.zeros((2, count, 2 * SIZE, LANE), f32)
    acc[...] = acc_in[...]

    @pl.when(n > 0)
    def _():
        for copy in loads():
            copy.wait()

    def step(i, _):
        @pl.when(i + 1 < n)
        def _():
            for copy in frame_copies(i + 1):
                copy.start()

        for copy in frame_copies(i):
            copy.wait()
        q = picked[i]
        pattern(
            ext, grad, acc, probe, frame.at[i % 2], (t0, t1, t2, t3), off[q, 0], off[q, 1] - first * LANE
        )
        return 0

    lax.fori_loop(0, n, step, 0)
    upper[...] = grad[:, 0:count, :SIZE]
    lower[...] = grad[:, 0:count, SIZE:]
    if not last:
        carry_out[...] = grad[:, count:]
    if last:
        over_upper[...] = grad[:, count:, :SIZE]
        over_lower[...] = grad[:, count:, SIZE:]
        for k in (0, 1):
            for part in (0, 1):
                for b in (0, 1):
                    view = ext.at[part, 2 * k + b]
                    at = slice(LANE * b, LANE * (b + 1))
                    for p in (0, 1):
                        rows = pl.ds(p, SIZE // 2, stride=2)
                        view[rows, :] = acc[k, part, LANE * p : LANE * (p + 1), at]
                    acc[k, part, :, at] = view[0:SIZE, :]


IN_HBM = pl.BlockSpec(memory_space=pltpu.HBM)
IN_SMEM = pl.BlockSpec(memory_space=pltpu.SMEM)
IN_VMEM = pl.BlockSpec(memory_space=pltpu.VMEM)


def run_group(first, count, bounds, live, off, field, halos, corner, measured, probe, tabs, carry, acc, after):
    wide = count + 2
    arrays, homes = [], [[], []]

    def index_in(array):
        for i, other in enumerate(arrays):
            if other is array:
                return i
        arrays.append(array)
        return len(arrays) - 1

    for b in range(first, first + wide):
        if b < bounds[-1]:
            chunk = next(i for i, end in enumerate(bounds) if b < end)
            begin = bounds[chunk - 1] if chunk else 0
            homes[0].append((index_in(field), 0, b * LANE))
            homes[1].append((index_in(halos[chunk]), 0, (b - begin) * LANE))
        else:
            at = (b - bounds[-1]) * LANE
            homes[0].append((index_in(corner), 0, at))
            homes[1].append((index_in(corner), SIZE, at))
    homes.append(arrays)
    args = [live, off, *arrays, *after, measured, probe, *tabs, carry, acc]
    specs = [IN_SMEM] * 2 + [IN_HBM] * (1 + len(arrays) + len(after)) + [IN_VMEM] * 7
    part = jax.ShapeDtypeStruct((2, count, SIZE, LANE), f32)
    last = first + count == bounds[-1]
    whole = jax.ShapeDtypeStruct((2, 2, 2 * SIZE, LANE), f32)
    edge = jax.ShapeDtypeStruct((2, 2, SIZE, LANE), f32)
    out_shape = (part, part) + ((edge, edge) if last else (whole,))
    out_shape += (jax.ShapeDtypeStruct((2, 2, SIZE, SIZE), f32),)
    return pl.pallas_call(
        functools.partial(group_kernel, first, count, (homes[0], homes[1], [None] * len(arrays)),
            len(after), last),
        out_shape=out_shape,
        in_specs=specs,
        out_specs=(IN_VMEM,) * len(out_shape),
        scratch_shapes=[
            pltpu.VMEM((2, wide, 2 * SIZE, LANE), f32),
            pltpu.VMEM((2, wide, 2 * SIZE, LANE), f32),
            pltpu.VMEM((2, 2, SIZE, LANE), f32),
            pltpu.SMEM((SLOTS + 1,), jnp.int32),
            pltpu.SemaphoreType.DMA((2 * wide,)),
            pltpu.SemaphoreType.DMA((4,)),
        ],
        compiler_params=pltpu.CompilerParams(vmem_limit_bytes=44 * 2**20),
        cost_estimate=pl.CostEstimate(flops=2**33, bytes_accessed=2**12, transcendentals=0),
        name=f"group_{first}",
    )(*args)


def finish_kernel(blocks, terms, *refs):
    out, buf, sem = refs[-3:]
    copies = []
    for at, (block, many) in enumerate(zip(blocks, terms)):
        value = None
        for which, b in many:
            term = refs[which][:, b, :SIZE]
            value = term if value is None else value + term
        buf[at] = value
        copy = pltpu.make_async_copy(
            buf.at[at], out.at[:, :, block * LANE : (block + 1) * LANE], sem.at[at]
        )
        copy.start()
        copies.append(copy)
    for copy in copies:
        copy.wait()


def finish(blocks, sources, shape, onto):
    args = [array for _, array in sources]
    terms = tuple(
        tuple(
            (i, block - first)
            for i, (first, array) in enumerate(sources)
            if first <= block < first + array.shape[1]
        )
        for block in blocks
    )
    specs = [IN_VMEM] * len(args)
    aliases = {}
    if onto is not None:
        aliases = {len(args): 0}
        args.append(onto)
        specs.append(IN_HBM)
    return pl.pallas_call(
        functools.partial(finish_kernel, tuple(blocks), terms),
        out_shape=jax.ShapeDtypeStruct(shape, f32),
        in_specs=specs,
        out_specs=IN_HBM,
        scratch_shapes=[
            pltpu.VMEM((len(blocks), 2, SIZE, LANE), f32),
            pltpu.SemaphoreType.DMA((len(blocks),)),
        ],
        input_output_aliases=aliases,
        compiler_params=pltpu.CompilerParams(vmem_limit_bytes=24 * 2**20),
        name=f"finish_{blocks[0]}",
    )(*args)


def shifted(array, axis, by, name):
    count = lax.axis_size(axis)
    pairs = [(i, i + by) for i in range(count) if 0 <= i + by < count]
    with jax.named_scope(name):
        return lax.ppermute(array, axis, pairs)


def shifted_both(array, name):
    rows, cols = (lax.axis_size(a) for a in AXES)
    pairs = [
        (i * cols + j, (i + 1) * cols + j + 1) for i in range(rows - 1) for j in range(cols - 1)
    ]
    with jax.named_scope(name):
        return lax.ppermute(array, AXES, pairs)


def place_of(index):
    s, m = divmod(index, 4)
    return [m % 2, (s // 16) * 2 + m // 2, (s // 4) % 4, s % 4]


def index_of(place):
    core, y, z, x = place
    return ((y // 2) * 16 + z * 4 + x) * 4 + (y % 2) * 2 + core


def swapped(array, axis, bits):
    pairs = []
    for i in range(128):
        place = place_of(i)
        place[axis] ^= bits
        pairs.append((i, index_of(place)))
    with jax.named_scope("swap_" + "cyzx"[axis] + str(bits)):
        return lax.ppermute(array, AXES, pairs)


def halved_sum(v, axis, here, pieces, held=None):
    v = v.reshape(pieces, -1, v.shape[-1])
    pick = functools.partial(lax.dynamic_index_in_dim, axis=0, keepdims=False)
    got = [swapped(pick(v, here ^ k), axis, k) for k in range(1, pieces)]
    if pieces == 2:
        return pick(v, here) + got[0], held
    if held is not None:
        got[0], held = lax.optimization_barrier((got[0], held))
    return (pick(v, here) + got[0]) + (got[1] + got[2]), held


def exchanged_sum(v, axis, held=None):
    a, b, c = [swapped(v, axis, k) for k in (1, 2, 3)]
    if held is not None:
        a, held = lax.optimization_barrier((a, held))
    return (v + a) + (b + c), held


def gathered(v, axis, here, pieces):
    parts = [v] + [swapped(v, axis, k) for k in range(1, pieces)]

    def part_of(i):
        which = here ^ i
        if pieces == 2:
            return jnp.where(which == 0, parts[0], parts[1])
        return jnp.where(
            which < 2,
            jnp.where(which == 0, parts[0], parts[1]),
            jnp.where(which == 2, parts[2], parts[3]),
        )

    return jnp.concatenate([part_of(i) for i in range(pieces)], 0)


BOUNDS = (5, 9, 13, 15, 16)


def shards(field, probe, measured, offsets, live):
    rows, cols = field.shape[1:]
    base = jnp.stack([lax.axis_index("scan") * rows, lax.axis_index("mode") * cols])
    off = offsets - base[None, :]
    tabs = [jnp.asarray(t) for t in tables()]
    probe_rows = probe.reshape(2, 2, 128, 2, 256).transpose(0, 1, 3, 2, 4).reshape(probe.shape)
    tie = lax.optimization_barrier
    head, rest = tie((field[:, :, : LANE * BOUNDS[0]], field))
    halos = [shifted(head, "scan", -1, "halo_0")]
    for i, (a, b) in enumerate(zip(BOUNDS[:-1], BOUNDS[1:])):
        part = rest[:, :, LANE * a : LANE * b]
        if i == 1:
            part, halos[0] = tie((part, halos[0]))
        halos.append(shifted(part, "scan", -1, f"halo_{i + 1}"))
    beside = jnp.concatenate([field[:, :, :SIZE], halos[0][:, :, :SIZE]], 1)
    corner = shifted(beside, "mode", -1, "corner")
    carry = jnp.zeros((2, 2, 2 * SIZE, LANE), f32)
    acc = jnp.zeros(probe.shape, f32)
    ends = [b - 2 for b in BOUNDS[:-1]] + [BOUNDS[-1]]
    plan = [(a, b - a) for a, b in zip([0] + ends[:-1], ends)]
    uppers, lowers, comings = [], [], []
    for i, (first, count) in enumerate(plan):
        after = {2: (0,), 3: (1, corner)}.get(i, ())
        after = [comings[j] if isinstance(j, int) else j for j in after]
        upper, lower, *rest, acc = run_group(
            first, count, BOUNDS, live, off, field, halos, corner, measured, probe_rows, tabs, carry, acc, after
        )
        uppers.append(upper)
        lowers.append(lower)
        if i + 1 < len(plan):
            carry = rest[0]
            comings.append(shifted(lower, "scan", 1, f"grad_{i}"))
    over_upper, over_lower = rest
    s, m = lax.axis_index("scan"), lax.axis_index("mode")
    core, y = m % 2, (s // 16) * 2 + m // 2
    v, _ = halved_sum(acc.reshape(1024, 256), 0, core, 2)
    v, comings[2], final = tie((v, comings[2], lowers[4]))
    comings.append(shifted(final, "scan", 1, "grad_4"))
    v, _ = halved_sum(v, 1, y, 4)
    v, comings[3], over_lower = tie((v, comings[3], over_lower))
    slant = shifted_both(over_lower, "slant")
    v, _ = exchanged_sum(v, 2)
    sources = [(first, array) for (first, _), pair in zip(plan, zip(uppers, comings)) for array in pair]
    step = finish(range(2, 13), sources[:8], field.shape, None)
    v, comings[4], over_upper = tie((v, comings[4], over_upper))
    over = shifted(over_upper, "mode", 1, "over")
    v, _ = exchanged_sum(v, 3)
    slots_all = lax.axis_size("scan") * lax.axis_size("mode") * SLOTS
    v = v * (1.0 / math.sqrt(slots_all))
    v, slant = tie((v, slant))
    v = gathered(v, 1, y, 4)
    v, step = tie((v, step))
    probe_step = gathered(v, 0, core, 2).reshape(probe.shape)
    sources = sources[:2] + [(13, uppers[4]), (13, comings[4]), (0, over), (0, slant)]
    step = finish([0, 1, 13, 14, 15], sources, field.shape, step)
    return (step, probe_step)


def solution(mesh):
    in_specs = (
        P(None, "scan", "mode"),
        P(),
        P(AXES, None, None),
        P(AXES, None),
        P(AXES),
    )
    out_specs = (P(None, "scan", "mode"), P())
    return jax.shard_map(shards, mesh=mesh, in_specs=in_specs, out_specs=out_specs, check_vma=False)
```

```python
import functools
import math

import jax
import jax.numpy as jnp
import ml_dtypes
import numpy as np
from jax import lax
from jax.experimental import pallas as pl
from jax.experimental.pallas import tpu as pltpu
from jax.sharding import PartitionSpec as P

SLOTS = 16
SIZE = 256
LANE = 128
CHUNK = 256
FLOOR = 0.5
AXES = ("scan", "mode")
f32 = jnp.float32
bf16 = jnp.bfloat16


def tables():
    n = SIZE
    place = np.arange(n)
    angles = (place[:, None] * place[None, :] % n) * (2.0 * math.pi / n)
    c = np.cos(angles) / math.sqrt(n)
    s = np.sin(angles) / math.sqrt(n)
    rows = np.concatenate([place[0 : n // 2 : 2], place[1 : n // 2 : 2]])

    def block(c, s):
        return np.block([[c, s], [-s, c]])

    def halves(c, s):
        return np.stack([block(c[rows, p::2], s[rows, p::2]) for p in (0, 1)])

    both = (halves(c, s), block(c, -s), halves(c, -s), block(c, s))
    return [t.astype(ml_dtypes.bfloat16) for t in both]


def stack(parts, axis):
    return jnp.concatenate(parts, axis)


def left_product(table, even, odd):
    dot = functools.partial(jnp.dot, preferred_element_type=f32)
    a = dot(table[0], even)
    b = dot(table[1], odd)
    return (a + b).astype(bf16), (a - b).astype(bf16)


def pattern(ext, grad, acc, probe, frame, tabs, r, c):
    left_fwd, right_fwd, left_bwd, right_bwd = tabs
    n = SIZE
    half, quarter = n // 2, n // 4
    block = c // LANE
    shift = c % LANE
    dot = functools.partial(jnp.dot, preferred_element_type=f32)

    def window(part):
        cols = []
        for j in range(3):
            view = ext.at[part, block + j]
            cols.append(stack([view[pl.ds(r + p, half, stride=2), :] for p in (0, 1)], 0))
        return pltpu.roll(stack(cols, 1), 3 * LANE - shift, 1)[:, :n]

    wr = window(0)
    wi = window(1)
    x_re = [probe[k, 0] * wr - probe[k, 1] * wi for k in (0, 1)]
    x_im = [probe[k, 0] * wi + probe[k, 1] * wr for k in (0, 1)]

    def rows_of(p):
        rows = slice(half * p, half * (p + 1))
        return stack([stack([x_re[k][rows], x_im[k][rows]], 0) for k in (0, 1)], 1).astype(bf16)

    sums = left_product(left_fwd, rows_of(0), rows_of(1))
    h = stack(
        [
            stack([t[:half, n * k : n * (k + 1)], t[half:, n * k : n * (k + 1)]], 1)
            for k in (0, 1)
            for t in sums
        ],
        0,
    )
    far = dot(h, right_fwd[...])
    sq = far * far
    intensity = (sq[:n, :n] + sq[:n, n:]) + (sq[n:, :n] + sq[n:, n:])
    amplitude = stack(
        [
            stack([frame.at[b][pl.ds(row, quarter, stride=2), :] for b in (0, 1)], 1)
            for row in (0, 1, half, half + 1)
        ],
        0,
    )
    factor = amplitude * lax.rsqrt(jnp.maximum(intensity, FLOOR)) - 1.0
    change = [
        [(far[n * k : n * (k + 1), n * p : n * (p + 1)] * factor).astype(bf16) for p in (0, 1)]
        for k in (0, 1)
    ]

    def quarters(q):
        return stack(
            [
                stack([change[k][p][at : at + quarter] for p in (0, 1) for at in (q, q + half)], 0)
                for k in (0, 1)
            ],
            1,
        )

    plus, minus = left_product(left_bwd, quarters(0), quarters(quarter))
    h = stack(
        [
            stack(
                [
                    t[at : at + quarter, n * k : n * (k + 1)],
                    t[half + at : half + at + quarter, n * k : n * (k + 1)],
                ],
                1,
            )
            for k in (0, 1)
            for t, at in ((plus, 0), (minus, 0), (plus, quarter), (minus, quarter))
        ],
        0,
    )
    delta = dot(h, right_bwd[...])
    terms = [None, None]
    for k in (0, 1):
        d_re = delta[n * k : n * k + n, :n]
        d_im = delta[n * k : n * k + n, n:]
        new = (
            probe[k, 0] * d_re + probe[k, 1] * d_im,
            probe[k, 0] * d_im - probe[k, 1] * d_re,
        )
        terms = [b if a is None else a + b for a, b in zip(terms, new)]
        acc[k, 0] += wr * d_re + wi * d_im
        acc[k, 1] += wr * d_im - wi * d_re
    blank = jnp.zeros((n, LANE), f32)
    for part, term in enumerate(terms):
        moved = pltpu.roll(stack([term, blank], 1), shift, 1)
        for j in range(3):
            view = grad.at[part, block + j]
            for p in (0, 1):
                rows = pl.ds(r + p, half, stride=2)
                view[rows, :] = view[rows, :] + moved[half * p : half * (p + 1), LANE * j : LANE * (j + 1)]


def group_kernel(first, count, homes, n_after, last, live, off, *refs):
    wide = count + 2
    refs = list(refs)
    sources = refs[: len(homes[2])]
    refs = refs[len(homes[2]) + n_after :]
    measured, probe, t0, t1, t2, t3, carry, acc_in = refs[:8]
    if last:
        upper, lower, over_upper, over_lower, acc = refs[8:13]
    else:
        upper, lower, carry_out, acc = refs[8:12]
    ext, grad, frame, picked, load_sem, frame_sem = refs[-6:]

    def pick(q, n):
        b = off[q, 1] // LANE - first
        picked[n] = q
        return n + jnp.where((b >= 0) & (b < count), 1, 0)

    n = lax.fori_loop(0, live[0], pick, jnp.int32(0))

    def loads():
        out = []
        for half in (0, 1):
            for b in range(wide):
                which, row, at = homes[half][b]
                src = sources[which].at[:, row : row + SIZE, at : at + LANE]
                dst = ext.at[:, b, SIZE * half : SIZE * (half + 1), :]
                out.append(pltpu.make_async_copy(src, dst, load_sem.at[2 * b + half]))
        return out

    def frame_copies(i):
        slot = i % 2
        return [
            pltpu.make_async_copy(
                measured.at[picked[i], :, LANE * b : LANE * (b + 1)],
                frame.at[slot, b],
                frame_sem.at[2 * slot + b],
            )
            for b in (0, 1)
        ]

    @pl.when(n > 0)
    def _():
        for copy in loads():
            copy.start()
        for copy in frame_copies(0):
            copy.start()

    grad[:, 0:2] = carry[...]
    grad[:, 2:] = jnp.zeros((2, count, 2 * SIZE, LANE), f32)
    acc[...] = acc_in[...]

    @pl.when(n > 0)
    def _():
        for copy in loads():
            copy.wait()

    def step(i, _):
        @pl.when(i + 1 < n)
        def _():
            for copy in frame_copies(i + 1):
                copy.start()

        for copy in frame_copies(i):
            copy.wait()
        q = picked[i]
        pattern(
            ext, grad, acc, probe, frame.at[i % 2], (t0, t1, t2, t3), off[q, 0], off[q, 1] - first * LANE
        )
        return 0

    lax.fori_loop(0, n, step, 0)
    upper[...] = grad[:, 0:count, :SIZE]
    lower[...] = grad[:, 0:count, SIZE:]
    if not last:
        carry_out[...] = grad[:, count:]
    if last:
        over_upper[...] = grad[:, count:, :SIZE]
        over_lower[...] = grad[:, count:, SIZE:]
        for k in (0, 1):
            for part in (0, 1):
                for b in (0, 1):
                    view = ext.at[part, 2 * k + b]
                    at = slice(LANE * b, LANE * (b + 1))
                    for p in (0, 1):
                        rows = pl.ds(p, SIZE // 2, stride=2)
                        view[rows, :] = acc[k, part, LANE * p : LANE * (p + 1), at]
                    acc[k, part, :, at] = view[0:SIZE, :]


IN_HBM = pl.BlockSpec(memory_space=pltpu.HBM)
IN_SMEM = pl.BlockSpec(memory_space=pltpu.SMEM)
IN_VMEM = pl.BlockSpec(memory_space=pltpu.VMEM)


def run_group(first, count, bounds, live, off, field, halos, corner, measured, probe, tabs, carry, acc, after):
    wide = count + 2
    arrays, homes = [], [[], []]

    def index_in(array):
        for i, other in enumerate(arrays):
            if other is array:
                return i
        arrays.append(array)
        return len(arrays) - 1

    for b in range(first, first + wide):
        if b < bounds[-1]:
            chunk = next(i for i, end in enumerate(bounds) if b < end)
            begin = bounds[chunk - 1] if chunk else 0
            homes[0].append((index_in(field), 0, b * LANE))
            homes[1].append((index_in(halos[chunk]), 0, (b - begin) * LANE))
        else:
            at = (b - bounds[-1]) * LANE
            homes[0].append((index_in(corner), 0, at))
            homes[1].append((index_in(corner), SIZE, at))
    homes.append(arrays)
    args = [live, off, *arrays, *after, measured, probe, *tabs, carry, acc]
    specs = [IN_SMEM] * 2 + [IN_HBM] * (1 + len(arrays) + len(after)) + [IN_VMEM] * 7
    part = jax.ShapeDtypeStruct((2, count, SIZE, LANE), f32)
    last = first + count == bounds[-1]
    whole = jax.ShapeDtypeStruct((2, 2, 2 * SIZE, LANE), f32)
    edge = jax.ShapeDtypeStruct((2, 2, SIZE, LANE), f32)
    out_shape = (part, part) + ((edge, edge) if last else (whole,))
    out_shape += (jax.ShapeDtypeStruct((2, 2, SIZE, SIZE), f32),)
    return pl.pallas_call(
        functools.partial(group_kernel, first, count, (homes[0], homes[1], [None] * len(arrays)),
            len(after), last),
        out_shape=out_shape,
        in_specs=specs,
        out_specs=(IN_VMEM,) * len(out_shape),
        scratch_shapes=[
            pltpu.VMEM((2, wide, 2 * SIZE, LANE), f32),
            pltpu.VMEM((2, wide, 2 * SIZE, LANE), f32),
            pltpu.VMEM((2, 2, SIZE, LANE), f32),
            pltpu.SMEM((SLOTS + 1,), jnp.int32),
            pltpu.SemaphoreType.DMA((2 * wide,)),
            pltpu.SemaphoreType.DMA((4,)),
        ],
        compiler_params=pltpu.CompilerParams(vmem_limit_bytes=44 * 2**20),
        cost_estimate=pl.CostEstimate(flops=2**33, bytes_accessed=2**12, transcendentals=0),
        name=f"group_{first}",
    )(*args)


def finish_kernel(blocks, terms, *refs):
    out, buf, sem = refs[-3:]
    copies = []
    for at, (block, many) in enumerate(zip(blocks, terms)):
        value = None
        for which, b in many:
            term = refs[which][:, b, :SIZE]
            value = term if value is None else value + term
        buf[at] = value
        copy = pltpu.make_async_copy(
            buf.at[at], out.at[:, :, block * LANE : (block + 1) * LANE], sem.at[at]
        )
        copy.start()
        copies.append(copy)
    for copy in copies:
        copy.wait()


def finish(blocks, sources, shape, onto):
    args = [array for _, array in sources]
    terms = tuple(
        tuple(
            (i, block - first)
            for i, (first, array) in enumerate(sources)
            if first <= block < first + array.shape[1]
        )
        for block in blocks
    )
    specs = [IN_VMEM] * len(args)
    aliases = {}
    if onto is not None:
        aliases = {len(args): 0}
        args.append(onto)
        specs.append(IN_HBM)
    return pl.pallas_call(
        functools.partial(finish_kernel, tuple(blocks), terms),
        out_shape=jax.ShapeDtypeStruct(shape, f32),
        in_specs=specs,
        out_specs=IN_HBM,
        scratch_shapes=[
            pltpu.VMEM((len(blocks), 2, SIZE, LANE), f32),
            pltpu.SemaphoreType.DMA((len(blocks),)),
        ],
        input_output_aliases=aliases,
        compiler_params=pltpu.CompilerParams(vmem_limit_bytes=24 * 2**20),
        name=f"finish_{blocks[0]}",
    )(*args)


def shifted(array, axis, by, name):
    count = lax.axis_size(axis)
    pairs = [(i, i + by) for i in range(count) if 0 <= i + by < count]
    with jax.named_scope(name):
        return lax.ppermute(array, axis, pairs)


def shifted_both(array, name):
    rows, cols = (lax.axis_size(a) for a in AXES)
    pairs = [
        (i * cols + j, (i + 1) * cols + j + 1) for i in range(rows - 1) for j in range(cols - 1)
    ]
    with jax.named_scope(name):
        return lax.ppermute(array, AXES, pairs)


def place_of(index):
    s, m = divmod(index, 4)
    return [m % 2, (s // 16) * 2 + m // 2, (s // 4) % 4, s % 4]


def index_of(place):
    core, y, z, x = place
    return ((y // 2) * 16 + z * 4 + x) * 4 + (y % 2) * 2 + core


def swapped(array, axis, bits):
    pairs = []
    for i in range(128):
        place = place_of(i)
        place[axis] ^= bits
        pairs.append((i, index_of(place)))
    with jax.named_scope("swap_" + "cyzx"[axis] + str(bits)):
        return lax.ppermute(array, AXES, pairs)


def halved_sum(v, axis, here, pieces, held=None):
    v = v.reshape(pieces, -1, v.shape[-1])
    pick = functools.partial(lax.dynamic_index_in_dim, axis=0, keepdims=False)
    got = [swapped(pick(v, here ^ k), axis, k) for k in range(1, pieces)]
    if pieces == 2:
        return pick(v, here) + got[0], held
    if held is not None:
        got[0], held = lax.optimization_barrier((got[0], held))
    return (pick(v, here) + got[0]) + (got[1] + got[2]), held


def exchanged_sum(v, axis, held=None):
    a, b, c = [swapped(v, axis, k) for k in (1, 2, 3)]
    if held is not None:
        a, held = lax.optimization_barrier((a, held))
    return (v + a) + (b + c), held


def gathered(v, axis, here, pieces):
    parts = [v] + [swapped(v, axis, k) for k in range(1, pieces)]

    def part_of(i):
        which = here ^ i
        if pieces == 2:
            return jnp.where(which == 0, parts[0], parts[1])
        return jnp.where(
            which < 2,
            jnp.where(which == 0, parts[0], parts[1]),
            jnp.where(which == 2, parts[2], parts[3]),
        )

    return jnp.concatenate([part_of(i) for i in range(pieces)], 0)


BOUNDS = (4, 8, 12, 15, 16)


def shards(field, probe, measured, offsets, live):
    rows, cols = field.shape[1:]
    base = jnp.stack([lax.axis_index("scan") * rows, lax.axis_index("mode") * cols])
    off = offsets - base[None, :]
    tabs = [jnp.asarray(t) for t in tables()]
    probe_rows = probe.reshape(2, 2, 128, 2, 256).transpose(0, 1, 3, 2, 4).reshape(probe.shape)
    tie = lax.optimization_barrier
    head, rest = tie((field[:, :, : LANE * BOUNDS[0]], field))
    halos = [shifted(head, "scan", -1, "halo_0")]
    for i, (a, b) in enumerate(zip(BOUNDS[:-1], BOUNDS[1:])):
        part = rest[:, :, LANE * a : LANE * b]
        if i == 1:
            part, halos[0] = tie((part, halos[0]))
        halos.append(shifted(part, "scan", -1, f"halo_{i + 1}"))
    beside = jnp.concatenate([field[:, :, :SIZE], halos[0][:, :, :SIZE]], 1)
    corner = shifted(beside, "mode", -1, "corner")
    carry = jnp.zeros((2, 2, 2 * SIZE, LANE), f32)
    acc = jnp.zeros(probe.shape, f32)
    ends = [b - 2 for b in BOUNDS[:-1]] + [BOUNDS[-1]]
    plan = [(a, b - a) for a, b in zip([0] + ends[:-1], ends)]
    uppers, lowers, comings = [], [], []
    for i, (first, count) in enumerate(plan):
        after = {2: (0,), 3: (1, corner)}.get(i, ())
        after = [comings[j] if isinstance(j, int) else j for j in after]
        upper, lower, *rest, acc = run_group(
            first, count, BOUNDS, live, off, field, halos, corner, measured, probe_rows, tabs, carry, acc, after
        )
        uppers.append(upper)
        lowers.append(lower)
        if i + 1 < len(plan):
            carry = rest[0]
            comings.append(shifted(lower, "scan", 1, f"grad_{i}"))
    over_upper, over_lower = rest
    s, m = lax.axis_index("scan"), lax.axis_index("mode")
    core, y = m % 2, (s // 16) * 2 + m // 2
    v, _ = halved_sum(acc.reshape(1024, 256), 0, core, 2)
    v, comings[2], final = tie((v, comings[2], lowers[4]))
    comings.append(shifted(final, "scan", 1, "grad_4"))
    v, _ = halved_sum(v, 1, y, 4)
    v, comings[3], over_lower = tie((v, comings[3], over_lower))
    slant = shifted_both(over_lower, "slant")
    v, _ = exchanged_sum(v, 2)
    sources = [(first, array) for (first, _), pair in zip(plan, zip(uppers, comings)) for array in pair]
    step = finish(range(2, 13), sources[:8], field.shape, None)
    v, comings[4], step, over_upper = tie((v, comings[4], step, over_upper))
    over = shifted(over_upper, "mode", 1, "over")
    v, _ = exchanged_sum(v, 3)
    slots_all = lax.axis_size("scan") * lax.axis_size("mode") * SLOTS
    v = v * (1.0 / math.sqrt(slots_all))
    v, slant = tie((v, slant))
    v = gathered(v, 1, y, 4)
    probe_step = gathered(v, 0, core, 2).reshape(probe.shape)
    sources = sources[:2] + [(13, uppers[4]), (13, comings[4]), (0, over), (0, slant)]
    step = finish([0, 1, 13, 14, 15], sources, field.shape, step)
    return (step, probe_step)


def solution(mesh):
    in_specs = (
        P(None, "scan", "mode"),
        P(),
        P(AXES, None, None),
        P(AXES, None),
        P(AXES),
    )
    out_specs = (P(None, "scan", "mode"), P())
    return jax.shard_map(shards, mesh=mesh, in_specs=in_specs, out_specs=out_specs, check_vma=False)
```
